768 devices in a mesh: gx: 32 (over x, z_hi, core), gy: 24 (over z_lo, y).
Axes of the slice: x: 4, y: 8, z: 12 (z_hi: 4, z_lo: 3; z = z_hi * 3 + z_lo), core: 2. Of those that a mesh axis runs over, the one named last changes fastest.
Arguments:
- fine_residual: float32 [5, 1536, 12288], P(None, 'gx', 'gy'), may hold values from -0.6 to 0.6
- owner_map: int32 [1536, 12288], P('gx', 'gy'), may hold values from 0 to 6143, as said below
- boundary_flags: int32 [768, 6144], P('gx', 'gy'), may hold values from 0 to 2
- jacobian: float32 [5, 5, 768, 6144], P(None, None, 'gx', 'gy'), may hold values from -0.6 to 20
- line_coef: float32 [5, 192, 1536], P(None, 'gx', 'gy'), may hold values from 2.0001 to 2.003
Outputs:
- correction: float32 [5, 768, 6144], P(None, 'gx', 'gy')
- level_residual: float32 [5, 768, 6144], P(None, 'gx', 'gy')
The draws below stay inside these ranges and needn't reach their ends.
Inputs may be any that keep to these rules, and one draw needn't show every extreme that they name: `owner_map`: each level-0 cell names a level-1 cell of its own device's tile of 24 x 256 cells, numbered row by row, at most one cell away in each direction from the cell covering its own position.
All inputs are finite; a program needn't handle non-finite values.
Results may differ from the reference program's by a relative error of at most 0.0003.
Values sent between devices are 32-bit elements; how exact they have to be, the bound alone decides.
No kernel may reach another device: no remote copies, remote signals or barrier semaphores. Data moves between devices by JAX's collectives and lax.ppermute only.
A program may use at most 64 MiB of HBM per device.

```python
import jax
import jax.numpy as jnp
from jax import lax

FIELDS = 5
CX = 24
CY = 256
PRE = 3
POST = 2
NX = 768
NY = 6144


def draw_fine_residual(key, part):
    key = jax.random.fold_in(key, 14)
    shape = (FIELDS, 2 * NX, 2 * NY)
    values = 0.1 * jax.random.truncated_normal(key, -6.0, 6.0, shape, jnp.float32)
    return values.astype(jnp.float32)


def draw_owner_map(key, part):
    key = jax.random.fold_in(key, 11)
    first, second, third = jax.random.split(key, 3)
    rows = 2 * NX
    cols = 2 * NY
    place_x = (jnp.arange(rows) % (2 * CX))[:, None]
    place_y = (jnp.arange(cols) % (2 * CY))[None, :]
    moving = jax.random.randint(first, (rows, cols), 0, 4) == 0
    step_x = jax.random.randint(second, (rows, cols), -1, 2)
    step_y = jax.random.randint(third, (rows, cols), -1, 2)
    cell_x = jnp.clip(place_x // 2 + jnp.where(moving, step_x, 0), 0, CX - 1)
    cell_y = jnp.clip(place_y // 2 + jnp.where(moving, step_y, 0), 0, CY - 1)
    return (cell_x * CY + cell_y).astype(jnp.int32)


def draw_jacobian(key, part):
    key = jax.random.fold_in(key, 12)
    first, second = jax.random.split(key)
    off_part = jax.random.uniform(first, (FIELDS, FIELDS, NX, NY), jnp.float32, -0.6, 0.6)
    diag_part = jax.random.uniform(second, (FIELDS, NX, NY), jnp.float32, 7.0, 14.0)
    identity = jnp.eye(FIELDS, dtype=jnp.float32)[:, :, None, None]
    return (off_part * (1.0 - identity) + identity * diag_part[:, None]).astype(jnp.float32)


def draw_line_coef(key, part):
    key = jax.random.fold_in(key, 13)
    upper_log = jnp.log(0.003)
    lower_log = jnp.log(0.0003)
    spread = jax.random.uniform(key, (FIELDS, NX // 4, NY // 4), jnp.float32, lower_log, upper_log)
    return (2.0 + jnp.exp(spread)).astype(jnp.float32)


def set_ends(entries, rng, smallest, high):
    longest = entries.shape.index(max(entries.shape))
    spots = []
    for shift in (0, 1):
        where = [jax.random.randint(jax.random.fold_in(rng, axis), (), 0, length) for axis, length in enumerate(entries.shape)]
        where[longest] = (where[longest] + shift) % entries.shape[longest]
        spots.append(tuple(where))
    return entries.at[spots[0]].set(smallest).at[spots[1]].set(high)


def setup_inputs(seed: int = 0) -> dict:
    seeds = jax.random.split(jax.random.key(seed), 6)
    fine_residual = draw_fine_residual(jax.random.fold_in(seeds[5], 71), 0)
    owner_map = draw_owner_map(jax.random.fold_in(seeds[5], 71), 0)
    boundary_flags = set_ends(jax.random.randint(seeds[2], (NX, NY), 0, 3), jax.random.fold_in(seeds[2], 1), 0, 2).astype(jnp.int32)
    jacobian = draw_jacobian(jax.random.fold_in(seeds[5], 71), 0)
    line_coef = draw_line_coef(jax.random.fold_in(seeds[5], 71), 0)
    return {"fine_residual": fine_residual, "owner_map": owner_map, "boundary_flags": boundary_flags, "jacobian": jacobian, "line_coef": line_coef}


def operate(field, jacobian):
    padded = jnp.pad(field, ((0, 0), (1, 1), (1, 1)))
    beside = padded[:, 2:, 1:-1] + padded[:, :-2, 1:-1] + padded[:, 1:-1, 2:] + padded[:, 1:-1, :-2]
    return jnp.sum(jacobian * field[None], axis=1) - beside

def line_solve(rhs, diag):
    rhs_t = jnp.transpose(rhs, (0, 2, 1))
    diag_t = jnp.transpose(diag, (0, 2, 1))
    count = diag_t.shape[-1]
    places = jnp.arange(count)
    lower = jnp.where(places == 0, jnp.zeros_like(diag_t), -jnp.ones_like(diag_t))
    upper = jnp.where(places == count - 1, jnp.zeros_like(diag_t), -jnp.ones_like(diag_t))
    solved = lax.linalg.tridiagonal_solve(lower, diag_t, upper, rhs_t[..., None])[..., 0]
    return jnp.transpose(solved, (0, 2, 1))

def make_mask(flags, fields):
    field_ids = jnp.arange(fields)[:, None, None]
    momentum = (field_ids == 1) | (field_ids == 2)
    interior = (flags == 0)[None]
    wall = (flags == 2)[None]
    return (interior | wall & jnp.logical_not(momentum)).astype(jnp.float32)

def reference(fine_residual, owner_map, boundary_flags, jacobian, line_coef):
    rows = 2 * NX
    cols = 2 * NY
    tile_x = (jnp.arange(rows) // (2 * CX))[:, None].astype(jnp.int32)
    tile_y = (jnp.arange(cols) // (2 * CY))[None, :].astype(jnp.int32)
    cell_x = tile_x * CX + owner_map // CY
    cell_y = tile_y * CY + owner_map % CY
    cell_ids = (cell_x * NY + cell_y).reshape(-1).astype(jnp.int32)
    flattened = fine_residual.reshape(FIELDS, -1)
    coarse_rhs = jax.vmap(lambda values: jax.ops.segment_sum(values, cell_ids, num_segments=NX * NY))(flattened)
    coarse_rhs = coarse_rhs.reshape(FIELDS, NX, NY)
    keep_mask = make_mask(boundary_flags, FIELDS)
    diagonal = jnp.stack([jacobian[f, f] for f in range(FIELDS)])
    scaled = 0.8 * keep_mask / diagonal
    sweep_state = jnp.zeros_like(coarse_rhs)
    for _ in range(PRE):
        sweep_state = sweep_state + scaled * (coarse_rhs - operate(sweep_state, jacobian))
    left_over = coarse_rhs - operate(sweep_state, jacobian)
    coarse_res = left_over.reshape(FIELDS, NX // 4, 4, NY // 4, 4).sum(axis=(2, 4)) / 16.0
    line_state = line_solve(coarse_res, line_coef)
    spread = jnp.repeat(jnp.repeat(line_state, 4, axis=1), 4, axis=2)
    sweep_state = sweep_state + keep_mask * spread
    for _ in range(POST):
        sweep_state = sweep_state + scaled * (coarse_rhs - operate(sweep_state, jacobian))
    level_residual = coarse_rhs - operate(sweep_state, jacobian)
    return (sweep_state, level_residual)
```

```python
import jax
import jax.numpy as jnp
from jax import lax
from jax.experimental import pallas as pl
from jax.experimental.pallas import tpu as pltpu
from jax.sharding import PartitionSpec as P

F = 5
TX = 24
TY = 256
EX = 40
EY = 384
ROWS = 6
PLANES = 31
HIGH = lax.Precision.HIGHEST
F32 = jnp.float32


def iota(shape, dim):
    return lax.broadcasted_iota(jnp.int32, shape, dim)


def dot(a, b):
    return jnp.dot(a, b, precision=HIGH, preferred_element_type=F32)


def roll(x, shift, axis):
    shift = shift % x.shape[axis]
    return x if shift == 0 else pltpu.roll(x, shift, axis)


def restrict_kernel(fine, owner, flags, jac, coef, rhs, top, bottom, left, right, tiles, owners):
    def halves(source, tile):
        for j in range(4):
            tile[j] = source[:, 128 * j : 128 * (j + 1)]
        return [
            jnp.concatenate([tile[j, pl.ds(start, TX, 2), :] for j in range(4)], axis=1)
            for start in (0, 1)
        ]

    shape = (TX, 2 * TY)
    row = iota(shape, 0)
    col = iota(shape, 1) // 2
    codes = [
        ((o // TY) - row + 1) * 3 + (o % TY) - col + 1
        for o in halves(owner, owners)
    ]
    masks = [[code == k for code in codes] for k in range(9)]
    gathered = []
    for f in range(F):
        values = halves(fine.at[f], tiles.at[f])
        total = None
        for dy in (-1, 0, 1):
            part = None
            for dx in (-1, 0, 1):
                mask = masks[(dx + 1) * 3 + dy + 1]
                moved = jnp.where(mask[0], values[0], 0.0) + jnp.where(mask[1], values[1], 0.0)
                moved = roll(moved, dx, 0)
                part = moved if part is None else part + moved
            part = roll(part, 2 * dy, 1)
            total = part if total is None else total + part
        gathered.append(total)
    pairs = (iota((2 * TY, TY), 0) // 2 == iota((2 * TY, TY), 1)).astype(F32)
    summed = dot(jnp.concatenate(gathered, axis=0), pairs)
    planes = [summed[TX * f : TX * (f + 1)] for f in range(F)]
    for f in range(F):
        rhs[f] = planes[f]
    planes.append((flags[...] + 1).astype(F32))
    for p in range(F + 1):
        for j in range(2):
            lanes = slice(128 * j, 128 * (j + 1))
            top[2 * p + j] = planes[p][0:8, lanes]
            bottom[2 * p + j] = planes[p][TX - 8 : TX, lanes]
    slot = iota((TX, 128), 1) // 8
    for a in range(2):
        first = jnp.zeros((TX, 128), F32)
        last = jnp.zeros((TX, 128), F32)
        for t in range(16):
            p = 16 * a + t
            if p >= PLANES:
                continue
            if p < F * F:
                head, tail = jac[p // F, p % F, :, 0:128], jac[p // F, p % F, :, TY - 128 : TY]
            else:
                head, tail = planes[p - F * F][:, 0:128], planes[p - F * F][:, TY - 128 : TY]
            first = jnp.where(slot == t, roll(head, 8 * t, 1), first)
            last = jnp.where(slot == t, roll(tail, 8 * t - 120, 1), last)
        left[a] = first
        right[a] = last
    lane = iota((ROWS, 128), 1)
    first = left[1, 0:ROWS, :]
    last = right[1, 0:ROWS, :]
    for f in range(F):
        wide = jnp.concatenate([coef[f], coef[f]], axis=1)
        first = jnp.where(lane == 120 + f, roll(wide, 120 + f, 1), first)
        last = jnp.where(lane == 120 + f, roll(wide, 120 + f - 63, 1), last)
    left[1, 0:ROWS, :] = first
    right[1, 0:ROWS, :] = last


def extended_planes(jac, jac_up, jac_down, rhs, flags, up, down, beside):
    def whole(upper, own, lower, aside):
        return jnp.concatenate([jnp.concatenate([upper, own, lower], axis=0), aside], axis=1)

    def strip(ref, p):
        return jnp.concatenate([ref[2 * p], ref[2 * p + 1]], axis=1)

    def jac_plane(f, g):
        return whole(jac_up[f, g], jac[f, g], jac_down[f, g], beside[f * F + g])

    def rhs_plane(f):
        return whole(strip(up, f), rhs[f], strip(down, f), beside[F * F + f])

    def code_plane():
        return whole(strip(up, F), (flags[...] + 1).astype(F32), strip(down, F), beside[F * F + F])

    return jac_plane, rhs_plane, code_plane


def scaled_planes(code, jac_plane):
    plain = (code == 1.0) | (code == 3.0)
    interior = code == 1.0
    kept = [interior if f in (1, 2) else plain for f in range(F)]
    return kept, [jnp.where(kept[f], 0.8 / jac_plane(f, f), 0.0) for f in range(F)]


def residual(f, state, rhs_plane, jac_plane):
    own = state[f]
    beside = roll(own, 1, 0) + roll(own, -1, 0) + roll(own, 1, 1) + roll(own, -1, 1)
    total = rhs_plane(f) + beside
    for g in range(F):
        total = total - jac_plane(f, g) * state[g]
    return total


def sweep(old, new, scaled, rhs_plane, jac_plane):
    for f in range(F):
        new[f] = old[f] + scaled[f] * residual(f, old, rhs_plane, jac_plane)


def columns(shape, fine_dim, coarse_dim):
    fine = iota(shape, fine_dim)
    coarse = iota(shape, coarse_dim)
    here = (coarse <= 64) & (fine // 4 == coarse)
    return (here | ((coarse == 65) & (fine >= EY - 4))).astype(F32)


def before_kernel(
    jac, jac_up, jac_down, rhs, flags, up, down, from_right, from_left, coef,
    state, beside, scaled, lines, sent, other, block, diag,
):
    lane = iota((EX, 128), 1)
    for a in range(2):
        right = jnp.concatenate([up[12 + a], from_right[a], down[12 + a]], axis=0)
        left = jnp.concatenate([up[14 + a], from_left[a], down[14 + a]], axis=0)
        for t in range(16):
            p = 16 * a + t
            if p < PLANES:
                beside[p] = jnp.where(
                    lane < 8,
                    roll(right, -8 * t, 1),
                    jnp.where(lane >= 120, roll(left, 120 - 8 * t, 1), 0.0),
                )
    jac_plane, rhs_plane, code_plane = extended_planes(
        jac, jac_up, jac_down, rhs, flags, up, down, beside
    )
    _, scale = scaled_planes(code_plane(), jac_plane)
    for f in range(F):
        scaled[f] = scale[f]
        state[f] = scale[f] * rhs_plane(f)
    sweep(state, other, scaled, rhs_plane, jac_plane)
    sweep(other, state, scaled, rhs_plane, jac_plane)
    left_over = jnp.concatenate(
        [residual(f, state, rhs_plane, jac_plane)[8 : 8 + TX] for f in range(F)], axis=0
    )
    by_column = dot(left_over, columns((EY, 128), 0, 1))
    shape = (8 * ROWS, F * TX)
    to, of = iota(shape, 0), iota(shape, 1)
    of_field = (of * 2731) >> 16
    chosen = (to % 8 == of_field) & (to // 8 == (of - TX * of_field) // 4)
    mean = dot(jnp.where(chosen, 0.0625, 0.0), by_column)

    row_lane = iota((ROWS, 128), 1)
    near, far = from_right[1, 0:ROWS, :], from_left[1, 0:ROWS, :]
    diag[...] = jnp.full((8 * ROWS, 128), 4.0, F32)
    for f in range(F):
        wide = jnp.concatenate([coef[f], coef[f]], axis=1)
        wide = jnp.where(row_lane == 64, roll(near, 64 - 120 - f, 1), wide)
        wide = jnp.where(row_lane == 65, roll(far, 65 - 120 - f, 1), wide)
        wide = jnp.where((row_lane <= 65) & (wide > 0.0), wide, 4.0)
        for k in range(ROWS):
            diag[8 * k + f : 8 * k + f + 1, :] = wide[k : k + 1, :]

    value, low, high = [], [], []
    for k in range(ROWS):
        here = mean[8 * k : 8 * k + 8]
        d = diag[8 * k : 8 * k + 8, :]
        if k == 0:
            inverse = 1.0 / d
            value.append(here * inverse)
            low.append(inverse)
        else:
            inverse = 1.0 / (d - high[-1])
            value.append((here + value[-1]) * inverse)
            low.append(low[-1] * inverse)
        high.append(inverse)
    for k in range(ROWS):
        lines[0, 8 * k : 8 * k + 8] = value[k]
        lines[1, 8 * k : 8 * k + 8] = low[k]
        lines[2, 8 * k : 8 * k + 8] = high[k]
    first, first_low = value[-1], low[-1]
    for k in range(ROWS - 2, -1, -1):
        first = value[k] + high[k] * first
        first_low = low[k] + high[k] * first_low
    parts = [first, value[-1], first_low, low[-1], high[-1]]
    lane = iota((8, 128), 1)
    ends = parts[0]
    for q in range(1, 5):
        ends = jnp.where(lane // 2 == 32 + q, roll(parts[q], 2 * q, 1), ends)
    block[...] = jnp.zeros((16, 128), F32)
    block[0:F] = jnp.where(lane < 64, parts[0], roll(parts[1], 64, 1))[0:F]
    block[F : 2 * F] = jnp.where(lane < 64, parts[2], roll(parts[3], 64, 1))[0:F]
    block[2 * F : 3 * F] = jnp.where(lane < 64, parts[4], ends)[0:F]
    whole = block[...]
    for k in range(sent.shape[0]):
        sent[k] = whole


def after_kernel(
    jac, jac_up, jac_down, rhs, flags, up, down, state_in, beside, scaled, lines, got, place,
    correction, level_residual, state, other, ends,
):
    count = got.shape[0]
    me = place[0]
    lane = iota((F, 128), 1)

    def segment(k):
        one, two, three = got[k, 0:F, :], got[k, F : 2 * F, :], got[k, 2 * F : 3 * F, :]
        main = [one, roll(one, 64, 1), two, roll(two, 64, 1), three]
        return [jnp.where(lane < 64, main[q], roll(three, -2 * q, 1)) for q in range(5)]

    def step(p, q, near, far, turn, through, back):
        w = q / (1.0 - turn * q)
        return far + through * (p + w * (near + turn * p)), back + through * through * w

    zero = jnp.zeros((F, 128), F32)
    p_low = q_low = p_high = q_high = zero
    for k in range(count - 1):
        a0, a1, b0, c, c1 = segment(k)
        p, q = step(p_low, q_low, a0, a1, b0, c, c1)
        p_low, q_low = jnp.where(k < me, p, p_low), jnp.where(k < me, q, q_low)
        j = count - 1 - k
        a0, a1, b0, c, c1 = segment(j)
        p, q = step(p_high, q_high, a1, a0, c1, c, b0)
        p_high, q_high = jnp.where(j > me, p, p_high), jnp.where(j > me, q, q_high)
    a0, a1, b0, c, c1 = segment(me)
    p, q = step(p_low, q_low, a0, a1, b0, c, c1)
    last = (p + q * p_high) / (1.0 - q * q_high)
    above = p_high + q_high * last
    first = (a0 + b0 * p_low + c * above) / (1.0 - b0 * q_low)
    below = p_low + q_low * first

    ends[...] = jnp.zeros((64, 128), F32)
    used = lane <= 65
    ends[0:F] = jnp.where(used, below, 0.0)
    ends[8 * (ROWS + 1) : 8 * (ROWS + 1) + F] = jnp.where(used, above, 0.0)
    here = above
    for k in range(ROWS - 1, -1, -1):
        rows = slice(8 * k, 8 * k + F)
        here = lines[0, rows] + lines[1, rows] * below + lines[2, rows] * here
        ends[8 * (k + 1) : 8 * (k + 1) + F] = jnp.where(used, here, 0.0)

    shape = (F * EX, 64)
    to, of = iota(shape, 0), iota(shape, 1)
    to_field = (to * 1639) >> 16
    to_row = to - EX * to_field
    chosen = (to_field == of % 8) & (to_row >= 4) & (to_row < EX - 4)
    chosen = chosen & ((to_row - 4) // 4 == of // 8)
    spread = dot(dot(chosen.astype(F32), ends[...]), columns((128, EY), 1, 0))

    jac_plane, rhs_plane, code_plane = extended_planes(
        jac, jac_up, jac_down, rhs, flags, up, down, beside
    )
    code = code_plane()
    plain = (code == 1.0) | (code == 3.0)
    interior = code == 1.0
    for f in range(F):
        kept = interior if f in (1, 2) else plain
        state[f] = state_in[f] + jnp.where(kept, spread[EX * f : EX * (f + 1)], 0.0)
    sweep(state, other, scaled, rhs_plane, jac_plane)
    sweep(other, state, scaled, rhs_plane, jac_plane)
    for f in range(F):
        correction[f] = state[f, 8 : 8 + TX, 0:TY]
        left_over = residual(f, state, rhs_plane, jac_plane)
        level_residual[f] = left_over[8 : 8 + TX, 0:TY]


def shape_of(*dims):
    return jax.ShapeDtypeStruct(dims, F32)


def call(kernel, outs, scratch, *args, scalars=0):
    vmem = pl.BlockSpec(memory_space=pltpu.VMEM)
    specs = [vmem] * (len(args) - scalars) + [pl.BlockSpec(memory_space=pltpu.SMEM)] * scalars
    return pl.pallas_call(
        kernel,
        out_shape=outs,
        in_specs=specs,
        out_specs=[vmem] * len(outs),
        scratch_shapes=scratch,
        compiler_params=pltpu.CompilerParams(vmem_limit_bytes=48 * 1024 * 1024),
    )(*args)


def shift(value, axis, step):
    count = lax.axis_size(axis)
    pairs = [(i, i + step) for i in range(count) if 0 <= i + step < count]
    return lax.ppermute(value, axis, pairs)


def local(fine, owner, flags, jac, coef):
    jac_up = shift(jac[:, :, TX - 8 :], "gx", 1)
    jac_down = shift(jac[:, :, :8], "gx", -1)
    rhs, top, bottom, left, right = call(
        restrict_kernel,
        [shape_of(F, TX, TY), shape_of(12, 8, 128), shape_of(12, 8, 128), shape_of(2, TX, 128), shape_of(2, TX, 128)],
        [pltpu.VMEM((F, 4, 2 * TX, 128), F32), pltpu.VMEM((4, 2 * TX, 128), jnp.int32)],
        fine, owner, flags, jac, coef,
    )
    from_left = shift(right, "gy", 1)
    from_right = shift(left, "gy", -1)
    top = jnp.concatenate([top, from_right[:, :8], from_left[:, :8]], axis=0)
    bottom = jnp.concatenate([bottom, from_right[:, TX - 8 :], from_left[:, TX - 8 :]], axis=0)
    up = shift(bottom, "gx", 1)
    down = shift(top, "gx", -1)
    count = lax.axis_size("gx")
    state, beside, scaled, lines, sent = call(
        before_kernel,
        [shape_of(F, EX, EY), shape_of(PLANES, EX, 128), shape_of(F, EX, EY), shape_of(3, 8 * ROWS, 128), shape_of(count, 16, 128)],
        [pltpu.VMEM((F, EX, EY), F32), pltpu.VMEM((16, 128), F32), pltpu.VMEM((8 * ROWS, 128), F32)],
        jac, jac_up, jac_down, rhs, flags, up, down, from_right, from_left, coef,
    )
    got = lax.all_to_all(sent, "gx", 0, 0, tiled=True)
    place = lax.axis_index("gx").astype(jnp.int32).reshape(1)
    return tuple(
        call(
            after_kernel,
            [shape_of(F, TX, TY), shape_of(F, TX, TY)],
            [pltpu.VMEM((F, EX, EY), F32), pltpu.VMEM((F, EX, EY), F32), pltpu.VMEM((64, 128), F32)],
            jac, jac_up, jac_down, rhs, flags, up, down, state, beside, scaled, lines, got, place,
            scalars=1,
        )
    )


def solution(mesh):
    in_specs = (
        P(None, "gx", "gy"),
        P("gx", "gy"),
        P("gx", "gy"),
        P(None, None, "gx", "gy"),
        P(None, "gx", "gy"),
    )
    out_specs = (P(None, "gx", "gy"), P(None, "gx", "gy"))
    return jax.shard_map(local, mesh=mesh, in_specs=in_specs, out_specs=out_specs, check_vma=False)
```

```python
import jax
import jax.numpy as jnp
from jax import lax
from jax.experimental import pallas as pl
from jax.experimental.pallas import tpu as pltpu
from jax.sharding import PartitionSpec as P

F = 5
TX = 24
TY = 256
EX = 40
EY = 384
ROWS = 6
PLANES = 31
HIGH = lax.Precision.HIGHEST
F32 = jnp.float32


def iota(shape, dim):
    return lax.broadcasted_iota(jnp.int32, shape, dim)


def dot(a, b):
    return jnp.dot(a, b, precision=HIGH, preferred_element_type=F32)


def roll(x, shift, axis):
    shift = shift % x.shape[axis]
    return x if shift == 0 else pltpu.roll(x, shift, axis)


def parity(axis):
    return lax.rem(lax.axis_index(axis), 2) == 1


def restrict_kernel(
    fine_in, owner_in, flags_in, jac_in, coef_in, rhs, top, bottom, near, far,
    fine, owner, flags, jac, coef, sems,
):
    copies = [
        pltpu.make_async_copy(owner_in.at[:, 128 * j : 128 * (j + 1)], owner.at[j], sems.at[j])
        for j in range(4)
    ]
    copies += [
        pltpu.make_async_copy(
            fine_in.at[:, :, 128 * j : 128 * (j + 1)], fine.at[j], sems.at[4 + j]
        )
        for j in range(4)
    ]
    late = [
        pltpu.make_async_copy(flags_in, flags, sems.at[8]),
        pltpu.make_async_copy(coef_in, coef, sems.at[9]),
        pltpu.make_async_copy(jac_in, jac, sems.at[10]),
    ]
    for copy in copies + late:
        copy.start()
    for copy in copies:
        copy.wait()

    def halves(load):
        return [
            jnp.concatenate([load(j, pl.ds(start, TX, 2)) for j in range(4)], axis=1)
            for start in (0, 1)
        ]

    shape = (TX, 2 * TY)
    row = iota(shape, 0)
    col = iota(shape, 1) // 2
    codes = [
        (o // TY - row + 1) * 3 + (o % TY) - col + 1
        for o in halves(lambda j, rows: owner[j, rows, :])
    ]
    masks = [[code == k for code in codes] for k in range(9)]
    gathered = []
    for f in range(F):
        values = halves(lambda j, rows: fine[j, f, rows, :])
        total = None
        for dy in (-1, 0, 1):
            part = None
            for dx in (-1, 0, 1):
                mask = masks[(dx + 1) * 3 + dy + 1]
                moved = jnp.where(mask[0], values[0], 0.0) + jnp.where(mask[1], values[1], 0.0)
                moved = roll(moved, dx, 0)
                part = moved if part is None else part + moved
            part = roll(part, 2 * dy, 1)
            total = part if total is None else total + part
        gathered.append(total)
    pairs = (iota((2 * TY, TY), 0) // 2 == iota((2 * TY, TY), 1)).astype(F32)
    summed = dot(jnp.concatenate(gathered, axis=0), pairs)
    planes = [summed[TX * f : TX * (f + 1)] for f in range(F)]
    for f in range(F):
        rhs[f] = planes[f]
    for copy in late:
        copy.wait()
    planes.append((flags[...] + 1).astype(F32))

    for p in range(F * F):
        top[4 * p : 4 * p + 4] = jac[p // F, p % F, 0:4, :]
        bottom[4 * p : 4 * p + 4] = jac[p // F, p % F, TX - 4 : TX, :]
    for p in range(F + 1):
        top[100 + 5 * p : 105 + 5 * p] = planes[p][0:5]
        bottom[100 + 5 * p : 105 + 5 * p] = planes[p][TX - 5 : TX]
    for f in range(F):
        top[130 + f : 131 + f] = jac[f, f, 4:5, :]
        bottom[130 + f : 131 + f] = jac[f, f, TX - 5 : TX - 4, :]
    top[135:136] = jnp.zeros((1, TY), F32)
    bottom[135:136] = jnp.zeros((1, TY), F32)

    odd = parity("gy")
    slot = iota((TX, 128), 1) // 8
    lane = iota((8, 128), 1)
    for a in range(2):
        first = jnp.zeros((TX, 128), F32)
        last = jnp.zeros((TX, 128), F32)
        for t in range(16):
            p = 16 * a + t
            if p >= PLANES:
                continue
            if p < F * F:
                head, tail = jac[p // F, p % F, :, 0:128], jac[p // F, p % F, :, TY - 128 : TY]
            else:
                head, tail = planes[p - F * F][:, 0:128], planes[p - F * F][:, TY - 128 : TY]
            first = jnp.where(slot == t, roll(head, 8 * t, 1), first)
            last = jnp.where(slot == t, roll(tail, 8 * t - 120, 1), last)
        near[a] = jnp.where(odd, first, last)
        far[a] = jnp.where(odd, last, first)
    lane = iota((ROWS, 128), 1)
    first, last = near[1, 0:ROWS, :], far[1, 0:ROWS, :]
    for f in range(F):
        wide = jnp.concatenate([coef[f], coef[f]], axis=1)
        head, tail = roll(wide, 120 + f, 1), roll(wide, 120 + f - 63, 1)
        first = jnp.where(lane == 120 + f, jnp.where(odd, head, tail), first)
        last = jnp.where(lane == 120 + f, jnp.where(odd, tail, head), last)
    near[1, 0:ROWS, :] = first
    far[1, 0:ROWS, :] = last


def extend(jac, rhs, flags, near_x, far_x, near_y, far_y, jac_all, rhs_all, scaled, sides):
    odd_x, odd_y = parity("gx"), parity("gy")
    upper, lower = (jnp.where(odd_x, near_x[...], far_x[...]), jnp.where(odd_x, far_x[...], near_x[...]))
    sides[0] = upper
    sides[1] = lower
    none = jnp.zeros((8, TY), F32)

    lane = iota((EX, 128), 1)

    def aside(p):
        return jnp.where(
            lane < 8,
            roll(right[p // 16], -8 * (p % 16), 1),
            jnp.where(lane >= 120, roll(left[p // 16], 120 - 8 * (p % 16), 1), 0.0),
        )

    right, left = [], []
    for a in range(2):
        near = jnp.concatenate(
            [sides[0, 136:144, 128 * a : 128 * (a + 1)], near_y[a], sides[1, 136:144, 128 * a : 128 * (a + 1)]],
            axis=0,
        )
        far = jnp.concatenate(
            [sides[0, 144:152, 128 * a : 128 * (a + 1)], far_y[a], sides[1, 144:152, 128 * a : 128 * (a + 1)]],
            axis=0,
        )
        right.append(jnp.where(odd_y, far, near))
        left.append(jnp.where(odd_y, near, far))

    for p in range(F * F):
        f, g = p // F, p % F
        jac_all[p, 8 : 8 + TX, 0:TY] = jac[f, g]
        jac_all[p, 0:8, 0:TY] = none
        jac_all[p, 8 + TX : EX, 0:TY] = none
        jac_all[p, 4:8, 0:TY] = sides[0, 4 * p : 4 * p + 4]
        jac_all[p, 8 + TX : 12 + TX, 0:TY] = sides[1, 4 * p : 4 * p + 4]
        if f == g:
            jac_all[p, 3:4, 0:TY] = sides[0, 130 + f : 131 + f]
            jac_all[p, 12 + TX : 13 + TX, 0:TY] = sides[1, 130 + f : 131 + f]
        jac_all[p, :, TY:EY] = aside(p)
    for f in range(F):
        rhs_all[f, 8 : 8 + TX, 0:TY] = rhs[f]
        rhs_all[f, 0:8, 0:TY] = none
        rhs_all[f, 8 + TX : EX, 0:TY] = none
        rhs_all[f, 3:8, 0:TY] = sides[0, 100 + 5 * f : 105 + 5 * f]
        rhs_all[f, 8 + TX : 13 + TX, 0:TY] = sides[1, 100 + 5 * f : 105 + 5 * f]
        rhs_all[f, :, TY:EY] = aside(F * F + f)
    code = scaled.at[0]
    code[8 : 8 + TX, 0:TY] = (flags[...] + 1).astype(F32)
    code[0:8, 0:TY] = none
    code[8 + TX : EX, 0:TY] = none
    code[3:8, 0:TY] = sides[0, 125:130]
    code[8 + TX : 13 + TX, 0:TY] = sides[1, 125:130]
    code[:, TY:EY] = aside(F * F + F)
    kinds = code[...]
    plain = (kinds == 1.0) | (kinds == 3.0)
    interior = kinds == 1.0
    for f in range(F):
        kept = interior if f in (1, 2) else plain
        scaled[f] = jnp.where(kept, 0.8 / jac_all[F * f + f], 0.0)
    return right[1][8 : 8 + ROWS], left[1][8 : 8 + ROWS]


def residual(f, state, rhs, jac):
    own = state[f]
    beside = roll(own, 1, 0) + roll(own, -1, 0) + roll(own, 1, 1) + roll(own, -1, 1)
    total = rhs[f] + beside
    for g in range(F):
        total = total - jac[F * f + g] * state[g]
    return total


def sweep(old, new, scaled, rhs, jac):
    for f in range(F):
        new[f] = old[f] + scaled[f] * residual(f, old, rhs, jac)


def columns(shape, fine_dim, coarse_dim):
    fine = iota(shape, fine_dim)
    coarse = iota(shape, coarse_dim)
    here = (coarse <= 64) & (fine // 4 == coarse)
    return (here | ((coarse == 65) & (fine >= EY - 4))).astype(F32)


def before_kernel(
    jac_in, rhs_in, flags, near_x, far_x, near_y, far_y, coef,
    state, jac, rhs, scaled, lines, sent, other, sides, block, diag,
):
    near, far = extend(
        jac_in, rhs_in, flags, near_x, far_x, near_y, far_y, jac, rhs, scaled, sides
    )
    for f in range(F):
        state[f] = scaled[f] * rhs[f]
    sweep(state, other, scaled, rhs, jac)
    sweep(other, state, scaled, rhs, jac)
    left_over = jnp.concatenate(
        [residual(f, state, rhs, jac)[8 : 8 + TX] for f in range(F)], axis=0
    )
    by_column = dot(left_over, columns((EY, 128), 0, 1))
    shape = (8 * ROWS, F * TX)
    to, of = iota(shape, 0), iota(shape, 1)
    of_field = (of * 2731) >> 16
    chosen = (to % 8 == of_field) & (to // 8 == (of - TX * of_field) // 4)
    mean = dot(jnp.where(chosen, 0.0625, 0.0), by_column)

    row_lane = iota((ROWS, 128), 1)
    diag[...] = jnp.full((8 * ROWS, 128), 4.0, F32)
    for f in range(F):
        wide = jnp.concatenate([coef[f], coef[f]], axis=1)
        wide = jnp.where(row_lane == 64, roll(near, 64 - 120 - f, 1), wide)
        wide = jnp.where(row_lane == 65, roll(far, 65 - 120 - f, 1), wide)
        wide = jnp.where((row_lane <= 65) & (wide > 0.0), wide, 4.0)
        for k in range(ROWS):
            diag[8 * k + f : 8 * k + f + 1, :] = wide[k : k + 1, :]

    value, low, high = [], [], []
    for k in range(ROWS):
        here = mean[8 * k : 8 * k + 8]
        d = diag[8 * k : 8 * k + 8, :]
        if k == 0:
            inverse = 1.0 / d
            value.append(here * inverse)
            low.append(inverse)
        else:
            inverse = 1.0 / (d - high[-1])
            value.append((here + value[-1]) * inverse)
            low.append(low[-1] * inverse)
        high.append(inverse)
    for k in range(ROWS):
        lines[0, 8 * k : 8 * k + 8] = value[k]
        lines[1, 8 * k : 8 * k + 8] = low[k]
        lines[2, 8 * k : 8 * k + 8] = high[k]
    first, first_low = value[-1], low[-1]
    for k in range(ROWS - 2, -1, -1):
        first = value[k] + high[k] * first
        first_low = low[k] + high[k] * first_low
    parts = [first, value[-1], first_low, low[-1], high[-1]]
    lane = iota((8, 128), 1)
    ends = parts[0]
    for q in range(1, 5):
        ends = jnp.where(lane // 2 == 32 + q, roll(parts[q], 2 * q, 1), ends)
    block[...] = jnp.zeros((16, 128), F32)
    block[0:F] = jnp.where(lane < 64, parts[0], roll(parts[1], 64, 1))[0:F]
    block[F : 2 * F] = jnp.where(lane < 64, parts[2], roll(parts[3], 64, 1))[0:F]
    block[2 * F : 3 * F] = jnp.where(lane < 64, parts[4], ends)[0:F]
    whole = block[...]
    for k in range(sent.shape[0]):
        sent[k] = whole


def after_kernel(
    jac, rhs, scaled, state_in, lines, got, correction, level_residual, state, other, ends
):
    count = got.shape[0]
    me = lax.axis_index("gx")
    lane = iota((F, 128), 1)

    def segment(k):
        one, two, three = got[k, 0:F, :], got[k, F : 2 * F, :], got[k, 2 * F : 3 * F, :]
        main = [one, roll(one, 64, 1), two, roll(two, 64, 1), three]
        return [jnp.where(lane < 64, main[q], roll(three, -2 * q, 1)) for q in range(5)]

    def step(p, q, near, far, turn, through, back):
        w = q / (1.0 - turn * q)
        return far + through * (p + w * (near + turn * p)), back + through * through * w

    zero = jnp.zeros((F, 128), F32)
    p_low = q_low = p_high = q_high = zero
    for k in range(count - 1):
        a0, a1, b0, c, c1 = segment(k)
        p, q = step(p_low, q_low, a0, a1, b0, c, c1)
        p_low, q_low = jnp.where(k < me, p, p_low), jnp.where(k < me, q, q_low)
        j = count - 1 - k
        a0, a1, b0, c, c1 = segment(j)
        p, q = step(p_high, q_high, a1, a0, c1, c, b0)
        p_high, q_high = jnp.where(j > me, p, p_high), jnp.where(j > me, q, q_high)
    a0, a1, b0, c, c1 = segment(me)
    p, q = step(p_low, q_low, a0, a1, b0, c, c1)
    last = (p + q * p_high) / (1.0 - q * q_high)
    above = p_high + q_high * last
    first = (a0 + b0 * p_low + c * above) / (1.0 - b0 * q_low)
    below = p_low + q_low * first

    ends[...] = jnp.zeros((64, 128), F32)
    used = lane <= 65
    ends[0:F] = jnp.where(used, below, 0.0)
    ends[8 * (ROWS + 1) : 8 * (ROWS + 1) + F] = jnp.where(used, above, 0.0)
    here = above
    for k in range(ROWS - 1, -1, -1):
        rows = slice(8 * k, 8 * k + F)
        here = lines[0, rows] + lines[1, rows] * below + lines[2, rows] * here
        ends[8 * (k + 1) : 8 * (k + 1) + F] = jnp.where(used, here, 0.0)

    shape = (F * EX, 64)
    to, of = iota(shape, 0), iota(shape, 1)
    to_field = (to * 1639) >> 16
    to_row = to - EX * to_field
    chosen = (to_field == of % 8) & (to_row >= 4) & (to_row < EX - 4)
    chosen = chosen & ((to_row - 4) // 4 == of // 8)
    spread = dot(dot(chosen.astype(F32), ends[...]), columns((128, EY), 1, 0))

    for f in range(F):
        added = jnp.where(scaled[f] != 0.0, spread[EX * f : EX * (f + 1)], 0.0)
        state[f] = state_in[f] + added
    sweep(state, other, scaled, rhs, jac)
    sweep(other, state, scaled, rhs, jac)
    for f in range(F):
        correction[f] = state[f, 8 : 8 + TX, 0:TY]
        level_residual[f] = residual(f, state, rhs, jac)[8 : 8 + TX, 0:TY]


def shape_of(*dims):
    return jax.ShapeDtypeStruct(dims, F32)


def call(kernel, outs, scratch, *args, space=pltpu.VMEM):
    return pl.pallas_call(
        kernel,
        out_shape=outs,
        in_specs=[pl.BlockSpec(memory_space=space)] * len(args),
        out_specs=[pl.BlockSpec(memory_space=pltpu.VMEM)] * len(outs),
        scratch_shapes=scratch,
        compiler_params=pltpu.CompilerParams(vmem_limit_bytes=48 * 1024 * 1024),
    )(*args)


def swap(value, axis, start):
    count = lax.axis_size(axis)
    firsts = range(start, count - 1, 2)
    return lax.ppermute(value, axis, [(i, i + 1) for i in firsts] + [(i + 1, i) for i in firsts])


def local(fine, owner, flags, jac, coef):
    strip = shape_of(2, TX, 128)
    rows = shape_of(136, TY)
    rhs, top, bottom, near, far = call(
        restrict_kernel,
        [shape_of(F, TX, TY), rows, rows, strip, strip],
        [
            pltpu.VMEM((4, F, 2 * TX, 128), F32),
            pltpu.VMEM((4, 2 * TX, 128), jnp.int32),
            pltpu.VMEM((TX, TY), jnp.int32),
            pltpu.VMEM((F, F, TX, TY), F32),
            pltpu.VMEM((F, ROWS, TY // 4), F32),
            pltpu.SemaphoreType.DMA((11,)),
        ],
        fine, owner, flags, jac, coef,
        space=pl.ANY,
    )
    near_y = swap(near, "gy", 0)
    far_y = swap(far, "gy", 1)

    def with_corners(own, rows):
        corners = [jnp.concatenate([side[0, rows], side[1, rows]], axis=1) for side in (near_y, far_y)]
        return jnp.concatenate([own, *corners], axis=0)

    top = with_corners(top, slice(0, 8))
    bottom = with_corners(bottom, slice(TX - 8, TX))
    odd = parity("gx")
    near_x = swap(jnp.where(odd, top, bottom), "gx", 0)
    far_x = swap(jnp.where(odd, bottom, top), "gx", 1)
    count = lax.axis_size("gx")
    tile = shape_of(F, EX, EY)
    state, jac_all, rhs_all, scaled, lines, sent = call(
        before_kernel,
        [tile, shape_of(F * F, EX, EY), tile, tile, shape_of(3, 8 * ROWS, 128), shape_of(count, 16, 128)],
        [
            pltpu.VMEM((F, EX, EY), F32),
            pltpu.VMEM((2, 152, TY), F32),
            pltpu.VMEM((16, 128), F32),
            pltpu.VMEM((8 * ROWS, 128), F32),
        ],
        jac, rhs, flags, near_x, far_x, near_y, far_y, coef,
    )
    got = lax.all_to_all(sent, "gx", 0, 0, tiled=True)
    tile = pltpu.VMEM((F, EX, EY), F32)
    return tuple(
        call(
            after_kernel,
            [shape_of(F, TX, TY), shape_of(F, TX, TY)],
            [tile, tile, pltpu.VMEM((64, 128), F32)],
            jac_all, rhs_all, scaled, state, lines, got,
        )
    )


def solution(mesh):
    in_specs = (
        P(None, "gx", "gy"),
        P("gx", "gy"),
        P("gx", "gy"),
        P(None, None, "gx", "gy"),
        P(None, "gx", "gy"),
    )
    out_specs = (P(None, "gx", "gy"), P(None, "gx", "gy"))
    return jax.shard_map(local, mesh=mesh, in_specs=in_specs, out_specs=out_specs, check_vma=False)
```

```python
import jax
import jax.numpy as jnp
from jax import lax
from jax.experimental import pallas as pl
from jax.experimental.pallas import tpu as pltpu
from jax.sharding import PartitionSpec as P

F = 5
TX = 24
TY = 256
EX = 40
EY = 384
ROWS = 6
PLANES = 31
HIGH = lax.Precision.HIGHEST
F32 = jnp.float32


def iota(shape, dim):
    return lax.broadcasted_iota(jnp.int32, shape, dim)


def dot(a, b):
    return jnp.dot(a, b, precision=HIGH, preferred_element_type=F32)


def roll(x, shift, axis):
    shift = shift % x.shape[axis]
    return x if shift == 0 else pltpu.roll(x, shift, axis)


def parity(axis):
    return lax.rem(lax.axis_index(axis), 2) == 1


def restrict_kernel(
    fine_in, owner_in, flags_in, jac_in, coef_in, rhs, top, bottom, near, far,
    fine, owner, flags, jac, coef, sems,
):
    copies = [
        pltpu.make_async_copy(owner_in.at[:, 128 * j : 128 * (j + 1)], owner.at[j], sems.at[j])
        for j in range(4)
    ]
    copies += [
        pltpu.make_async_copy(
            fine_in.at[:, :, 128 * j : 128 * (j + 1)], fine.at[j], sems.at[4 + j]
        )
        for j in range(4)
    ]
    late = [
        pltpu.make_async_copy(flags_in, flags, sems.at[8]),
        pltpu.make_async_copy(coef_in, coef, sems.at[9]),
        pltpu.make_async_copy(jac_in, jac, sems.at[10]),
    ]
    for copy in copies + late:
        copy.start()
    for copy in copies:
        copy.wait()

    def halves(load):
        return [
            jnp.concatenate([load(j, pl.ds(start, TX, 2)) for j in range(4)], axis=1)
            for start in (0, 1)
        ]

    shape = (TX, 2 * TY)
    row = iota(shape, 0)
    col = iota(shape, 1) // 2
    codes = [
        (o // TY - row + 1) * 3 + (o % TY) - col + 1
        for o in halves(lambda j, rows: owner[j, rows, :])
    ]
    masks = [[code == k for code in codes] for k in range(9)]
    gathered = []
    for f in range(F):
        values = halves(lambda j, rows: fine[j, f, rows, :])
        total = None
        for dy in (-1, 0, 1):
            part = None
            for dx in (-1, 0, 1):
                mask = masks[(dx + 1) * 3 + dy + 1]
                moved = jnp.where(mask[0], values[0], 0.0) + jnp.where(mask[1], values[1], 0.0)
                moved = roll(moved, dx, 0)
                part = moved if part is None else part + moved
            part = roll(part, 2 * dy, 1)
            total = part if total is None else total + part
        gathered.append(total)
    pairs = (iota((2 * TY, TY), 0) // 2 == iota((2 * TY, TY), 1)).astype(F32)
    summed = dot(jnp.concatenate(gathered, axis=0), pairs)
    planes = [summed[TX * f : TX * (f + 1)] for f in range(F)]
    for f in range(F):
        rhs[f] = planes[f]
    for copy in late:
        copy.wait()
    planes.append((flags[...] + 1).astype(F32))

    for p in range(F * F):
        top[4 * p : 4 * p + 4] = jac[p // F, p % F, 0:4, :]
        bottom[4 * p : 4 * p + 4] = jac[p // F, p % F, TX - 4 : TX, :]
    for p in range(F + 1):
        top[100 + 5 * p : 105 + 5 * p] = planes[p][0:5]
        bottom[100 + 5 * p : 105 + 5 * p] = planes[p][TX - 5 : TX]
    for f in range(F):
        top[130 + f : 131 + f] = jac[f, f, 4:5, :]
        bottom[130 + f : 131 + f] = jac[f, f, TX - 5 : TX - 4, :]
    top[135:136] = jnp.zeros((1, TY), F32)
    bottom[135:136] = jnp.zeros((1, TY), F32)

    odd = parity("gy")
    slot = iota((TX, 128), 1) // 8
    lane = iota((8, 128), 1)
    for a in range(2):
        first = jnp.zeros((TX, 128), F32)
        last = jnp.zeros((TX, 128), F32)
        for t in range(16):
            p = 16 * a + t
            if p >= PLANES:
                continue
            if p < F * F:
                head, tail = jac[p // F, p % F, :, 0:128], jac[p // F, p % F, :, TY - 128 : TY]
            else:
                head, tail = planes[p - F * F][:, 0:128], planes[p - F * F][:, TY - 128 : TY]
            first = jnp.where(slot == t, roll(head, 8 * t, 1), first)
            last = jnp.where(slot == t, roll(tail, 8 * t - 120, 1), last)
        near[a] = jnp.where(odd, first, last)
        far[a] = jnp.where(odd, last, first)
    lane = iota((ROWS, 128), 1)
    first, last = near[1, 0:ROWS, :], far[1, 0:ROWS, :]
    for f in range(F):
        wide = jnp.concatenate([coef[f], coef[f]], axis=1)
        head, tail = roll(wide, 120 + f, 1), roll(wide, 120 + f - 63, 1)
        first = jnp.where(lane == 120 + f, jnp.where(odd, head, tail), first)
        last = jnp.where(lane == 120 + f, jnp.where(odd, tail, head), last)
    near[1, 0:ROWS, :] = first
    far[1, 0:ROWS, :] = last


def extend(jac, rhs, flags, near_x, far_x, near_y, far_y, jac_all, rhs_all, scaled, sides):
    odd_x, odd_y = parity("gx"), parity("gy")
    upper, lower = (jnp.where(odd_x, near_x[...], far_x[...]), jnp.where(odd_x, far_x[...], near_x[...]))
    sides[0] = upper
    sides[1] = lower
    none = jnp.zeros((8, TY), F32)

    lane = iota((EX, 128), 1)

    def aside(p):
        return jnp.where(
            lane < 8,
            roll(right[p // 16], -8 * (p % 16), 1),
            jnp.where(lane >= 120, roll(left[p // 16], 120 - 8 * (p % 16), 1), 0.0),
        )

    right, left = [], []
    for a in range(2):
        near = jnp.concatenate(
            [sides[0, 144:152, 128 * a : 128 * (a + 1)], near_y[a], sides[1, 144:152, 128 * a : 128 * (a + 1)]],
            axis=0,
        )
        far = jnp.concatenate(
            [sides[0, 136:144, 128 * a : 128 * (a + 1)], far_y[a], sides[1, 136:144, 128 * a : 128 * (a + 1)]],
            axis=0,
        )
        right.append(jnp.where(odd_y, far, near))
        left.append(jnp.where(odd_y, near, far))

    for p in range(F * F):
        f, g = p // F, p % F
        jac_all[p, 8 : 8 + TX, 0:TY] = jac[f, g]
        jac_all[p, 0:8, 0:TY] = none
        jac_all[p, 8 + TX : EX, 0:TY] = none
        jac_all[p, 4:8, 0:TY] = sides[0, 4 * p : 4 * p + 4]
        jac_all[p, 8 + TX : 12 + TX, 0:TY] = sides[1, 4 * p : 4 * p + 4]
        if f == g:
            jac_all[p, 3:4, 0:TY] = sides[0, 130 + f : 131 + f]
            jac_all[p, 12 + TX : 13 + TX, 0:TY] = sides[1, 130 + f : 131 + f]
        jac_all[p, :, TY:EY] = aside(p)
    for f in range(F):
        rhs_all[f, 8 : 8 + TX, 0:TY] = rhs[f]
        rhs_all[f, 0:8, 0:TY] = none
        rhs_all[f, 8 + TX : EX, 0:TY] = none
        rhs_all[f, 3:8, 0:TY] = sides[0, 100 + 5 * f : 105 + 5 * f]
        rhs_all[f, 8 + TX : 13 + TX, 0:TY] = sides[1, 100 + 5 * f : 105 + 5 * f]
        rhs_all[f, :, TY:EY] = aside(F * F + f)
    code = scaled.at[0]
    code[8 : 8 + TX, 0:TY] = (flags[...] + 1).astype(F32)
    code[0:8, 0:TY] = none
    code[8 + TX : EX, 0:TY] = none
    code[3:8, 0:TY] = sides[0, 125:130]
    code[8 + TX : 13 + TX, 0:TY] = sides[1, 125:130]
    code[:, TY:EY] = aside(F * F + F)
    kinds = code[...]
    plain = (kinds == 1.0) | (kinds == 3.0)
    interior = kinds == 1.0
    for f in range(F):
        kept = interior if f in (1, 2) else plain
        scaled[f] = jnp.where(kept, 0.8 / jac_all[F * f + f], 0.0)
    return right[1][8 : 8 + ROWS], left[1][8 : 8 + ROWS]


def residual(f, state, rhs, jac):
    own = state[f]
    beside = roll(own, 1, 0) + roll(own, -1, 0) + roll(own, 1, 1) + roll(own, -1, 1)
    total = rhs[f] + beside
    for g in range(F):
        total = total - jac[F * f + g] * state[g]
    return total


def sweep(old, new, scaled, rhs, jac):
    for f in range(F):
        new[f] = old[f] + scaled[f] * residual(f, old, rhs, jac)


def columns(shape, fine_dim, coarse_dim):
    fine = iota(shape, fine_dim)
    coarse = iota(shape, coarse_dim)
    here = (coarse <= 64) & (fine // 4 == coarse)
    return (here | ((coarse == 65) & (fine >= EY - 4))).astype(F32)


def before_kernel(
    jac_in, rhs_in, flags, far_x, near_x, far_y, near_y, coef,
    state, jac, rhs, scaled, lines, sent, other, sides, block, diag,
):
    near, far = extend(
        jac_in, rhs_in, flags, near_x, far_x, near_y, far_y, jac, rhs, scaled, sides
    )
    for f in range(F):
        state[f] = scaled[f] * rhs[f]
    sweep(state, other, scaled, rhs, jac)
    sweep(other, state, scaled, rhs, jac)
    left_over = jnp.concatenate(
        [residual(f, state, rhs, jac)[8 : 8 + TX] for f in range(F)], axis=0
    )
    by_column = dot(left_over, columns((EY, 128), 0, 1))
    shape = (8 * ROWS, F * TX)
    to, of = iota(shape, 0), iota(shape, 1)
    of_field = (of * 2731) >> 16
    chosen = (to % 8 == of_field) & (to // 8 == (of - TX * of_field) // 4)
    mean = dot(jnp.where(chosen, 0.0625, 0.0), by_column)

    row_lane = iota((ROWS, 128), 1)
    diag[...] = jnp.full((8 * ROWS, 128), 4.0, F32)
    for f in range(F):
        wide = jnp.concatenate([coef[f], coef[f]], axis=1)
        wide = jnp.where(row_lane == 64, roll(near, 64 - 120 - f, 1), wide)
        wide = jnp.where(row_lane == 65, roll(far, 65 - 120 - f, 1), wide)
        wide = jnp.where((row_lane <= 65) & (wide > 0.0), wide, 4.0)
        for k in range(ROWS):
            diag[8 * k + f : 8 * k + f + 1, :] = wide[k : k + 1, :]

    value, low, high = [], [], []
    for k in range(ROWS):
        here = mean[8 * k : 8 * k + 8]
        d = diag[8 * k : 8 * k + 8, :]
        if k == 0:
            inverse = 1.0 / d
            value.append(here * inverse)
            low.append(inverse)
        else:
            inverse = 1.0 / (d - high[-1])
            value.append((here + value[-1]) * inverse)
            low.append(low[-1] * inverse)
        high.append(inverse)
    for k in range(ROWS):
        lines[0, 8 * k : 8 * k + 8] = value[k]
        lines[1, 8 * k : 8 * k + 8] = low[k]
        lines[2, 8 * k : 8 * k + 8] = high[k]
    first, first_low = value[-1], low[-1]
    for k in range(ROWS - 2, -1, -1):
        first = value[k] + high[k] * first
        first_low = low[k] + high[k] * first_low
    parts = [first, value[-1], first_low, low[-1], high[-1]]
    lane = iota((8, 128), 1)
    ends = parts[0]
    for q in range(1, 5):
        ends = jnp.where(lane // 2 == 32 + q, roll(parts[q], 2 * q, 1), ends)
    block[...] = jnp.zeros((16, 128), F32)
    block[0:F] = jnp.where(lane < 64, parts[0], roll(parts[1], 64, 1))[0:F]
    block[F : 2 * F] = jnp.where(lane < 64, parts[2], roll(parts[3], 64, 1))[0:F]
    block[2 * F : 3 * F] = jnp.where(lane < 64, parts[4], ends)[0:F]
    whole = block[...]
    for k in range(sent.shape[0]):
        sent[k] = whole


def after_kernel(
    jac, rhs, scaled, state_in, lines, got, correction, level_residual, state, other, ends
):
    count = got.shape[0]
    me = lax.axis_index("gx")
    lane = iota((F, 128), 1)

    def segment(k):
        one, two, three = got[k, 0:F, :], got[k, F : 2 * F, :], got[k, 2 * F : 3 * F, :]
        main = [one, roll(one, 64, 1), two, roll(two, 64, 1), three]
        return [jnp.where(lane < 64, main[q], roll(three, -2 * q, 1)) for q in range(5)]

    def step(p, q, near, far, turn, through, back):
        w = q / (1.0 - turn * q)
        return far + through * (p + w * (near + turn * p)), back + through * through * w

    zero = jnp.zeros((F, 128), F32)
    p_low = q_low = p_high = q_high = zero
    for k in range(count - 1):
        a0, a1, b0, c, c1 = segment(k)
        p, q = step(p_low, q_low, a0, a1, b0, c, c1)
        p_low, q_low = jnp.where(k < me, p, p_low), jnp.where(k < me, q, q_low)
        j = count - 1 - k
        a0, a1, b0, c, c1 = segment(j)
        p, q = step(p_high, q_high, a1, a0, c1, c, b0)
        p_high, q_high = jnp.where(j > me, p, p_high), jnp.where(j > me, q, q_high)
    a0, a1, b0, c, c1 = segment(me)
    p, q = step(p_low, q_low, a0, a1, b0, c, c1)
    last = (p + q * p_high) / (1.0 - q * q_high)
    above = p_high + q_high * last
    first = (a0 + b0 * p_low + c * above) / (1.0 - b0 * q_low)
    below = p_low + q_low * first

    ends[...] = jnp.zeros((64, 128), F32)
    used = lane <= 65
    ends[0:F] = jnp.where(used, below, 0.0)
    ends[8 * (ROWS + 1) : 8 * (ROWS + 1) + F] = jnp.where(used, above, 0.0)
    here = above
    for k in range(ROWS - 1, -1, -1):
        rows = slice(8 * k, 8 * k + F)
        here = lines[0, rows] + lines[1, rows] * below + lines[2, rows] * here
        ends[8 * (k + 1) : 8 * (k + 1) + F] = jnp.where(used, here, 0.0)

    shape = (F * EX, 64)
    to, of = iota(shape, 0), iota(shape, 1)
    to_field = (to * 1639) >> 16
    to_row = to - EX * to_field
    chosen = (to_field == of % 8) & (to_row >= 4) & (to_row < EX - 4)
    chosen = chosen & ((to_row - 4) // 4 == of // 8)
    spread = dot(dot(chosen.astype(F32), ends[...]), columns((128, EY), 1, 0))

    for f in range(F):
        added = jnp.where(scaled[f] != 0.0, spread[EX * f : EX * (f + 1)], 0.0)
        state[f] = state_in[f] + added
    sweep(state, other, scaled, rhs, jac)
    sweep(other, state, scaled, rhs, jac)
    for f in range(F):
        correction[f] = state[f, 8 : 8 + TX, 0:TY]
        level_residual[f] = residual(f, state, rhs, jac)[8 : 8 + TX, 0:TY]


def shape_of(*dims):
    return jax.ShapeDtypeStruct(dims, F32)


def call(kernel, outs, scratch, *args, space=pltpu.VMEM, limit=32 * 1024 * 1024):
    return pl.pallas_call(
        kernel,
        out_shape=outs,
        in_specs=[pl.BlockSpec(memory_space=space)] * len(args),
        out_specs=[pl.BlockSpec(memory_space=pltpu.VMEM)] * len(outs),
        scratch_shapes=scratch,
        compiler_params=pltpu.CompilerParams(vmem_limit_bytes=limit),
    )(*args)


def swap(value, axis, start):
    count = lax.axis_size(axis)
    firsts = range(start, count - 1, 2)
    return lax.ppermute(value, axis, [(i, i + 1) for i in firsts] + [(i + 1, i) for i in firsts])


def local(fine, owner, flags, jac, coef):
    strip = shape_of(2, TX, 128)
    rows = shape_of(136, TY)
    rhs, top, bottom, near, far = call(
        restrict_kernel,
        [shape_of(F, TX, TY), rows, rows, strip, strip],
        [
            pltpu.VMEM((4, F, 2 * TX, 128), F32),
            pltpu.VMEM((4, 2 * TX, 128), jnp.int32),
            pltpu.VMEM((TX, TY), jnp.int32),
            pltpu.VMEM((F, F, TX, TY), F32),
            pltpu.VMEM((F, ROWS, TY // 4), F32),
            pltpu.SemaphoreType.DMA((11,)),
        ],
        *[pltpu.with_memory_space_constraint(x, pltpu.HBM) for x in (fine, owner, flags, jac, coef)],
        space=pltpu.HBM,
    )
    far_y = swap(far, "gy", 1)
    near_y = swap(near, "gy", 0)

    def with_corners(own, rows):
        corners = [jnp.concatenate([side[0, rows], side[1, rows]], axis=1) for side in (far_y, near_y)]
        return jnp.concatenate([own, *corners], axis=0)

    top = with_corners(top, slice(0, 8))
    bottom = with_corners(bottom, slice(TX - 8, TX))
    odd = parity("gx")
    far_x = swap(jnp.where(odd, bottom, top), "gx", 1)
    near_x = swap(jnp.where(odd, top, bottom), "gx", 0)
    count = lax.axis_size("gx")
    tile = shape_of(F, EX, EY)
    state, jac_all, rhs_all, scaled, lines, sent = call(
        before_kernel,
        [tile, shape_of(F * F, EX, EY), tile, tile, shape_of(3, 8 * ROWS, 128), shape_of(count, 16, 128)],
        [
            pltpu.VMEM((F, EX, EY), F32),
            pltpu.VMEM((2, 152, TY), F32),
            pltpu.VMEM((16, 128), F32),
            pltpu.VMEM((8 * ROWS, 128), F32),
        ],
        jac, rhs, flags, far_x, near_x, far_y, near_y, coef,
    )
    got = lax.all_to_all(sent, "gx", 0, 0, tiled=True)
    tile = pltpu.VMEM((F, EX, EY), F32)
    return tuple(
        call(
            after_kernel,
            [shape_of(F, TX, TY), shape_of(F, TX, TY)],
            [tile, tile, pltpu.VMEM((64, 128), F32)],
            jac_all, rhs_all, scaled, state, lines, got,
        )
    )


def solution(mesh):
    in_specs = (
        P(None, "gx", "gy"),
        P("gx", "gy"),
        P("gx", "gy"),
        P(None, None, "gx", "gy"),
        P(None, "gx", "gy"),
    )
    out_specs = (P(None, "gx", "gy"), P(None, "gx", "gy"))
    return jax.shard_map(local, mesh=mesh, in_specs=in_specs, out_specs=out_specs, check_vma=False)
```

```python
import jax
import jax.numpy as jnp
from jax import lax
from jax.experimental import pallas as pl
from jax.experimental.pallas import tpu as pltpu
from jax.sharding import PartitionSpec as P

F = 5
TX = 24
TY = 256
EX = 40
EY = 384
ROWS = 6
PLANES = 31
F32 = jnp.float32


def iota(shape, dim):
    return lax.broadcasted_iota(jnp.int32, shape, dim)


def parts_of(x):
    head = x.astype(jnp.bfloat16)
    rest = x - head.astype(F32)
    middle = rest.astype(jnp.bfloat16)
    return head, middle, (rest - middle.astype(F32)).astype(jnp.bfloat16)


def select_columns(x, chosen):
    rows = x.shape[0]
    whole = jnp.concatenate(parts_of(x), axis=0)
    out = jnp.dot(whole, chosen.astype(jnp.bfloat16), preferred_element_type=F32)
    return out[0:rows] + out[rows : 2 * rows] + out[2 * rows :]


def roll(x, shift, axis):
    shift = shift % x.shape[axis]
    return x if shift == 0 else pltpu.roll(x, shift, axis)


def parity(axis):
    return lax.rem(lax.axis_index(axis), 2) == 1


def restrict_kernel(
    fine_in, owner_in, flags_in, jac_in, coef_in, rhs, top, bottom, near, far,
    fine, owner, flags, jac, coef, sems,
):
    def tile_copy(source, target, sem, j):
        return pltpu.make_async_copy(source.at[:, 128 * j : 128 * (j + 1)], target.at[j], sem)

    owners = [tile_copy(owner_in, owner, sems.at[0, j], j) for j in range(4)]
    fines = [
        [tile_copy(fine_in.at[f], fine.at[f], sems.at[1 + f, j], j) for j in range(4)]
        for f in range(F)
    ]
    late = [
        pltpu.make_async_copy(flags_in, flags, sems.at[F + 1, 0]),
        pltpu.make_async_copy(coef_in, coef, sems.at[F + 1, 1]),
        pltpu.make_async_copy(jac_in, jac, sems.at[F + 1, 2]),
    ]
    for copy in owners + sum(fines, []) + late:
        copy.start()
    for copy in owners:
        copy.wait()

    def halves(load):
        return [
            jnp.concatenate([load(j, pl.ds(start, TX, 2)) for j in range(4)], axis=1)
            for start in (0, 1)
        ]

    shape = (TX, 2 * TY)
    row = iota(shape, 0)
    col = iota(shape, 1) >> 1
    codes = [
        ((o >> 8) - row + 1) * 3 + (o & (TY - 1)) - col + 1
        for o in halves(lambda j, rows: owner[j, rows, :])
    ]
    masks = [[code == k for code in codes] for k in range(9)]
    gathered = []
    for f in range(F):
        for copy in fines[f]:
            copy.wait()
        values = halves(lambda j, rows: fine[f, j, rows, :])
        total = None
        for dy in (-1, 0, 1):
            part = None
            for dx in (-1, 0, 1):
                mask = masks[(dx + 1) * 3 + dy + 1]
                moved = jnp.where(mask[0], values[0], 0.0) + jnp.where(mask[1], values[1], 0.0)
                moved = roll(moved, dx, 0)
                part = moved if part is None else part + moved
            part = roll(part, 2 * dy, 1)
            total = part if total is None else total + part
        gathered.append(total)
    pairs = ((iota((2 * TY, TY), 0) >> 1) == iota((2 * TY, TY), 1)).astype(F32)
    gathered.append(jnp.zeros((8, 2 * TY), F32))
    summed = select_columns(jnp.concatenate(gathered, axis=0), pairs)
    planes = [summed[TX * f : TX * (f + 1)] for f in range(F)]
    for f in range(F):
        rhs[f] = planes[f]
    for copy in late:
        copy.wait()
    planes.append((flags[...] + 1).astype(F32))

    for p in range(F * F):
        top[4 * p : 4 * p + 4] = jac[p // F, p % F, 0:4, :]
        bottom[4 * p : 4 * p + 4] = jac[p // F, p % F, TX - 4 : TX, :]
    for p in range(F + 1):
        top[100 + 5 * p : 105 + 5 * p] = planes[p][0:5]
        bottom[100 + 5 * p : 105 + 5 * p] = planes[p][TX - 5 : TX]
    for f in range(F):
        top[130 + f : 131 + f] = jac[f, f, 4:5, :]
        bottom[130 + f : 131 + f] = jac[f, f, TX - 5 : TX - 4, :]
    top[135:136] = jnp.zeros((1, TY), F32)
    bottom[135:136] = jnp.zeros((1, TY), F32)

    odd = parity("gy")
    slot = iota((TX, 128), 1) >> 3
    for a in range(2):
        first = jnp.zeros((TX, 128), F32)
        last = jnp.zeros((TX, 128), F32)
        for t in range(16):
            p = 16 * a + t
            if p >= PLANES:
                continue
            if p < F * F:
                head, tail = jac[p // F, p % F, :, 0:128], jac[p // F, p % F, :, TY - 128 : TY]
            else:
                head, tail = planes[p - F * F][:, 0:128], planes[p - F * F][:, TY - 128 : TY]
            first = jnp.where(slot == t, roll(head, 8 * t, 1), first)
            last = jnp.where(slot == t, roll(tail, 8 * t - 120, 1), last)
        near[a] = jnp.where(odd, first, last)
        far[a] = jnp.where(odd, last, first)
    lane = iota((ROWS, 128), 1)
    first, last = near[1, 0:ROWS, :], far[1, 0:ROWS, :]
    for f in range(F):
        wide = jnp.concatenate([coef[f], coef[f]], axis=1)
        head, tail = roll(wide, 120 + f, 1), roll(wide, 120 + f - 63, 1)
        first = jnp.where(lane == 120 + f, jnp.where(odd, head, tail), first)
        last = jnp.where(lane == 120 + f, jnp.where(odd, tail, head), last)
    near[1, 0:ROWS, :] = first
    far[1, 0:ROWS, :] = last


def unpack(near, far, p):
    odd = parity("gy")
    right = jnp.where(odd, far, near)
    left = jnp.where(odd, near, far)
    lane = iota(near.shape, 1)
    return jnp.where(
        lane < 8,
        roll(right, -8 * (p % 16), 1),
        jnp.where(lane >= 120, roll(left, 120 - 8 * (p % 16), 1), 0.0),
    )


def scale(code, jac, scaled):
    plain = (code == 1.0) | (code == 3.0)
    interior = code == 1.0
    for f in range(F):
        kept = interior if f in (1, 2) else plain
        scaled[f] = jnp.where(kept, 0.8 / jac[F * f + f], 0.0)


def own_kernel(
    jac_in, rhs_in, flags, far_y, near_y, coef, jac, rhs, scaled, low, high, block, diag
):
    near, far = [near_y[0], near_y[1]], [far_y[0], far_y[1]]
    for p in range(F * F):
        jac[p, :, 0:TY] = jac_in[p // F, p % F]
        jac[p, :, TY:EY] = unpack(near[p // 16], far[p // 16], p)
    for f in range(F):
        rhs[f, :, 0:TY] = rhs_in[f]
        rhs[f, :, TY:EY] = unpack(near[1], far[1], F * F + f)
    aside = unpack(near[1], far[1], F * F + F)
    code = jnp.concatenate([(flags[...] + 1).astype(F32), aside], axis=1)
    scale(code, jac, scaled)

    lane = iota((ROWS, 128), 1)
    odd = parity("gy")
    right = jnp.where(odd, far[1], near[1])[0:ROWS]
    left = jnp.where(odd, near[1], far[1])[0:ROWS]
    diag[...] = jnp.full((8 * ROWS, 128), 4.0, F32)
    for f in range(F):
        wide = jnp.concatenate([coef[f], coef[f]], axis=1)
        wide = jnp.where(lane == 64, roll(right, 64 - 120 - f, 1), wide)
        wide = jnp.where(lane == 65, roll(left, 65 - 120 - f, 1), wide)
        wide = jnp.where((lane <= 65) & (wide > 0.0), wide, 4.0)
        for k in range(ROWS):
            diag[8 * k + f : 8 * k + f + 1, :] = wide[k : k + 1, :]
    lows, highs = [], []
    for k in range(ROWS):
        d = diag[8 * k : 8 * k + 8, :]
        inverse = 1.0 / (d - highs[-1] if k else d)
        lows.append(lows[-1] * inverse if k else inverse)
        highs.append(inverse)
        low[8 * k : 8 * k + 8] = lows[k]
        high[8 * k : 8 * k + 8] = highs[k]
    first_low = lows[-1]
    for k in range(ROWS - 2, -1, -1):
        first_low = lows[k] + highs[k] * first_low
    lane = iota((8, 128), 1)
    last = highs[-1]
    for q, part in ((2, first_low), (3, lows[-1]), (4, highs[-1])):
        last = jnp.where(lane >> 1 == 32 + q, roll(part, 2 * q, 1), last)
    block[...] = jnp.zeros((16, 128), F32)
    block[F : 2 * F] = jnp.where(lane < 64, first_low, roll(lows[-1], 64, 1))[0:F]
    block[2 * F : 3 * F] = last[0:F]


def residual(f, state, rhs, jac):
    own = state[f]
    beside = roll(own, 1, 0) + roll(own, -1, 0) + roll(own, 1, 1) + roll(own, -1, 1)
    total = rhs(f) + beside
    for g in range(F):
        total = total - jac(F * f + g) * state[g]
    return total


def sweep(old, new, scaled, rhs, jac):
    for f in range(F):
        new[f] = old[f] + scaled(f) * residual(f, old, rhs, jac)


def planes_of(own, beyond):
    return lambda p: jnp.concatenate([beyond[p, 0:8], own[p], beyond[p, 8:16]], axis=0)


def columns(shape, fine_dim, coarse_dim):
    fine = iota(shape, fine_dim)
    coarse = iota(shape, coarse_dim)
    here = (coarse <= 64) & (fine >> 2 == coarse)
    return (here | ((coarse == 65) & (fine >= EY - 4))).astype(F32)


def before_kernel(
    jac_own, rhs_own, scaled_own, high, block, far_x, near_x,
    state, jac, rhs, scaled, value, sent, other, sides, means, whole_block,
):
    odd = parity("gx")
    sides[0] = jnp.where(odd, near_x[...], far_x[...])
    sides[1] = jnp.where(odd, far_x[...], near_x[...])
    none = jnp.zeros((16, TY), F32)

    def corners(start, a):
        lanes = slice(128 * a, 128 * (a + 1))
        return jnp.concatenate([sides[s, start : start + 8, lanes] for s in range(2)], axis=0)

    far = [corners(136, a) for a in range(2)]
    near = [corners(144, a) for a in range(2)]
    for p in range(F * F):
        jac[p, :, 0:TY] = none
        jac[p, 4:8, 0:TY] = sides[0, 4 * p : 4 * p + 4]
        jac[p, 8:12, 0:TY] = sides[1, 4 * p : 4 * p + 4]
        if p % (F + 1) == 0:
            f = p // (F + 1)
            jac[p, 3:4, 0:TY] = sides[0, 130 + f : 131 + f]
            jac[p, 12:13, 0:TY] = sides[1, 130 + f : 131 + f]
        jac[p, :, TY:EY] = unpack(near[p // 16], far[p // 16], p)
    for f in range(F):
        rhs[f, :, 0:TY] = none
        rhs[f, 3:8, 0:TY] = sides[0, 100 + 5 * f : 105 + 5 * f]
        rhs[f, 8:13, 0:TY] = sides[1, 100 + 5 * f : 105 + 5 * f]
        rhs[f, :, TY:EY] = unpack(near[1], far[1], F * F + f)
    code = scaled.at[F - 1]
    code[:, 0:TY] = none
    code[3:8, 0:TY] = sides[0, 125:130]
    code[8:13, 0:TY] = sides[1, 125:130]
    code[:, TY:EY] = unpack(near[1], far[1], F * F + F)
    scale(code[...], jac, scaled)

    jac_plane, rhs_plane = planes_of(jac_own, jac), planes_of(rhs_own, rhs)
    scaled_plane = planes_of(scaled_own, scaled)
    for f in range(F):
        state[f] = scaled_plane(f) * rhs_plane(f)
    sweep(state, other, scaled_plane, rhs_plane, jac_plane)
    sweep(other, state, scaled_plane, rhs_plane, jac_plane)
    means[...] = jnp.zeros((8 * ROWS, EY), F32)
    for f in range(F):
        left_over = residual(f, state, rhs_plane, jac_plane)[8 : 8 + TX]
        left_over = left_over + roll(left_over, -1, 0)
        left_over = left_over + roll(left_over, -2, 0)
        for k in range(ROWS):
            means[8 * k + f : 8 * k + f + 1, :] = left_over[4 * k : 4 * k + 1]
    mean = select_columns(means[...] * 0.0625, columns((EY, 128), 0, 1))
    values = []
    for k in range(ROWS):
        rows = slice(8 * k, 8 * k + 8)
        here = mean[rows] + values[-1] if k else mean[rows]
        values.append(here * high[rows, :])
        value[rows] = values[k]
    first, last = values[-1], values[-1]
    for k in range(ROWS - 2, -1, -1):
        first = values[k] + high[8 * k : 8 * k + 8, :] * first
    lane = iota((8, 128), 1)
    ends = jnp.where(lane >> 1 == 32, first, roll(last, 2, 1))[0:F]
    whole_block[...] = block[...]
    whole_block[0:F] = jnp.where(lane < 64, first, roll(last, 64, 1))[0:F]
    kept = whole_block[2 * F : 3 * F]
    pair = lane[0:F] >> 1
    whole_block[2 * F : 3 * F] = jnp.where((pair == 32) | (pair == 33), ends, kept)
    whole = whole_block[...]
    for k in range(sent.shape[0]):
        sent[k] = whole


def merge(one, two):
    a0, a1, b0, c, c1 = one
    d0, d1, e0, g, g1 = two
    w = 1.0 / (1.0 - c1 * e0)
    cw, gw = c * w, g * w
    return (
        a0 + cw * (d0 + e0 * a1),
        d1 + gw * (a1 + c1 * d0),
        b0 + c * cw * e0,
        cw * g,
        g1 + g * gw * c1,
    )


def between(one, two, below, above):
    a0, a1, b0, c, c1 = one
    d0, d1, e0, g, g1 = two
    outer = d0 + g * above
    last = (a1 + c * below + c1 * outer) / (1.0 - c1 * e0)
    return last, outer + e0 * last


def after_kernel(
    jac_own, rhs_own, scaled_own, low, high, jac_beyond, rhs_beyond, scaled_beyond, state_in, value, got,
    correction_out, level_residual_out,
    state, other, ends, spread, tree, correction, level_residual, sems,
):
    count = got.shape[0]
    me = lax.axis_index("gx")
    lane = iota((F, 128), 1)

    def segment(k):
        one, two, three = got[k, 0:F, :], got[k, F : 2 * F, :], got[k, 2 * F : 3 * F, :]
        main = [one, roll(one, 64, 1), two, roll(two, 64, 1), three]
        return [jnp.where(lane < 64, main[q], roll(three, -2 * q, 1)) for q in range(5)]

    level, starts, total = [segment(k) for k in range(count)], [], 0
    while len(level) > 2:
        level = [merge(level[2 * k], level[2 * k + 1]) for k in range(len(level) // 2)]
        starts.append(total)
        for parts in level:
            for q in range(5):
                tree[total, q, 0:F] = parts[q]
            total += 1
    below = above = jnp.zeros((F, 128), F32)
    for size in range(len(starts), -1, -1):
        pair = me >> (size + 1)
        if size:
            at = starts[size - 1] + 2 * pair
            one = [tree[at, q, 0:F] for q in range(5)]
            two = [tree[at + 1, q, 0:F] for q in range(5)]
        else:
            one, two = segment(2 * pair), segment(2 * pair + 1)
        last, first = between(one, two, below, above)
        second = (me >> size) & 1 == 1
        below, above = jnp.where(second, last, below), jnp.where(second, above, first)

    used = lane <= 65
    ends[...] = jnp.zeros((64, 128), F32)
    ends[0:F] = jnp.where(used, below, 0.0)
    ends[8 * (ROWS + 1) : 8 * (ROWS + 1) + F] = jnp.where(used, above, 0.0)
    here = above
    for k in range(ROWS - 1, -1, -1):
        rows = slice(8 * k, 8 * k + F)
        here = value[rows] + low[rows] * below + high[rows] * here
        ends[8 * (k + 1) : 8 * (k + 1) + F] = jnp.where(used, here, 0.0)
    spread[...] = select_columns(ends[...], columns((128, EY), 1, 0))

    jac_plane, rhs_plane = planes_of(jac_own, jac_beyond), planes_of(rhs_own, rhs_beyond)
    scaled_plane = planes_of(scaled_own, scaled_beyond)
    upper = iota((8, EY), 0) < 4

    def repeated(row):
        return jnp.broadcast_to(spread[row : row + 1, :], (8, EY))

    for f in range(F):
        tiles = []
        for v in range(EX // 8):
            one = repeated(8 * (2 * v - 1) + f) if v else 0.0
            two = repeated(8 * (2 * v) + f) if v < EX // 8 - 1 else 0.0
            tiles.append(jnp.where(upper, one, two))
        added = jnp.where(scaled_plane(f) != 0.0, jnp.concatenate(tiles, axis=0), 0.0)
        state[f] = state_in[f] + added
    sweep(state, other, scaled_plane, rhs_plane, jac_plane)
    sweep(other, state, scaled_plane, rhs_plane, jac_plane)
    copies = []
    for f in range(F):
        correction[f] = state[f, 8 : 8 + TX, 0:TY]
        copies.append(
            pltpu.make_async_copy(correction.at[f], correction_out.at[f], sems.at[0, f])
        )
        copies[-1].start()
    for f in range(F):
        level_residual[f] = residual(f, state, rhs_plane, jac_plane)[8 : 8 + TX, 0:TY]
        copies.append(
            pltpu.make_async_copy(level_residual.at[f], level_residual_out.at[f], sems.at[1, f])
        )
        copies[-1].start()
    for copy in copies:
        copy.wait()


def shape_of(*dims):
    return jax.ShapeDtypeStruct(dims, F32)


def call(kernel, outs, scratch, *args, space=pltpu.VMEM, out_space=pltpu.VMEM):
    return pl.pallas_call(
        kernel,
        out_shape=outs,
        in_specs=[pl.BlockSpec(memory_space=space)] * len(args),
        out_specs=[pl.BlockSpec(memory_space=out_space)] * len(outs),
        scratch_shapes=scratch,
        compiler_params=pltpu.CompilerParams(vmem_limit_bytes=32 * 1024 * 1024),
    )(*args)


def swap(value, axis, start):
    count = lax.axis_size(axis)
    firsts = range(start, count - 1, 2)
    return lax.ppermute(value, axis, [(i, i + 1) for i in firsts] + [(i + 1, i) for i in firsts])


def local(fine, owner, flags, jac, coef):
    strip = shape_of(2, TX, 128)
    rows = shape_of(136, TY)
    rhs, top, bottom, near, far = call(
        restrict_kernel,
        [shape_of(F, TX, TY), rows, rows, strip, strip],
        [
            pltpu.VMEM((F, 4, 2 * TX, 128), F32),
            pltpu.VMEM((4, 2 * TX, 128), jnp.int32),
            pltpu.VMEM((TX, TY), jnp.int32),
            pltpu.VMEM((F, F, TX, TY), F32),
            pltpu.VMEM((F, ROWS, TY // 4), F32),
            pltpu.SemaphoreType.DMA((F + 2, 4)),
        ],
        *[pltpu.with_memory_space_constraint(x, pltpu.HBM) for x in (fine, owner, flags, jac, coef)],
        space=pltpu.HBM,
    )
    far_y = swap(far, "gy", 1)
    near_y = swap(near, "gy", 0)

    def with_corners(own, rows):
        corners = [jnp.concatenate([side[0, rows], side[1, rows]], axis=1) for side in (far_y, near_y)]
        return jnp.concatenate([own, *corners], axis=0)

    top = with_corners(top, slice(0, 8))
    bottom = with_corners(bottom, slice(TX - 8, TX))
    odd = parity("gx")
    far_x = swap(jnp.where(odd, bottom, top), "gx", 1)
    near_x = swap(jnp.where(odd, top, bottom), "gx", 0)
    count = lax.axis_size("gx")
    lines = shape_of(8 * ROWS, 128)
    own = shape_of(F, TX, EY)
    jac_own, rhs_own, scaled_own, low, high, block = call(
        own_kernel,
        [shape_of(F * F, TX, EY), own, own, lines, lines, shape_of(16, 128)],
        [pltpu.VMEM((8 * ROWS, 128), F32)],
        jac, rhs, flags, far_y, near_y, coef,
    )
    tile = pltpu.VMEM((F, EX, EY), F32)
    beyond = shape_of(F, 16, EY)
    state, jac_beyond, rhs_beyond, scaled_beyond, value, sent = call(
        before_kernel,
        [shape_of(F, EX, EY), shape_of(F * F, 16, EY), beyond, beyond, lines, shape_of(count, 16, 128)],
        [tile, pltpu.VMEM((2, 152, TY), F32), pltpu.VMEM((8 * ROWS, EY), F32), pltpu.VMEM((16, 128), F32)],
        jac_own, rhs_own, scaled_own, high, block, far_x, near_x,
    )
    got = lax.all_to_all(sent, "gx", 0, 0, tiled=True)
    return tuple(
        call(
            after_kernel,
            [shape_of(F, TX, TY), shape_of(F, TX, TY)],
            [
                tile,
                tile,
                pltpu.VMEM((64, 128), F32),
                pltpu.VMEM((64, EY), F32),
                pltpu.VMEM((count, 5, 8, 128), F32),
                pltpu.VMEM((F, TX, TY), F32),
                pltpu.VMEM((F, TX, TY), F32),
                pltpu.SemaphoreType.DMA((2, F)),
            ],
            jac_own, rhs_own, scaled_own, low, high, jac_beyond, rhs_beyond, scaled_beyond, state, value, got,
            out_space=pl.ANY,
        )
    )


def solution(mesh):
    in_specs = (
        P(None, "gx", "gy"),
        P("gx", "gy"),
        P("gx", "gy"),
        P(None, None, "gx", "gy"),
        P(None, "gx", "gy"),
    )
    out_specs = (P(None, "gx", "gy"), P(None, "gx", "gy"))
    return jax.shard_map(local, mesh=mesh, in_specs=in_specs, out_specs=out_specs, check_vma=False)
```

```python
import jax
import jax.numpy as jnp
from jax import lax
from jax.experimental import pallas as pl
from jax.experimental.pallas import tpu as pltpu
from jax.sharding import PartitionSpec as P

F = 5
TX = 24
TY = 256
EX = 40
EY = 384
ROWS = 6
PLANES = 31
F32 = jnp.float32


def iota(shape, dim):
    return lax.broadcasted_iota(jnp.int32, shape, dim)


def parts_of(x):
    head = x.astype(jnp.bfloat16)
    rest = x - head.astype(F32)
    middle = rest.astype(jnp.bfloat16)
    return head, middle, (rest - middle.astype(F32)).astype(jnp.bfloat16)


def select_columns(x, chosen):
    rows = x.shape[0]
    whole = jnp.concatenate(parts_of(x), axis=0)
    out = jnp.dot(whole, chosen.astype(jnp.bfloat16), preferred_element_type=F32)
    return out[0:rows] + out[rows : 2 * rows] + out[2 * rows :]


def roll(x, shift, axis):
    shift = shift % x.shape[axis]
    return x if shift == 0 else pltpu.roll(x, shift, axis)


def parity(axis):
    return lax.rem(lax.axis_index(axis), 2) == 1


def restrict_kernel(
    fine_in, owner_in, flags_in, jac_in, coef_in, rhs, near, far,
    fine, owner, flags, jac, coef, sems,
):
    def tile_copy(source, target, sem, j):
        return pltpu.make_async_copy(source.at[:, 128 * j : 128 * (j + 1)], target.at[j], sem)

    owners = [tile_copy(owner_in, owner, sems.at[0, j], j) for j in range(4)]
    fines = [
        [tile_copy(fine_in.at[f], fine.at[f], sems.at[1 + f, j], j) for j in range(4)]
        for f in range(F)
    ]
    late = [
        pltpu.make_async_copy(flags_in, flags, sems.at[F + 1, 0]),
        pltpu.make_async_copy(coef_in, coef, sems.at[F + 1, 1]),
        pltpu.make_async_copy(jac_in, jac, sems.at[F + 1, 2]),
    ]
    for copy in owners + sum(fines, []) + late:
        copy.start()
    for copy in owners + sum(fines, []) + late:
        copy.wait()

    def halves(load):
        return [
            jnp.concatenate([load(j, pl.ds(start, TX, 2)) for j in range(4)], axis=1)
            for start in (0, 1)
        ]

    shape = (TX, 2 * TY)
    row = iota(shape, 0)
    col = iota(shape, 1) >> 1
    codes = [
        ((o >> 8) - row + 1) * 3 + (o & (TY - 1)) - col + 1
        for o in halves(lambda j, rows: owner[j, rows, :])
    ]
    masks = [[code == k for code in codes] for k in range(9)]
    gathered = []
    for f in range(F):
        values = halves(lambda j, rows: fine[f, j, rows, :])
        total = None
        for dy in (-1, 0, 1):
            part = None
            for dx in (-1, 0, 1):
                mask = masks[(dx + 1) * 3 + dy + 1]
                moved = jnp.where(mask[0], values[0], 0.0) + jnp.where(mask[1], values[1], 0.0)
                moved = roll(moved, dx, 0)
                part = moved if part is None else part + moved
            part = roll(part, 2 * dy, 1)
            total = part if total is None else total + part
        gathered.append(total)
    pairs = ((iota((2 * TY, TY), 0) >> 1) == iota((2 * TY, TY), 1)).astype(F32)
    gathered.append(jnp.zeros((8, 2 * TY), F32))
    summed = select_columns(jnp.concatenate(gathered, axis=0), pairs)
    planes = [summed[TX * f : TX * (f + 1)] for f in range(F)]
    for f in range(F):
        rhs[f] = planes[f]
    planes.append((flags[...] + 1).astype(F32))

    odd = parity("gy")
    slot = iota((TX, 128), 1) >> 3
    for a in range(2):
        first = jnp.zeros((TX, 128), F32)
        last = jnp.zeros((TX, 128), F32)
        for t in range(16):
            p = 16 * a + t
            if p >= PLANES:
                continue
            if p < F * F:
                head, tail = jac[p // F, p % F, :, 0:128], jac[p // F, p % F, :, TY - 128 : TY]
            else:
                head, tail = planes[p - F * F][:, 0:128], planes[p - F * F][:, TY - 128 : TY]
            first = jnp.where(slot == t, roll(head, 8 * t, 1), first)
            last = jnp.where(slot == t, roll(tail, 8 * t - 120, 1), last)
        near[a] = jnp.where(odd, first, last)
        far[a] = jnp.where(odd, last, first)
    lane = iota((ROWS, 128), 1)
    first, last = near[1, 0:ROWS, :], far[1, 0:ROWS, :]
    for f in range(F):
        wide = jnp.concatenate([coef[f], coef[f]], axis=1)
        head, tail = roll(wide, 120 + f, 1), roll(wide, 120 + f - 63, 1)
        first = jnp.where(lane == 120 + f, jnp.where(odd, head, tail), first)
        last = jnp.where(lane == 120 + f, jnp.where(odd, tail, head), last)
    near[1, 0:ROWS, :] = first
    far[1, 0:ROWS, :] = last


JAC_AT, RHS_AT, CODE_AT, DIAG_AT, CORNER_AT, ROWS_SENT = 0, 50, 65, 68, 74, 80


def rows_kernel(jac, rhs, flags, near, far):
    def write(out, first):
        start = 0 if first else TX - 2
        wide = 0 if first else TX - 3
        third = 2 if first else TX - 3
        for p in range(F * F):
            out[2 * p : 2 * p + 2] = jac[p // F, p % F, start : start + 2, :]
        for f in range(F):
            at = RHS_AT + 3 * f
            out[at : at + 3] = rhs[f, wide : wide + 3, :]
            out[DIAG_AT + f : DIAG_AT + f + 1] = jac[f, f, third : third + 1, :]
        out[CODE_AT : CODE_AT + 3] = (flags[wide : wide + 3, :] + 1).astype(F32)
        out[73:ROWS_SENT] = jnp.zeros((ROWS_SENT - 73, TY), F32)

    odd = parity("gx")

    @pl.when(odd)
    def _():
        write(near, True)
        write(far, False)

    @pl.when(jnp.logical_not(odd))
    def _():
        write(near, False)
        write(far, True)


def corners_kernel(near_rows, far_rows, far_y, near_y, near, far):
    odd = parity("gx")
    near[...] = near_rows[...]
    far[...] = far_rows[...]
    for side, strip in enumerate((far_y, near_y)):
        at = CORNER_AT + 3 * side
        for a in range(2):
            lanes = slice(128 * a, 128 * (a + 1))
            first, last = strip[a, 0:3, :], strip[a, TX - 3 : TX, :]
            near[at : at + 3, lanes] = jnp.where(odd, first, last)
            far[at : at + 3, lanes] = jnp.where(odd, last, first)


def unpack(near, far, p):
    odd = parity("gy")
    right = jnp.where(odd, far, near)
    left = jnp.where(odd, near, far)
    lane = iota(near.shape, 1)
    return jnp.where(
        lane < 8,
        roll(right, -8 * (p % 16), 1),
        jnp.where(lane >= 120, roll(left, 120 - 8 * (p % 16), 1), 0.0),
    )


def scale(code, jac, scaled):
    plain = (code == 1.0) | (code == 3.0)
    interior = code == 1.0
    for f in range(F):
        kept = interior if f in (1, 2) else plain
        scaled[f] = jnp.where(kept, 0.8 / jac[F * f + f], 0.0)


def own_kernel(
    jac_in, rhs_in, flags, far_y, near_y, coef, jac, rhs, scaled, low, high, block, diag
):
    near, far = [near_y[0], near_y[1]], [far_y[0], far_y[1]]
    for p in range(F * F):
        jac[p, :, 0:TY] = jac_in[p // F, p % F]
        jac[p, :, TY:EY] = unpack(near[p // 16], far[p // 16], p)
    for f in range(F):
        rhs[f, :, 0:TY] = rhs_in[f]
        rhs[f, :, TY:EY] = unpack(near[1], far[1], F * F + f)
    aside = unpack(near[1], far[1], F * F + F)
    code = jnp.concatenate([(flags[...] + 1).astype(F32), aside], axis=1)
    scale(code, jac, scaled)

    lane = iota((ROWS, 128), 1)
    odd = parity("gy")
    right = jnp.where(odd, far[1], near[1])[0:ROWS]
    left = jnp.where(odd, near[1], far[1])[0:ROWS]
    diag[...] = jnp.full((8 * ROWS, 128), 4.0, F32)
    for f in range(F):
        wide = jnp.concatenate([coef[f], coef[f]], axis=1)
        wide = jnp.where(lane == 64, roll(right, 64 - 120 - f, 1), wide)
        wide = jnp.where(lane == 65, roll(left, 65 - 120 - f, 1), wide)
        wide = jnp.where((lane <= 65) & (wide > 0.0), wide, 4.0)
        for k in range(ROWS):
            diag[8 * k + f : 8 * k + f + 1, :] = wide[k : k + 1, :]
    lows, highs = [], []
    for k in range(ROWS):
        d = diag[8 * k : 8 * k + 8, :]
        inverse = 1.0 / (d - highs[-1] if k else d)
        lows.append(lows[-1] * inverse if k else inverse)
        highs.append(inverse)
        low[8 * k : 8 * k + 8] = lows[k]
        high[8 * k : 8 * k + 8] = highs[k]
    first_low = lows[-1]
    for k in range(ROWS - 2, -1, -1):
        first_low = lows[k] + highs[k] * first_low
    lane = iota((8, 128), 1)
    last = highs[-1]
    for q, part in ((2, first_low), (3, lows[-1]), (4, highs[-1])):
        last = jnp.where(lane >> 1 == 32 + q, roll(part, 2 * q, 1), last)
    block[...] = jnp.zeros((16, 128), F32)
    block[F : 2 * F] = jnp.where(lane < 64, first_low, roll(lows[-1], 64, 1))[0:F]
    block[2 * F : 3 * F] = last[0:F]


def residual(f, state, rhs, jac):
    own = state[f]
    beside = roll(own, 1, 0) + roll(own, -1, 0) + roll(own, 1, 1) + roll(own, -1, 1)
    total = rhs(f) + beside
    for g in range(F):
        total = total - jac(F * f + g) * state[g]
    return total


def sweep(old, new, scaled, rhs, jac):
    for f in range(F):
        new[f] = old[f] + scaled(f) * residual(f, old, rhs, jac)


def planes_of(own, beyond):
    return lambda p: jnp.concatenate([beyond[p, 0:8], own[p], beyond[p, 8:16]], axis=0)


def columns(shape, fine_dim, coarse_dim):
    fine = iota(shape, fine_dim)
    coarse = iota(shape, coarse_dim)
    here = (coarse <= 64) & (fine >> 2 == coarse)
    return (here | ((coarse == 65) & (fine >= EY - 4))).astype(F32)


def before_kernel(
    jac_own, rhs_own, scaled_own, high, block, far_x, near_x,
    state, jac, rhs, scaled, value, sent, near_state, far_state, other, sides, beside, means, whole_block,
):
    odd = parity("gx")
    sides[0] = jnp.where(odd, near_x[...], far_x[...])
    sides[1] = jnp.where(odd, far_x[...], near_x[...])
    none = jnp.zeros((16, TY), F32)

    def put(out, at, rows):
        out[8 - rows : 8, 0:TY] = sides[0, at : at + rows]
        out[8 : 8 + rows, 0:TY] = sides[1, at : at + rows]

    for side in range(2):
        at = CORNER_AT + 3 * side
        for a in range(2):
            lanes = slice(128 * a, 128 * (a + 1))
            beside[side, a] = jnp.zeros((16, 128), F32)
            beside[side, a, 5:8] = sides[0, at : at + 3, lanes]
            beside[side, a, 8:11] = sides[1, at : at + 3, lanes]
    far, near = [[beside[side, a] for a in range(2)] for side in range(2)]
    for p in range(F * F):
        jac[p, :, 0:TY] = none
        put(jac.at[p], 2 * p, 2)
        if p % (F + 1) == 0:
            f = p // (F + 1)
            jac[p, 5:6, 0:TY] = sides[0, DIAG_AT + f : DIAG_AT + f + 1]
            jac[p, 10:11, 0:TY] = sides[1, DIAG_AT + f : DIAG_AT + f + 1]
        jac[p, :, TY:EY] = unpack(near[p // 16], far[p // 16], p)
    for f in range(F):
        rhs[f, :, 0:TY] = none
        put(rhs.at[f], RHS_AT + 3 * f, 3)
        rhs[f, :, TY:EY] = unpack(near[1], far[1], F * F + f)
    code = scaled.at[F - 1]
    code[:, 0:TY] = none
    put(code, CODE_AT, 3)
    code[:, TY:EY] = unpack(near[1], far[1], F * F + F)
    scale(code[...], jac, scaled)

    jac_plane, rhs_plane = planes_of(jac_own, jac), planes_of(rhs_own, rhs)
    scaled_plane = planes_of(scaled_own, scaled)
    for f in range(F):
        state[f] = scaled_plane(f) * rhs_plane(f)
    sweep(state, other, scaled_plane, rhs_plane, jac_plane)
    sweep(other, state, scaled_plane, rhs_plane, jac_plane)
    near_state[15:16] = jnp.zeros((1, EY), F32)
    far_state[15:16] = jnp.zeros((1, EY), F32)
    for f in range(F):
        first, last = state[f, 8:11], state[f, 5 + TX : 8 + TX]
        near_state[3 * f : 3 * f + 3] = jnp.where(odd, first, last)
        far_state[3 * f : 3 * f + 3] = jnp.where(odd, last, first)
    means[...] = jnp.zeros((8 * ROWS, EY), F32)
    for f in range(F):
        left_over = residual(f, state, rhs_plane, jac_plane)[8 : 8 + TX]
        left_over = left_over + roll(left_over, -1, 0)
        left_over = left_over + roll(left_over, -2, 0)
        for k in range(ROWS):
            means[8 * k + f : 8 * k + f + 1, :] = left_over[4 * k : 4 * k + 1]
    mean = select_columns(means[...] * 0.0625, columns((EY, 128), 0, 1))
    values = []
    for k in range(ROWS):
        rows = slice(8 * k, 8 * k + 8)
        here = mean[rows] + values[-1] if k else mean[rows]
        values.append(here * high[rows, :])
        value[rows] = values[k]
    first, last = values[-1], values[-1]
    for k in range(ROWS - 2, -1, -1):
        first = values[k] + high[8 * k : 8 * k + 8, :] * first
    lane = iota((8, 128), 1)
    ends = jnp.where(lane >> 1 == 32, first, roll(last, 2, 1))[0:F]
    whole_block[...] = block[...]
    whole_block[0:F] = jnp.where(lane < 64, first, roll(last, 64, 1))[0:F]
    kept = whole_block[2 * F : 3 * F]
    pair = lane[0:F] >> 1
    whole_block[2 * F : 3 * F] = jnp.where((pair == 32) | (pair == 33), ends, kept)
    whole = whole_block[...]
    for k in range(sent.shape[0]):
        sent[k] = whole


def merge(one, two):
    a0, a1, b0, c, c1 = one
    d0, d1, e0, g, g1 = two
    w = 1.0 / (1.0 - c1 * e0)
    cw, gw = c * w, g * w
    return (
        a0 + cw * (d0 + e0 * a1),
        d1 + gw * (a1 + c1 * d0),
        b0 + c * cw * e0,
        cw * g,
        g1 + g * gw * c1,
    )


def between(one, two, below, above):
    a0, a1, b0, c, c1 = one
    d0, d1, e0, g, g1 = two
    outer = d0 + g * above
    last = (a1 + c * below + c1 * outer) / (1.0 - c1 * e0)
    return last, outer + e0 * last


def after_kernel(
    jac_own, rhs_own, scaled_own, low, high, jac_beyond, rhs_beyond, scaled_beyond, state_in, value, far_state, near_state, got,
    correction_out, level_residual_out,
    state, other, ends, spread, tree, correction, level_residual, sems,
):
    count = got.shape[0]
    me = lax.axis_index("gx")
    lane = iota((F, 128), 1)

    def segment(k):
        one, two, three = got[k, 0:F, :], got[k, F : 2 * F, :], got[k, 2 * F : 3 * F, :]
        main = [one, roll(one, 64, 1), two, roll(two, 64, 1), three]
        return [jnp.where(lane < 64, main[q], roll(three, -2 * q, 1)) for q in range(5)]

    level, starts, total = [segment(k) for k in range(count)], [], 0
    while len(level) > 2:
        level = [merge(level[2 * k], level[2 * k + 1]) for k in range(len(level) // 2)]
        starts.append(total)
        for parts in level:
            for q in range(5):
                tree[total, q, 0:F] = parts[q]
            total += 1
    below = above = jnp.zeros((F, 128), F32)
    for size in range(len(starts), -1, -1):
        pair = me >> (size + 1)
        if size:
            at = starts[size - 1] + 2 * pair
            one = [tree[at, q, 0:F] for q in range(5)]
            two = [tree[at + 1, q, 0:F] for q in range(5)]
        else:
            one, two = segment(2 * pair), segment(2 * pair + 1)
        last, first = between(one, two, below, above)
        second = (me >> size) & 1 == 1
        below, above = jnp.where(second, last, below), jnp.where(second, above, first)

    used = lane <= 65
    ends[...] = jnp.zeros((64, 128), F32)
    ends[0:F] = jnp.where(used, below, 0.0)
    ends[8 * (ROWS + 1) : 8 * (ROWS + 1) + F] = jnp.where(used, above, 0.0)
    here = above
    for k in range(ROWS - 1, -1, -1):
        rows = slice(8 * k, 8 * k + F)
        here = value[rows] + low[rows] * below + high[rows] * here
        ends[8 * (k + 1) : 8 * (k + 1) + F] = jnp.where(used, here, 0.0)
    spread[...] = select_columns(ends[...], columns((128, EY), 1, 0))

    jac_plane, rhs_plane = planes_of(jac_own, jac_beyond), planes_of(rhs_own, rhs_beyond)
    scaled_plane = planes_of(scaled_own, scaled_beyond)
    upper = iota((8, EY), 0) < 4
    odd = parity("gx")

    def repeated(row):
        return jnp.broadcast_to(spread[row : row + 1, :], (8, EY))

    for f in range(F):
        tiles = []
        for v in range(EX // 8):
            one = repeated(8 * (2 * v - 1) + f) if v else 0.0
            two = repeated(8 * (2 * v) + f) if v < EX // 8 - 1 else 0.0
            tiles.append(jnp.where(upper, one, two))
        added = jnp.where(scaled_plane(f) != 0.0, jnp.concatenate(tiles, axis=0), 0.0)
        other[f] = state_in[f]
        far, near = far_state[3 * f : 3 * f + 3], near_state[3 * f : 3 * f + 3]
        other[f, 5:8] = jnp.where(odd, near, far)
        other[f, 8 + TX : 11 + TX] = jnp.where(odd, far, near)
        state[f] = other[f] + added
    sweep(state, other, scaled_plane, rhs_plane, jac_plane)
    sweep(other, state, scaled_plane, rhs_plane, jac_plane)
    copies = []
    for f in range(F):
        correction[f] = state[f, 8 : 8 + TX, 0:TY]
        copies.append(
            pltpu.make_async_copy(correction.at[f], correction_out.at[f], sems.at[0, f])
        )
        copies[-1].start()
    for f in range(F):
        level_residual[f] = residual(f, state, rhs_plane, jac_plane)[8 : 8 + TX, 0:TY]
        copies.append(
            pltpu.make_async_copy(level_residual.at[f], level_residual_out.at[f], sems.at[1, f])
        )
        copies[-1].start()
    for copy in copies:
        copy.wait()


def shape_of(*dims):
    return jax.ShapeDtypeStruct(dims, F32)


def call(kernel, outs, scratch, *args, space=pltpu.VMEM, out_space=pltpu.VMEM):
    return pl.pallas_call(
        kernel,
        out_shape=outs,
        in_specs=[pl.BlockSpec(memory_space=space)] * len(args),
        out_specs=[pl.BlockSpec(memory_space=out_space)] * len(outs),
        scratch_shapes=scratch,
        compiler_params=pltpu.CompilerParams(vmem_limit_bytes=32 * 1024 * 1024),
    )(*args)


def swap(value, axis, start):
    count = lax.axis_size(axis)
    firsts = range(start, count - 1, 2)
    return lax.ppermute(value, axis, [(i, i + 1) for i in firsts] + [(i + 1, i) for i in firsts])


def local(fine, owner, flags, jac, coef):
    strip = shape_of(2, TX, 128)
    rhs, near, far = call(
        restrict_kernel,
        [shape_of(F, TX, TY), strip, strip],
        [
            pltpu.VMEM((F, 4, 2 * TX, 128), F32),
            pltpu.VMEM((4, 2 * TX, 128), jnp.int32),
            pltpu.VMEM((TX, TY), jnp.int32),
            pltpu.VMEM((F, F, TX, TY), F32),
            pltpu.VMEM((F, ROWS, TY // 4), F32),
            pltpu.SemaphoreType.DMA((F + 2, 4)),
        ],
        *[pltpu.with_memory_space_constraint(x, pltpu.HBM) for x in (fine, owner, flags, jac, coef)],
        space=pltpu.HBM,
    )
    near_rows, far_rows = call(
        rows_kernel, [shape_of(ROWS_SENT, TY), shape_of(ROWS_SENT, TY)], [], jac, rhs, flags
    )
    far_y = swap(far, "gy", 1)
    near_y = swap(near, "gy", 0)
    rows = shape_of(ROWS_SENT, TY)
    near_rows, far_rows = call(corners_kernel, [rows, rows], [], near_rows, far_rows, far_y, near_y)
    far_x = swap(far_rows, "gx", 1)
    near_x = swap(near_rows, "gx", 0)
    count = lax.axis_size("gx")
    lines = shape_of(8 * ROWS, 128)
    own = shape_of(F, TX, EY)
    jac_own, rhs_own, scaled_own, low, high, block = call(
        own_kernel,
        [shape_of(F * F, TX, EY), own, own, lines, lines, shape_of(16, 128)],
        [pltpu.VMEM((8 * ROWS, 128), F32)],
        jac, rhs, flags, far_y, near_y, coef,
    )
    tile = pltpu.VMEM((F, EX, EY), F32)
    beyond = shape_of(F, 16, EY)
    ends = shape_of(16, EY)
    state, jac_beyond, rhs_beyond, scaled_beyond, value, sent, near_state, far_state = call(
        before_kernel,
        [shape_of(F, EX, EY), shape_of(F * F, 16, EY), beyond, beyond, lines, shape_of(count, 16, 128), ends, ends],
        [
            tile,
            pltpu.VMEM((2, ROWS_SENT, TY), F32),
            pltpu.VMEM((2, 2, 16, 128), F32),
            pltpu.VMEM((8 * ROWS, EY), F32),
            pltpu.VMEM((16, 128), F32),
        ],
        jac_own, rhs_own, scaled_own, high, block, far_x, near_x,
    )
    got = lax.all_to_all(sent, "gx", 0, 0, tiled=True)
    far_state = swap(far_state, "gx", 1)
    near_state = swap(near_state, "gx", 0)
    return tuple(
        call(
            after_kernel,
            [shape_of(F, TX, TY), shape_of(F, TX, TY)],
            [
                tile,
                tile,
                pltpu.VMEM((64, 128), F32),
                pltpu.VMEM((64, EY), F32),
                pltpu.VMEM((count, 5, 8, 128), F32),
                pltpu.VMEM((F, TX, TY), F32),
                pltpu.VMEM((F, TX, TY), F32),
                pltpu.SemaphoreType.DMA((2, F)),
            ],
            jac_own, rhs_own, scaled_own, low, high, jac_beyond, rhs_beyond, scaled_beyond, state, value, far_state, near_state, got,
            out_space=pl.ANY,
        )
    )


def solution(mesh):
    in_specs = (
        P(None, "gx", "gy"),
        P("gx", "gy"),
        P("gx", "gy"),
        P(None, None, "gx", "gy"),
        P(None, "gx", "gy"),
    )
    out_specs = (P(None, "gx", "gy"), P(None, "gx", "gy"))
    return jax.shard_map(local, mesh=mesh, in_specs=in_specs, out_specs=out_specs, check_vma=False)
```

```python
import jax
import jax.numpy as jnp
from jax import lax
from jax.experimental import pallas as pl
from jax.experimental.pallas import tpu as pltpu
from jax.sharding import PartitionSpec as P

F = 5
TX = 24
TY = 256
EX = 40
EY = 384
ROWS = 6
PLANES = 31
F32 = jnp.float32


def iota(shape, dim):
    return lax.broadcasted_iota(jnp.int32, shape, dim)


def parts_of(x):
    head = x.astype(jnp.bfloat16)
    rest = x - head.astype(F32)
    middle = rest.astype(jnp.bfloat16)
    return head, middle, (rest - middle.astype(F32)).astype(jnp.bfloat16)


def select_columns(x, chosen):
    rows = x.shape[0]
    whole = jnp.concatenate(parts_of(x), axis=0)
    out = jnp.dot(whole, chosen.astype(jnp.bfloat16), preferred_element_type=F32)
    return out[0:rows] + out[rows : 2 * rows] + out[2 * rows :]


def roll(x, shift, axis):
    shift = shift % x.shape[axis]
    return x if shift == 0 else pltpu.roll(x, shift, axis)


def parity(axis):
    return lax.rem(lax.axis_index(axis), 2) == 1


def restrict_kernel(
    fine_in, owner_in, flags_in, jac_in, coef_in, rhs, near, far,
    fine, owner, flags, jac, coef, sems,
):
    def tile_copy(source, target, sem, j):
        return pltpu.make_async_copy(source.at[:, 128 * j : 128 * (j + 1)], target.at[j], sem)

    owners = [tile_copy(owner_in, owner, sems.at[0, j], j) for j in range(4)]
    fines = [
        [tile_copy(fine_in.at[f], fine.at[f], sems.at[1 + f, j], j) for j in range(4)]
        for f in range(F)
    ]
    late = [
        pltpu.make_async_copy(flags_in, flags, sems.at[F + 1, 0]),
        pltpu.make_async_copy(coef_in, coef, sems.at[F + 1, 1]),
        pltpu.make_async_copy(jac_in, jac, sems.at[F + 1, 2]),
    ]
    for copy in owners + sum(fines, []) + late:
        copy.start()
    for copy in owners:
        copy.wait()

    def halves(load):
        return [
            jnp.concatenate([load(j, pl.ds(start, TX, 2)) for j in range(4)], axis=1)
            for start in (0, 1)
        ]

    shape = (TX, 2 * TY)
    row = iota(shape, 0)
    col = iota(shape, 1) >> 1
    codes = [
        ((o >> 8) - row + 1) * 3 + (o & (TY - 1)) - col + 1
        for o in halves(lambda j, rows: owner[j, rows, :])
    ]
    masks = [[code == k for code in codes] for k in range(9)]
    gathered = []
    for f in range(F):
        for copy in fines[f]:
            copy.wait()
        values = halves(lambda j, rows: fine[f, j, rows, :])
        total = None
        for dy in (-1, 0, 1):
            part = None
            for dx in (-1, 0, 1):
                mask = masks[(dx + 1) * 3 + dy + 1]
                moved = jnp.where(mask[0], values[0], 0.0) + jnp.where(mask[1], values[1], 0.0)
                moved = roll(moved, dx, 0)
                part = moved if part is None else part + moved
            part = roll(part, 2 * dy, 1)
            total = part if total is None else total + part
        gathered.append(total)
    pairs = ((iota((2 * TY, TY), 0) >> 1) == iota((2 * TY, TY), 1)).astype(F32)
    gathered.append(jnp.zeros((8, 2 * TY), F32))
    summed = select_columns(jnp.concatenate(gathered, axis=0), pairs)
    for copy in late:
        copy.wait()
    planes = [summed[TX * f : TX * (f + 1)] for f in range(F)]
    for f in range(F):
        rhs[f] = planes[f]
    planes.append((flags[...] + 1).astype(F32))

    odd = parity("gy")
    slot = iota((TX, 128), 1) >> 3
    for a in range(2):
        first = jnp.zeros((TX, 128), F32)
        last = jnp.zeros((TX, 128), F32)
        for t in range(16):
            p = 16 * a + t
            if p >= PLANES:
                continue
            if p < F * F:
                head, tail = jac[p // F, p % F, :, 0:128], jac[p // F, p % F, :, TY - 128 : TY]
            else:
                head, tail = planes[p - F * F][:, 0:128], planes[p - F * F][:, TY - 128 : TY]
            first = jnp.where(slot == t, roll(head, 8 * t, 1), first)
            last = jnp.where(slot == t, roll(tail, 8 * t - 120, 1), last)
        near[a] = jnp.where(odd, first, last)
        far[a] = jnp.where(odd, last, first)
    lane = iota((ROWS, 128), 1)
    first, last = near[1, 0:ROWS, :], far[1, 0:ROWS, :]
    for f in range(F):
        wide = jnp.concatenate([coef[f], coef[f]], axis=1)
        head, tail = roll(wide, 120 + f, 1), roll(wide, 120 + f - 63, 1)
        first = jnp.where(lane == 120 + f, jnp.where(odd, head, tail), first)
        last = jnp.where(lane == 120 + f, jnp.where(odd, tail, head), last)
    near[1, 0:ROWS, :] = first
    far[1, 0:ROWS, :] = last


JAC_AT, RHS_AT, CODE_AT, DIAG_AT, CORNER_AT, ROWS_SENT = 0, 50, 65, 68, 74, 80


def rows_kernel(jac, rhs, flags, near, far):
    def write(out, first):
        start = 0 if first else TX - 2
        wide = 0 if first else TX - 3
        third = 2 if first else TX - 3
        for p in range(F * F):
            out[2 * p : 2 * p + 2] = jac[p // F, p % F, start : start + 2, :]
        for f in range(F):
            at = RHS_AT + 3 * f
            out[at : at + 3] = rhs[f, wide : wide + 3, :]
            out[DIAG_AT + f : DIAG_AT + f + 1] = jac[f, f, third : third + 1, :]
        out[CODE_AT : CODE_AT + 3] = (flags[wide : wide + 3, :] + 1).astype(F32)
        out[73:ROWS_SENT] = jnp.zeros((ROWS_SENT - 73, TY), F32)

    odd = parity("gx")

    @pl.when(odd)
    def _():
        write(near, True)
        write(far, False)

    @pl.when(jnp.logical_not(odd))
    def _():
        write(near, False)
        write(far, True)


def corners_kernel(near_rows, far_rows, coef, far_y, near_y, near, far, low, high, turn, diag):
    odd = parity("gx")
    near[0:ROWS_SENT] = near_rows[...]
    far[0:ROWS_SENT] = far_rows[...]
    far[ROWS_SENT : ROWS_SENT + 8] = jnp.zeros((8, TY), F32)
    for side, strip in enumerate((far_y, near_y)):
        at = CORNER_AT + 3 * side
        for a in range(2):
            lanes = slice(128 * a, 128 * (a + 1))
            first, last = strip[a, 0:3, :], strip[a, TX - 3 : TX, :]
            near[at : at + 3, lanes] = jnp.where(odd, first, last)
            far[at : at + 3, lanes] = jnp.where(odd, last, first)

    lane = iota((ROWS, 128), 1)
    odd_y = parity("gy")
    right = jnp.where(odd_y, far_y[1, 0:ROWS, :], near_y[1, 0:ROWS, :])
    left = jnp.where(odd_y, near_y[1, 0:ROWS, :], far_y[1, 0:ROWS, :])
    diag[...] = jnp.full((8 * ROWS, 128), 4.0, F32)
    for f in range(F):
        wide = jnp.concatenate([coef[f], coef[f]], axis=1)
        wide = jnp.where(lane == 64, roll(right, 64 - 120 - f, 1), wide)
        wide = jnp.where(lane == 65, roll(left, 65 - 120 - f, 1), wide)
        wide = jnp.where((lane <= 65) & (wide > 0.0), wide, 4.0)
        for k in range(ROWS):
            diag[8 * k + f : 8 * k + f + 1, :] = wide[k : k + 1, :]
    lows, highs = [], []
    for k in range(ROWS):
        d = diag[8 * k : 8 * k + 8, :]
        inverse = 1.0 / (d - highs[-1] if k else d)
        lows.append(lows[-1] * inverse if k else inverse)
        highs.append(inverse)
        low[8 * k : 8 * k + 8] = lows[k]
        high[8 * k : 8 * k + 8] = highs[k]
    first_low = lows[-1]
    for k in range(ROWS - 2, -1, -1):
        first_low = lows[k] + highs[k] * first_low
    turn[...] = first_low
    lane = iota((8, 128), 1)
    ends = highs[-1]
    for q, part in enumerate((first_low, lows[-1], highs[-1])):
        ends = jnp.where(lane >> 1 == 33 + q, roll(part, 2 * (q + 1), 1), ends)
    near[ROWS_SENT : ROWS_SENT + 8, 0:128] = jnp.where(lane < 64, first_low, roll(lows[-1], 64, 1))
    near[ROWS_SENT : ROWS_SENT + 8, 128:TY] = ends


def unpack(near, far, p):
    odd = parity("gy")
    right = jnp.where(odd, far, near)
    left = jnp.where(odd, near, far)
    lane = iota(near.shape, 1)
    return jnp.where(
        lane < 8,
        roll(right, -8 * (p % 16), 1),
        jnp.where(lane >= 120, roll(left, 120 - 8 * (p % 16), 1), 0.0),
    )


def scale(code, jac, scaled):
    plain = (code == 1.0) | (code == 3.0)
    interior = code == 1.0
    for f in range(F):
        kept = interior if f in (1, 2) else plain
        scaled[f] = jnp.where(kept, 0.8 / jac[F * f + f], 0.0)


def own_kernel(
    jac_in, rhs_in, flags, far_y, near_y, jac, rhs, scaled
):
    near, far = [near_y[0], near_y[1]], [far_y[0], far_y[1]]
    for p in range(F * F):
        jac[p, :, 0:TY] = jac_in[p // F, p % F]
        jac[p, :, TY:EY] = unpack(near[p // 16], far[p // 16], p)
    for f in range(F):
        rhs[f, :, 0:TY] = rhs_in[f]
        rhs[f, :, TY:EY] = unpack(near[1], far[1], F * F + f)
    aside = unpack(near[1], far[1], F * F + F)
    code = jnp.concatenate([(flags[...] + 1).astype(F32), aside], axis=1)
    scale(code, jac, scaled)


def residual(f, state, rhs, jac):
    own = state[f]
    beside = roll(own, 1, 0) + roll(own, -1, 0) + roll(own, 1, 1) + roll(own, -1, 1)
    total = rhs(f) + beside
    for g in range(F):
        total = total - jac(F * f + g) * state[g]
    return total


def sweep(old, new, scaled, rhs, jac):
    for f in range(F):
        new[f] = old[f] + scaled(f) * residual(f, old, rhs, jac)


def planes_of(own, beyond):
    return lambda p: jnp.concatenate([beyond[p, 0:8], own[p], beyond[p, 8:16]], axis=0)


def columns(shape, fine_dim, coarse_dim):
    fine = iota(shape, fine_dim)
    coarse = iota(shape, coarse_dim)
    here = (coarse <= 64) & (fine >> 2 == coarse)
    return (here | ((coarse == 65) & (fine >= EY - 4))).astype(F32)


def before_kernel(
    jac_own, rhs_own, scaled_own, low, high, turn, far_x, near_x,
    state, jac, rhs, scaled, value, chip, near_state, far_state, sent, other, sides, beside, means, block, sems,
):
    odd = parity("gx")
    near_rows, far_rows = near_x[0:ROWS_SENT, :], far_x[0:ROWS_SENT, :]
    sides[0] = jnp.where(odd, near_rows, far_rows)
    sides[1] = jnp.where(odd, far_rows, near_rows)
    none = jnp.zeros((16, TY), F32)

    def put(out, at, rows):
        out[8 - rows : 8, 0:TY] = sides[0, at : at + rows]
        out[8 : 8 + rows, 0:TY] = sides[1, at : at + rows]

    for side in range(2):
        at = CORNER_AT + 3 * side
        for a in range(2):
            lanes = slice(128 * a, 128 * (a + 1))
            beside[side, a] = jnp.zeros((16, 128), F32)
            beside[side, a, 5:8] = sides[0, at : at + 3, lanes]
            beside[side, a, 8:11] = sides[1, at : at + 3, lanes]
    far, near = [[beside[side, a] for a in range(2)] for side in range(2)]
    for p in range(F * F):
        jac[p, :, 0:TY] = none
        put(jac.at[p], 2 * p, 2)
        if p % (F + 1) == 0:
            f = p // (F + 1)
            jac[p, 5:6, 0:TY] = sides[0, DIAG_AT + f : DIAG_AT + f + 1]
            jac[p, 10:11, 0:TY] = sides[1, DIAG_AT + f : DIAG_AT + f + 1]
        jac[p, :, TY:EY] = unpack(near[p // 16], far[p // 16], p)
    for f in range(F):
        rhs[f, :, 0:TY] = none
        put(rhs.at[f], RHS_AT + 3 * f, 3)
        rhs[f, :, TY:EY] = unpack(near[1], far[1], F * F + f)
    code = scaled.at[F - 1]
    code[:, 0:TY] = none
    put(code, CODE_AT, 3)
    code[:, TY:EY] = unpack(near[1], far[1], F * F + F)
    scale(code[...], jac, scaled)

    jac_plane, rhs_plane = planes_of(jac_own, jac), planes_of(rhs_own, rhs)
    scaled_plane = planes_of(scaled_own, scaled)
    for f in range(F):
        state[f] = scaled_plane(f) * rhs_plane(f)
    sweep(state, other, scaled_plane, rhs_plane, jac_plane)
    sweep(other, state, scaled_plane, rhs_plane, jac_plane)
    means[...] = jnp.zeros((8 * ROWS, EY), F32)
    for f in range(F):
        left_over = residual(f, state, rhs_plane, jac_plane)[8 : 8 + TX]
        left_over = left_over + roll(left_over, -1, 0)
        left_over = left_over + roll(left_over, -2, 0)
        for k in range(ROWS):
            means[8 * k + f : 8 * k + f + 1, :] = left_over[4 * k : 4 * k + 1]
    mean = select_columns(means[...] * 0.0625, columns((EY, 128), 0, 1))
    values = []
    for k in range(ROWS):
        rows = slice(8 * k, 8 * k + 8)
        here = mean[rows] + values[-1] if k else mean[rows]
        values.append(here * high[rows, :])
        value[rows] = values[k]
    first, last = values[-1], values[-1]
    for k in range(ROWS - 2, -1, -1):
        first = values[k] + high[8 * k : 8 * k + 8, :] * first
    lane = iota((8, 128), 1)

    packed = [near_x[ROWS_SENT : ROWS_SENT + 8, 128 * a : 128 * (a + 1)] for a in range(2)]
    theirs = [packed[0], roll(packed[0], 64, 1), packed[1]]
    theirs = [jnp.where(lane < 64, theirs[q], roll(packed[1], -2 * (q + 1), 1)) for q in range(3)]
    own = [turn[...], low[8 * ROWS - 8 :, :], high[8 * ROWS - 8 :, :]]
    b0, c, c1 = [jnp.where(odd, theirs[q], own[q]) for q in range(3)]
    e0, g, g1 = [jnp.where(odd, own[q], theirs[q]) for q in range(3)]
    w = 1.0 / (1.0 - c1 * e0)
    cw, gw = c * w, g * w
    x0 = jnp.where(odd, cw * first, first + cw * e0 * last)
    x1 = jnp.where(odd, last + gw * c1 * first, gw * last)
    chip[0] = w
    chip[1] = jnp.where(odd, gw, cw)
    chip[2] = jnp.where(odd, first, last)
    chip[3] = jnp.where(odd, c1, e0)
    chip[4] = c
    chip[5] = g
    whole_b0, whole_c, whole_c1 = b0 + c * cw * e0, cw * g, g1 + g * gw * c1
    middle = roll(whole_c, 64, 1)
    pair = lane >> 1
    even_part = jnp.where(lane < 64, whole_b0, middle)
    for q, part in enumerate((x0, x1, whole_b0, whole_c, whole_c1)):
        even_part = jnp.where(pair == 48 + q, roll(part, 32 + 2 * q, 1), even_part)
    odd_part = jnp.where(lane < 64, whole_c1, middle)
    odd_part = jnp.where(pair == 32, x0, jnp.where(pair == 33, roll(x1, 2, 1), odd_part))
    main = jnp.where(lane < 64, x0, roll(x1, 64, 1))
    rest = jnp.where(odd, odd_part, even_part)
    for f in range(F):
        block[f, 0:1] = main[f : f + 1]
        block[f, 1:2] = rest[f : f + 1]
    copies = [pltpu.make_async_copy(block, sent.at[k], sems.at[k]) for k in range(sent.shape[0])]
    for copy in copies:
        copy.start()
    near_state[15:16] = jnp.zeros((1, EY), F32)
    far_state[15:16] = jnp.zeros((1, EY), F32)
    for f in range(F):
        first, last = state[f, 8:11], state[f, 5 + TX : 8 + TX]
        near_state[3 * f : 3 * f + 3] = jnp.where(odd, first, last)
        far_state[3 * f : 3 * f + 3] = jnp.where(odd, last, first)
    for copy in copies:
        copy.wait()


def merge(one, two):
    a0, a1, b0, c, c1 = one
    d0, d1, e0, g, g1 = two
    w = 1.0 / (1.0 - c1 * e0)
    cw, gw = c * w, g * w
    return (
        a0 + cw * (d0 + e0 * a1),
        d1 + gw * (a1 + c1 * d0),
        b0 + c * cw * e0,
        cw * g,
        g1 + g * gw * c1,
    )


def between(one, two, below, above):
    a0, a1, b0, c, c1 = one
    d0, d1, e0, g, g1 = two
    outer = d0 + g * above
    last = (a1 + c * below + c1 * outer) / (1.0 - c1 * e0)
    return last, outer + e0 * last


def after_kernel(
    jac_own, rhs_own, scaled_own, low, high, jac_beyond, rhs_beyond, scaled_beyond, state_in, value, chip, far_state, near_state, got,
    correction_out, level_residual_out,
    state, other, ends, spread, tree, correction, level_residual, sems,
):
    count = got.shape[0]
    me = lax.axis_index("gx")
    lane = iota((F, 128), 1)

    odd = parity("gx")

    def stacked(k, part):
        return jnp.concatenate([got[k, f, part : part + 1, :] for f in range(F)], axis=0)

    def segment(k):
        main = stacked(2 * k, 0) + stacked(2 * k + 1, 0)
        even, other_core = stacked(2 * k, 1), stacked(2 * k + 1, 1)
        ends = roll(even, 64 - 96, 1)
        moving = ends + other_core
        middle = roll(jnp.where(lane < 96, even, other_core), 64, 1)
        inner = [main, roll(main, 64, 1), even, middle, other_core]
        outer = [moving, roll(moving, -2, 1)] + [roll(ends, -2 * q, 1) for q in (2, 3, 4)]
        return [jnp.where(lane < 64, inner[q], outer[q]) for q in range(5)]

    level, starts, total = [segment(k) for k in range(count // 2)], [], 0
    while True:
        starts.append(total)
        for parts in level:
            for q in range(5):
                tree[total, q, 0:F] = parts[q]
            total += 1
        if len(level) <= 2:
            break
        level = [merge(level[2 * k], level[2 * k + 1]) for k in range(len(level) // 2)]
    below = above = jnp.zeros((F, 128), F32)
    my_chip = me >> 1
    if count > 2:
        for size in range(len(starts) - 1, -1, -1):
            at = starts[size] + 2 * (my_chip >> (size + 1))
            one = [tree[at, q, 0:F] for q in range(5)]
            two = [tree[at + 1, q, 0:F] for q in range(5)]
            last, first = between(one, two, below, above)
            second = (my_chip >> size) & 1 == 1
            below, above = jnp.where(second, last, below), jnp.where(second, above, first)
    partner = me + 1 - 2 * (me & 1)
    main, rest = stacked(partner, 0), stacked(partner, 1)
    from_even = jnp.where(lane < 64, roll(main, 64, 1), roll(rest, 64 - 98, 1))
    from_odd = jnp.where(lane < 64, main, rest)
    w, share, own, turn, c, g = [chip[q, 0:F, :] for q in range(6)]
    theirs = jnp.where(odd, from_even, from_odd) / share
    lower, upper = c * below, g * above
    inside = jnp.where(odd, lower, upper) + theirs
    inside = w * (inside + turn * (own + jnp.where(odd, upper, lower)))
    below, above = jnp.where(odd, inside, below), jnp.where(odd, above, inside)

    used = lane <= 65
    ends[...] = jnp.zeros((64, 128), F32)
    ends[0:F] = jnp.where(used, below, 0.0)
    ends[8 * (ROWS + 1) : 8 * (ROWS + 1) + F] = jnp.where(used, above, 0.0)
    here = above
    for k in range(ROWS - 1, -1, -1):
        rows = slice(8 * k, 8 * k + F)
        here = value[rows] + low[rows] * below + high[rows] * here
        ends[8 * (k + 1) : 8 * (k + 1) + F] = jnp.where(used, here, 0.0)
    spread[...] = select_columns(ends[...], columns((128, EY), 1, 0))

    jac_plane, rhs_plane = planes_of(jac_own, jac_beyond), planes_of(rhs_own, rhs_beyond)
    scaled_plane = planes_of(scaled_own, scaled_beyond)
    upper = iota((8, EY), 0) < 4

    def repeated(row):
        return jnp.broadcast_to(spread[row : row + 1, :], (8, EY))

    for f in range(F):
        tiles = []
        for v in range(EX // 8):
            one = repeated(8 * (2 * v - 1) + f) if v else 0.0
            two = repeated(8 * (2 * v) + f) if v < EX // 8 - 1 else 0.0
            tiles.append(jnp.where(upper, one, two))
        added = jnp.where(scaled_plane(f) != 0.0, jnp.concatenate(tiles, axis=0), 0.0)
        other[f] = state_in[f]
        far, near = far_state[3 * f : 3 * f + 3], near_state[3 * f : 3 * f + 3]
        other[f, 5:8] = jnp.where(odd, near, far)
        other[f, 8 + TX : 11 + TX] = jnp.where(odd, far, near)
        state[f] = other[f] + added
    sweep(state, other, scaled_plane, rhs_plane, jac_plane)
    sweep(other, state, scaled_plane, rhs_plane, jac_plane)
    copies = []
    for f in range(F):
        correction[f] = state[f, 8 : 8 + TX, 0:TY]
        copies.append(
            pltpu.make_async_copy(correction.at[f], correction_out.at[f], sems.at[0, f])
        )
        copies[-1].start()
    for f in range(F):
        level_residual[f] = residual(f, state, rhs_plane, jac_plane)[8 : 8 + TX, 0:TY]
        copies.append(
            pltpu.make_async_copy(level_residual.at[f], level_residual_out.at[f], sems.at[1, f])
        )
        copies[-1].start()
    for copy in copies:
        copy.wait()


def shape_of(*dims):
    return jax.ShapeDtypeStruct(dims, F32)


def call(kernel, outs, scratch, *args, space=pltpu.VMEM, out_space=None):
    return pl.pallas_call(
        kernel,
        out_shape=outs,
        in_specs=[pl.BlockSpec(memory_space=space)] * len(args),
        out_specs=[pl.BlockSpec(memory_space=o) for o in out_space or [pltpu.VMEM] * len(outs)],
        scratch_shapes=scratch,
        compiler_params=pltpu.CompilerParams(vmem_limit_bytes=32 * 1024 * 1024),
    )(*args)


def swap(value, axis, start):
    count = lax.axis_size(axis)
    firsts = range(start, count - 1, 2)
    return lax.ppermute(value, axis, [(i, i + 1) for i in firsts] + [(i + 1, i) for i in firsts])


def local(fine, owner, flags, jac, coef):
    strip = shape_of(2, TX, 128)
    rhs, near, far = call(
        restrict_kernel,
        [shape_of(F, TX, TY), strip, strip],
        [
            pltpu.VMEM((F, 4, 2 * TX, 128), F32),
            pltpu.VMEM((4, 2 * TX, 128), jnp.int32),
            pltpu.VMEM((TX, TY), jnp.int32),
            pltpu.VMEM((F, F, TX, TY), F32),
            pltpu.VMEM((F, ROWS, TY // 4), F32),
            pltpu.SemaphoreType.DMA((F + 2, 4)),
        ],
        *[pltpu.with_memory_space_constraint(x, pltpu.HBM) for x in (fine, owner, flags, jac, coef)],
        space=pltpu.HBM,
    )
    near_rows, far_rows = call(
        rows_kernel, [shape_of(ROWS_SENT, TY), shape_of(ROWS_SENT, TY)], [], jac, rhs, flags
    )
    far_y = swap(far, "gy", 1)
    near_y = swap(near, "gy", 0)
    rows, lines, line = shape_of(ROWS_SENT, TY), shape_of(8 * ROWS, 128), shape_of(8, 128)
    near_rows, far_rows, low, high, turn = call(
        corners_kernel,
        [shape_of(ROWS_SENT + 8, TY), shape_of(ROWS_SENT + 8, TY), lines, lines, line],
        [pltpu.VMEM((8 * ROWS, 128), F32)],
        near_rows, far_rows, coef, far_y, near_y,
    )
    far_x = swap(far_rows, "gx", 1)
    near_x = swap(near_rows, "gx", 0)
    count = lax.axis_size("gx")
    own = shape_of(F, TX, EY)
    jac_own, rhs_own, scaled_own = call(
        own_kernel, [shape_of(F * F, TX, EY), own, own], [], jac, rhs, flags, far_y, near_y
    )
    tile = pltpu.VMEM((F, EX, EY), F32)
    beyond = shape_of(F, 16, EY)
    ends = shape_of(16, EY)
    state, jac_beyond, rhs_beyond, scaled_beyond, value, chip, near_state, far_state, sent = call(
        before_kernel,
        [
            shape_of(F, EX, EY), shape_of(F * F, 16, EY), beyond, beyond, lines, shape_of(6, 8, 128), ends, ends,
            shape_of(count, F, 2, 128),
        ],
        [
            tile,
            pltpu.VMEM((2, ROWS_SENT, TY), F32),
            pltpu.VMEM((2, 2, 16, 128), F32),
            pltpu.VMEM((8 * ROWS, EY), F32),
            pltpu.VMEM((F, 2, 128), F32),
            pltpu.SemaphoreType.DMA((count,)),
        ],
        jac_own, rhs_own, scaled_own, low, high, turn, far_x, near_x,
        out_space=[pltpu.VMEM] * 8 + [pl.ANY],
    )
    got = lax.all_to_all(sent, "gx", 0, 0, tiled=True)
    far_state = swap(far_state, "gx", 1)
    near_state = swap(near_state, "gx", 0)
    return tuple(
        call(
            after_kernel,
            [shape_of(F, TX, TY), shape_of(F, TX, TY)],
            [
                tile,
                tile,
                pltpu.VMEM((64, 128), F32),
                pltpu.VMEM((64, EY), F32),
                pltpu.VMEM((count, 5, 8, 128), F32),
                pltpu.VMEM((F, TX, TY), F32),
                pltpu.VMEM((F, TX, TY), F32),
                pltpu.SemaphoreType.DMA((2, F)),
            ],
            jac_own, rhs_own, scaled_own, low, high, jac_beyond, rhs_beyond, scaled_beyond, state, value, chip,
            far_state, near_state, got,
            out_space=[pl.ANY] * 2,
        )
    )


def solution(mesh):
    in_specs = (
        P(None, "gx", "gy"),
        P("gx", "gy"),
        P("gx", "gy"),
        P(None, None, "gx", "gy"),
        P(None, "gx", "gy"),
    )
    out_specs = (P(None, "gx", "gy"), P(None, "gx", "gy"))
    return jax.shard_map(local, mesh=mesh, in_specs=in_specs, out_specs=out_specs, check_vma=False)
```

```python
import jax
import jax.numpy as jnp
from jax import lax
from jax.experimental import pallas as pl
from jax.experimental.pallas import tpu as pltpu
from jax.sharding import PartitionSpec as P

F = 5
TX = 24
TY = 256
EX = 32
EY = 384
ROWS = 6
PLANES = 31
F32 = jnp.float32


def iota(shape, dim):
    return lax.broadcasted_iota(jnp.int32, shape, dim)


def parts_of(x):
    head = x.astype(jnp.bfloat16)
    rest = x - head.astype(F32)
    middle = rest.astype(jnp.bfloat16)
    return head, middle, (rest - middle.astype(F32)).astype(jnp.bfloat16)


def select_columns(x, chosen):
    rows = x.shape[0]
    whole = jnp.concatenate(parts_of(x), axis=0)
    out = jnp.dot(whole, chosen.astype(jnp.bfloat16), preferred_element_type=F32)
    return out[0:rows] + out[rows : 2 * rows] + out[2 * rows :]


def roll(x, shift, axis):
    shift = shift % x.shape[axis]
    return x if shift == 0 else pltpu.roll(x, shift, axis)


def parity(axis):
    return lax.rem(lax.axis_index(axis), 2) == 1


def restrict_kernel(
    fine_in, owner_in, flags_in, jac_in, coef_in, rhs, near, far,
    fine, owner, flags, jac, coef, sems,
):
    def tile_copy(source, target, sem, j):
        return pltpu.make_async_copy(source.at[:, 128 * j : 128 * (j + 1)], target.at[j], sem)

    owners = [tile_copy(owner_in, owner, sems.at[0, j], j) for j in range(4)]
    fines = [
        [tile_copy(fine_in.at[f], fine.at[f], sems.at[1 + f, j], j) for j in range(4)]
        for f in range(F)
    ]
    late = [
        pltpu.make_async_copy(flags_in, flags, sems.at[F + 1, 0]),
        pltpu.make_async_copy(coef_in, coef, sems.at[F + 1, 1]),
        pltpu.make_async_copy(jac_in, jac, sems.at[F + 1, 2]),
    ]
    for copy in owners + sum(fines, []) + late:
        copy.start()
    for copy in owners:
        copy.wait()

    def halves(load):
        return [
            jnp.concatenate([load(j, pl.ds(start, TX, 2)) for j in range(4)], axis=1)
            for start in (0, 1)
        ]

    shape = (TX, 2 * TY)
    row = iota(shape, 0)
    col = iota(shape, 1) >> 1
    codes = [
        ((o >> 8) - row + 1) * 3 + (o & (TY - 1)) - col + 1
        for o in halves(lambda j, rows: owner[j, rows, :])
    ]
    masks = [[code == k for code in codes] for k in range(9)]
    gathered = []
    for f in range(F):
        for copy in fines[f]:
            copy.wait()
        values = halves(lambda j, rows: fine[f, j, rows, :])
        total = None
        for dy in (-1, 0, 1):
            part = None
            for dx in (-1, 0, 1):
                mask = masks[(dx + 1) * 3 + dy + 1]
                moved = jnp.where(mask[0], values[0], 0.0) + jnp.where(mask[1], values[1], 0.0)
                moved = roll(moved, dx, 0)
                part = moved if part is None else part + moved
            part = roll(part, 2 * dy, 1)
            total = part if total is None else total + part
        gathered.append(total)
    pairs = ((iota((2 * TY, TY), 0) >> 1) == iota((2 * TY, TY), 1)).astype(F32)
    gathered.append(jnp.zeros((8, 2 * TY), F32))
    for copy in late:
        copy.wait()
    summed = select_columns(jnp.concatenate(gathered, axis=0), pairs)
    planes = [summed[TX * f : TX * (f + 1)] for f in range(F)]
    for f in range(F):
        rhs[f] = planes[f]
    planes.append((flags[...] + 1).astype(F32))

    odd = parity("gy")
    slot = iota((TX, 128), 1) >> 3
    for a in range(2):
        first = jnp.zeros((TX, 128), F32)
        last = jnp.zeros((TX, 128), F32)
        for t in range(16):
            p = 16 * a + t
            if p >= PLANES:
                continue
            if p < F * F:
                head, tail = jac[p // F, p % F, :, 0:128], jac[p // F, p % F, :, TY - 128 : TY]
            else:
                head, tail = planes[p - F * F][:, 0:128], planes[p - F * F][:, TY - 128 : TY]
            first = jnp.where(slot == t, roll(head, 8 * t, 1), first)
            last = jnp.where(slot == t, roll(tail, 8 * t - 120, 1), last)
        near[a] = jnp.where(odd, first, last)
        far[a] = jnp.where(odd, last, first)
    lane = iota((ROWS, 128), 1)
    first, last = near[1, 0:ROWS, :], far[1, 0:ROWS, :]
    for f in range(F):
        wide = jnp.concatenate([coef[f], coef[f]], axis=1)
        head, tail = roll(wide, 120 + f, 1), roll(wide, 120 + f - 63, 1)
        first = jnp.where(lane == 120 + f, jnp.where(odd, head, tail), first)
        last = jnp.where(lane == 120 + f, jnp.where(odd, tail, head), last)
    near[1, 0:ROWS, :] = first
    far[1, 0:ROWS, :] = last


JAC_AT, RHS_AT, CODE_AT, DIAG_AT, CORNER_AT, ROWS_SENT = 0, 50, 65, 68, 74, 80


def rows_kernel(jac, rhs, flags, near, far):
    def write(out, first):
        start = 0 if first else TX - 2
        wide = 0 if first else TX - 3
        third = 2 if first else TX - 3
        for p in range(F * F):
            out[2 * p : 2 * p + 2] = jac[p // F, p % F, start : start + 2, :]
        for f in range(F):
            at = RHS_AT + 3 * f
            out[at : at + 3] = rhs[f, wide : wide + 3, :]
            out[DIAG_AT + f : DIAG_AT + f + 1] = jac[f, f, third : third + 1, :]
        out[CODE_AT : CODE_AT + 3] = (flags[wide : wide + 3, :] + 1).astype(F32)
        out[73:ROWS_SENT] = jnp.zeros((ROWS_SENT - 73, TY), F32)

    odd = parity("gx")

    @pl.when(odd)
    def _():
        write(near, True)
        write(far, False)

    @pl.when(jnp.logical_not(odd))
    def _():
        write(near, False)
        write(far, True)


def corners_kernel(near_rows, far_rows, coef, far_y, near_y, near, far, low, high, turn, diag):
    odd = parity("gx")
    near[0:ROWS_SENT] = near_rows[...]
    far[0:ROWS_SENT] = far_rows[...]
    far[ROWS_SENT : ROWS_SENT + 8] = jnp.zeros((8, TY), F32)
    for side, strip in enumerate((far_y, near_y)):
        at = CORNER_AT + 3 * side
        for a in range(2):
            lanes = slice(128 * a, 128 * (a + 1))
            first, last = strip[a, 0:3, :], strip[a, TX - 3 : TX, :]
            near[at : at + 3, lanes] = jnp.where(odd, first, last)
            far[at : at + 3, lanes] = jnp.where(odd, last, first)

    lane = iota((ROWS, 128), 1)
    odd_y = parity("gy")
    right = jnp.where(odd_y, far_y[1, 0:ROWS, :], near_y[1, 0:ROWS, :])
    left = jnp.where(odd_y, near_y[1, 0:ROWS, :], far_y[1, 0:ROWS, :])
    diag[...] = jnp.full((8 * ROWS, 128), 4.0, F32)
    for f in range(F):
        wide = jnp.concatenate([coef[f], coef[f]], axis=1)
        wide = jnp.where(lane == 64, roll(right, 64 - 120 - f, 1), wide)
        wide = jnp.where(lane == 65, roll(left, 65 - 120 - f, 1), wide)
        wide = jnp.where((lane <= 65) & (wide > 0.0), wide, 4.0)
        for k in range(ROWS):
            diag[8 * k + f : 8 * k + f + 1, :] = wide[k : k + 1, :]
    lows, highs = [], []
    for k in range(ROWS):
        d = diag[8 * k : 8 * k + 8, :]
        inverse = 1.0 / (d - highs[-1] if k else d)
        lows.append(lows[-1] * inverse if k else inverse)
        highs.append(inverse)
        low[8 * k : 8 * k + 8] = lows[k]
        high[8 * k : 8 * k + 8] = highs[k]
    first_low = lows[-1]
    for k in range(ROWS - 2, -1, -1):
        first_low = lows[k] + highs[k] * first_low
    turn[...] = first_low
    lane = iota((8, 128), 1)
    ends = highs[-1]
    for q, part in enumerate((first_low, lows[-1], highs[-1])):
        ends = jnp.where(lane >> 1 == 33 + q, roll(part, 2 * (q + 1), 1), ends)
    near[ROWS_SENT : ROWS_SENT + 8, 0:128] = jnp.where(lane < 64, first_low, roll(lows[-1], 64, 1))
    near[ROWS_SENT : ROWS_SENT + 8, 128:TY] = ends


def unpack(near, far, p):
    odd = parity("gy")
    right = jnp.where(odd, far, near)
    left = jnp.where(odd, near, far)
    lane = iota(near.shape, 1)
    return jnp.where(
        lane < 8,
        roll(right, -8 * (p % 16), 1),
        jnp.where(lane >= 120, roll(left, 120 - 8 * (p % 16), 1), 0.0),
    )


def scale(code, jac, scaled):
    plain = (code == 1.0) | (code == 3.0)
    interior = code == 1.0
    for f in range(F):
        kept = interior if f in (1, 2) else plain
        scaled[f] = jnp.where(kept, 0.8 / jac[F * f + f], 0.0)


def own_kernel(
    jac_in, rhs_in, flags, far_y, near_y, jac, rhs, scaled
):
    near, far = [near_y[0], near_y[1]], [far_y[0], far_y[1]]
    for p in range(F * F):
        jac[p, :, 0:TY] = jac_in[p // F, p % F]
        jac[p, :, TY:EY] = unpack(near[p // 16], far[p // 16], p)
    for f in range(F):
        rhs[f, :, 0:TY] = rhs_in[f]
        rhs[f, :, TY:EY] = unpack(near[1], far[1], F * F + f)
    aside = unpack(near[1], far[1], F * F + F)
    code = jnp.concatenate([(flags[...] + 1).astype(F32), aside], axis=1)
    scale(code, jac, scaled)


def residual(f, state, rhs, jac):
    own = state[f]
    beside = roll(own, 1, 0) + roll(own, -1, 0) + roll(own, 1, 1) + roll(own, -1, 1)
    total = rhs(f) + beside
    for g in range(F):
        total = total - jac(F * f + g) * state[g]
    return total


def sweep(old, new, scaled, rhs, jac):
    for f in range(F):
        new[f] = old[f] + scaled(f) * residual(f, old, rhs, jac)


def planes_of(own, beyond):
    return lambda p: jnp.concatenate([own[p], beyond[p]], axis=0)


def columns(shape, fine_dim, coarse_dim):
    fine = iota(shape, fine_dim)
    coarse = iota(shape, coarse_dim)
    here = (coarse <= 64) & (fine >> 2 == coarse)
    return (here | ((coarse == 65) & (fine >= EY - 4))).astype(F32)


def before_kernel(
    jac_own, rhs_own, scaled_own, low, high, turn, far_x, near_x,
    state, jac, rhs, scaled, value, chip, near_state, far_state, sent, other, sides, beside, means, block, sems,
):
    odd = parity("gx")
    near_rows, far_rows = near_x[0:ROWS_SENT, :], far_x[0:ROWS_SENT, :]
    sides[0] = jnp.where(odd, near_rows, far_rows)
    sides[1] = jnp.where(odd, far_rows, near_rows)
    none = jnp.zeros((8, TY), F32)

    def put(out, at, rows):
        out[8 - rows : 8, 0:TY] = sides[0, at : at + rows]
        out[0:rows, 0:TY] = sides[1, at : at + rows]

    for side in range(2):
        at = CORNER_AT + 3 * side
        for a in range(2):
            lanes = slice(128 * a, 128 * (a + 1))
            beside[side, a] = jnp.zeros((8, 128), F32)
            beside[side, a, 5:8] = sides[0, at : at + 3, lanes]
            beside[side, a, 0:3] = sides[1, at : at + 3, lanes]
    far, near = [[beside[side, a] for a in range(2)] for side in range(2)]
    for p in range(F * F):
        jac[p, :, 0:TY] = none
        put(jac.at[p], 2 * p, 2)
        if p % (F + 1) == 0:
            f = p // (F + 1)
            jac[p, 5:6, 0:TY] = sides[0, DIAG_AT + f : DIAG_AT + f + 1]
            jac[p, 2:3, 0:TY] = sides[1, DIAG_AT + f : DIAG_AT + f + 1]
        jac[p, :, TY:EY] = unpack(near[p // 16], far[p // 16], p)
    for f in range(F):
        rhs[f, :, 0:TY] = none
        put(rhs.at[f], RHS_AT + 3 * f, 3)
        rhs[f, :, TY:EY] = unpack(near[1], far[1], F * F + f)
    code = scaled.at[F - 1]
    code[:, 0:TY] = none
    put(code, CODE_AT, 3)
    code[:, TY:EY] = unpack(near[1], far[1], F * F + F)
    scale(code[...], jac, scaled)

    jac_plane, rhs_plane = planes_of(jac_own, jac), planes_of(rhs_own, rhs)
    scaled_plane = planes_of(scaled_own, scaled)
    for f in range(F):
        state[f] = scaled_plane(f) * rhs_plane(f)
    sweep(state, other, scaled_plane, rhs_plane, jac_plane)
    sweep(other, state, scaled_plane, rhs_plane, jac_plane)
    means[...] = jnp.zeros((8 * ROWS, EY), F32)
    for f in range(F):
        left_over = residual(f, state, rhs_plane, jac_plane)[0:TX]
        left_over = left_over + roll(left_over, -1, 0)
        left_over = left_over + roll(left_over, -2, 0)
        for k in range(ROWS):
            means[8 * k + f : 8 * k + f + 1, :] = left_over[4 * k : 4 * k + 1]
    mean = select_columns(means[...] * 0.0625, columns((EY, 128), 0, 1))
    values = []
    for k in range(ROWS):
        rows = slice(8 * k, 8 * k + 8)
        here = mean[rows] + values[-1] if k else mean[rows]
        values.append(here * high[rows, :])
        value[rows] = values[k]
    first, last = values[-1], values[-1]
    for k in range(ROWS - 2, -1, -1):
        first = values[k] + high[8 * k : 8 * k + 8, :] * first
    lane = iota((8, 128), 1)

    packed = [near_x[ROWS_SENT : ROWS_SENT + 8, 128 * a : 128 * (a + 1)] for a in range(2)]
    theirs = [packed[0], roll(packed[0], 64, 1), packed[1]]
    theirs = [jnp.where(lane < 64, theirs[q], roll(packed[1], -2 * (q + 1), 1)) for q in range(3)]
    own = [turn[...], low[8 * ROWS - 8 :, :], high[8 * ROWS - 8 :, :]]
    b0, c, c1 = [jnp.where(odd, theirs[q], own[q]) for q in range(3)]
    e0, g, g1 = [jnp.where(odd, own[q], theirs[q]) for q in range(3)]
    w = 1.0 / (1.0 - c1 * e0)
    cw, gw = c * w, g * w
    x0 = jnp.where(odd, cw * first, first + cw * e0 * last)
    x1 = jnp.where(odd, last + gw * c1 * first, gw * last)
    chip[0] = w
    chip[1] = jnp.where(odd, gw, cw)
    chip[2] = jnp.where(odd, first, last)
    chip[3] = jnp.where(odd, c1, e0)
    chip[4] = c
    chip[5] = g
    whole_b0, whole_c, whole_c1 = b0 + c * cw * e0, cw * g, g1 + g * gw * c1
    middle = roll(whole_c, 64, 1)
    pair = lane >> 1
    even_part = jnp.where(lane < 64, whole_b0, middle)
    for q, part in enumerate((x0, x1, whole_b0, whole_c, whole_c1)):
        even_part = jnp.where(pair == 48 + q, roll(part, 32 + 2 * q, 1), even_part)
    odd_part = jnp.where(lane < 64, whole_c1, middle)
    odd_part = jnp.where(pair == 32, x0, jnp.where(pair == 33, roll(x1, 2, 1), odd_part))
    main = jnp.where(lane < 64, x0, roll(x1, 64, 1))
    rest = jnp.where(odd, odd_part, even_part)
    each = block.shape[0]
    for f in range(F):
        both = jnp.concatenate([main[f : f + 1], rest[f : f + 1]], axis=0)
        for k in range(each):
            block[k, f] = both
    copies = [
        pltpu.make_async_copy(block, sent.at[k * each : (k + 1) * each], sems.at[k])
        for k in range(sent.shape[0] // each)
    ]
    for copy in copies:
        copy.start()
    near_state[15:16] = jnp.zeros((1, EY), F32)
    far_state[15:16] = jnp.zeros((1, EY), F32)
    for f in range(F):
        first, last = state[f, 0:3], state[f, TX - 3 : TX]
        near_state[3 * f : 3 * f + 3] = jnp.where(odd, first, last)
        far_state[3 * f : 3 * f + 3] = jnp.where(odd, last, first)
    for copy in copies:
        copy.wait()


def merge(one, two):
    a0, a1, b0, c, c1 = one
    d0, d1, e0, g, g1 = two
    w = 1.0 / (1.0 - c1 * e0)
    cw, gw = c * w, g * w
    return (
        a0 + cw * (d0 + e0 * a1),
        d1 + gw * (a1 + c1 * d0),
        b0 + c * cw * e0,
        cw * g,
        g1 + g * gw * c1,
    )


def between(one, two, below, above):
    a0, a1, b0, c, c1 = one
    d0, d1, e0, g, g1 = two
    outer = d0 + g * above
    last = (a1 + c * below + c1 * outer) / (1.0 - c1 * e0)
    return last, outer + e0 * last


def after_kernel(
    jac_own, rhs_own, scaled_own, low, high, jac_beyond, rhs_beyond, scaled_beyond, state_in, value, chip, far_state, near_state, got,
    correction_out, level_residual_out,
    state, other, ends, spread, tree, correction, level_residual, sems,
):
    count = got.shape[0]
    me = lax.axis_index("gx")
    lane = iota((F, 128), 1)

    odd = parity("gx")

    def stacked(k, part):
        return jnp.concatenate([got[k, f, part : part + 1, :] for f in range(F)], axis=0)

    def segment(k):
        main = stacked(2 * k, 0) + stacked(2 * k + 1, 0)
        even, other_core = stacked(2 * k, 1), stacked(2 * k + 1, 1)
        ends = roll(even, 64 - 96, 1)
        moving = ends + other_core
        middle = roll(jnp.where(lane < 96, even, other_core), 64, 1)
        inner = [main, roll(main, 64, 1), even, middle, other_core]
        outer = [moving, roll(moving, -2, 1)] + [roll(ends, -2 * q, 1) for q in (2, 3, 4)]
        return [jnp.where(lane < 64, inner[q], outer[q]) for q in range(5)]

    level, starts, total = [segment(k) for k in range(count // 2)], [], 0
    while True:
        starts.append(total)
        for parts in level:
            for q in range(5):
                tree[total, q, 0:F] = parts[q]
            total += 1
        if len(level) <= 2:
            break
        level = [merge(level[2 * k], level[2 * k + 1]) for k in range(len(level) // 2)]
    below = above = jnp.zeros((F, 128), F32)
    my_chip = me >> 1
    if count > 2:
        for size in range(len(starts) - 1, -1, -1):
            at = starts[size] + 2 * (my_chip >> (size + 1))
            one = [tree[at, q, 0:F] for q in range(5)]
            two = [tree[at + 1, q, 0:F] for q in range(5)]
            last, first = between(one, two, below, above)
            second = (my_chip >> size) & 1 == 1
            below, above = jnp.where(second, last, below), jnp.where(second, above, first)
    partner = me + 1 - 2 * (me & 1)
    main, rest = stacked(partner, 0), stacked(partner, 1)
    from_even = jnp.where(lane < 64, roll(main, 64, 1), roll(rest, 64 - 98, 1))
    from_odd = jnp.where(lane < 64, main, rest)
    w, share, own, turn, c, g = [chip[q, 0:F, :] for q in range(6)]
    theirs = jnp.where(odd, from_even, from_odd) / share
    lower, upper = c * below, g * above
    inside = jnp.where(odd, lower, upper) + theirs
    inside = w * (inside + turn * (own + jnp.where(odd, upper, lower)))
    below, above = jnp.where(odd, inside, below), jnp.where(odd, above, inside)

    used = lane <= 65
    ends[...] = jnp.zeros((64, 128), F32)
    ends[0:F] = jnp.where(used, below, 0.0)
    ends[8 * (ROWS + 1) : 8 * (ROWS + 1) + F] = jnp.where(used, above, 0.0)
    here = above
    for k in range(ROWS - 1, -1, -1):
        rows = slice(8 * k, 8 * k + F)
        here = value[rows] + low[rows] * below + high[rows] * here
        ends[8 * (k + 1) : 8 * (k + 1) + F] = jnp.where(used, here, 0.0)
    spread[...] = select_columns(ends[...], columns((128, EY), 1, 0))

    jac_plane, rhs_plane = planes_of(jac_own, jac_beyond), planes_of(rhs_own, rhs_beyond)
    scaled_plane = planes_of(scaled_own, scaled_beyond)
    upper = iota((8, EY), 0) < 4

    def repeated(row):
        return jnp.broadcast_to(spread[row : row + 1, :], (8, EY))

    for f in range(F):
        tiles = []
        for v in range(EX // 8):
            groups = (2 * v + 1, (2 * v + 2) % 8)
            one, two = [repeated(8 * group + f) for group in groups]
            tiles.append(jnp.where(upper, one, two))
        added = jnp.where(scaled_plane(f) != 0.0, jnp.concatenate(tiles, axis=0), 0.0)
        other[f] = state_in[f]
        far, near = far_state[3 * f : 3 * f + 3], near_state[3 * f : 3 * f + 3]
        other[f, EX - 3 : EX] = jnp.where(odd, near, far)
        other[f, TX : TX + 3] = jnp.where(odd, far, near)
        state[f] = other[f] + added
    sweep(state, other, scaled_plane, rhs_plane, jac_plane)
    sweep(other, state, scaled_plane, rhs_plane, jac_plane)
    copies = []
    for f in range(F):
        correction[f] = state[f, 0:TX, 0:TY]
        copies.append(
            pltpu.make_async_copy(correction.at[f], correction_out.at[f], sems.at[0, f])
        )
        copies[-1].start()
    for f in range(F):
        level_residual[f] = residual(f, state, rhs_plane, jac_plane)[0:TX, 0:TY]
        copies.append(
            pltpu.make_async_copy(level_residual.at[f], level_residual_out.at[f], sems.at[1, f])
        )
        copies[-1].start()
    for copy in copies:
        copy.wait()


def shape_of(*dims):
    return jax.ShapeDtypeStruct(dims, F32)


def call(kernel, outs, scratch, *args, space=pltpu.VMEM, out_space=None):
    return pl.pallas_call(
        kernel,
        out_shape=outs,
        in_specs=[pl.BlockSpec(memory_space=space)] * len(args),
        out_specs=[pl.BlockSpec(memory_space=o) for o in out_space or [pltpu.VMEM] * len(outs)],
        scratch_shapes=scratch,
        compiler_params=pltpu.CompilerParams(vmem_limit_bytes=32 * 1024 * 1024),
    )(*args)


def swap(value, axis, start):
    count = lax.axis_size(axis)
    firsts = range(start, count - 1, 2)
    return lax.ppermute(value, axis, [(i, i + 1) for i in firsts] + [(i + 1, i) for i in firsts])


def local(fine, owner, flags, jac, coef):
    strip = shape_of(2, TX, 128)
    rhs, near, far = call(
        restrict_kernel,
        [shape_of(F, TX, TY), strip, strip],
        [
            pltpu.VMEM((F, 4, 2 * TX, 128), F32),
            pltpu.VMEM((4, 2 * TX, 128), jnp.int32),
            pltpu.VMEM((TX, TY), jnp.int32),
            pltpu.VMEM((F, F, TX, TY), F32),
            pltpu.VMEM((F, ROWS, TY // 4), F32),
            pltpu.SemaphoreType.DMA((F + 2, 4)),
        ],
        *[pltpu.with_memory_space_constraint(x, pltpu.HBM) for x in (fine, owner, flags, jac, coef)],
        space=pltpu.HBM,
    )
    near_rows, far_rows = call(
        rows_kernel, [shape_of(ROWS_SENT, TY), shape_of(ROWS_SENT, TY)], [], jac, rhs, flags
    )
    far_y = swap(far, "gy", 1)
    near_y = swap(near, "gy", 0)
    rows, lines, line = shape_of(ROWS_SENT, TY), shape_of(8 * ROWS, 128), shape_of(8, 128)
    near_rows, far_rows, low, high, turn = call(
        corners_kernel,
        [shape_of(ROWS_SENT + 8, TY), shape_of(ROWS_SENT + 8, TY), lines, lines, line],
        [pltpu.VMEM((8 * ROWS, 128), F32)],
        near_rows, far_rows, coef, far_y, near_y,
    )
    far_x = swap(far_rows, "gx", 1)
    near_x = swap(near_rows, "gx", 0)
    count = lax.axis_size("gx")
    own = shape_of(F, TX, EY)
    jac_own, rhs_own, scaled_own = call(
        own_kernel, [shape_of(F * F, TX, EY), own, own], [], jac, rhs, flags, far_y, near_y
    )
    tile = pltpu.VMEM((F, EX, EY), F32)
    beyond = shape_of(F, 8, EY)
    ends = shape_of(16, EY)
    state, jac_beyond, rhs_beyond, scaled_beyond, value, chip, near_state, far_state, sent = call(
        before_kernel,
        [
            shape_of(F, EX, EY), shape_of(F * F, 8, EY), beyond, beyond, lines, shape_of(6, 8, 128), ends, ends,
            shape_of(count, F, 2, 128),
        ],
        [
            tile,
            pltpu.VMEM((2, ROWS_SENT, TY), F32),
            pltpu.VMEM((2, 2, 8, 128), F32),
            pltpu.VMEM((8 * ROWS, EY), F32),
            pltpu.VMEM((min(count, 8), F, 2, 128), F32),
            pltpu.SemaphoreType.DMA((count,)),
        ],
        jac_own, rhs_own, scaled_own, low, high, turn, far_x, near_x,
        out_space=[pltpu.VMEM] * 8 + [pl.ANY],
    )
    got = lax.all_to_all(sent, "gx", 0, 0, tiled=True)
    far_state = swap(far_state, "gx", 1)
    near_state = swap(near_state, "gx", 0)
    return tuple(
        call(
            after_kernel,
            [shape_of(F, TX, TY), shape_of(F, TX, TY)],
            [
                tile,
                tile,
                pltpu.VMEM((64, 128), F32),
                pltpu.VMEM((64, EY), F32),
                pltpu.VMEM((count, 5, 8, 128), F32),
                pltpu.VMEM((F, TX, TY), F32),
                pltpu.VMEM((F, TX, TY), F32),
                pltpu.SemaphoreType.DMA((2, F)),
            ],
            jac_own, rhs_own, scaled_own, low, high, jac_beyond, rhs_beyond, scaled_beyond, state, value, chip,
            far_state, near_state, got,
            out_space=[pl.ANY] * 2,
        )
    )


def solution(mesh):
    in_specs = (
        P(None, "gx", "gy"),
        P("gx", "gy"),
        P("gx", "gy"),
        P(None, None, "gx", "gy"),
        P(None, "gx", "gy"),
    )
    out_specs = (P(None, "gx", "gy"), P(None, "gx", "gy"))
    return jax.shard_map(local, mesh=mesh, in_specs=in_specs, out_specs=out_specs, check_vma=False)
```

```python
import jax
import jax.numpy as jnp
from jax import lax
from jax.experimental import pallas as pl
from jax.experimental.pallas import tpu as pltpu
from jax.sharding import PartitionSpec as P

F = 5
TX = 24
TY = 256
EX = 32
EY = 384
ROWS = 6
PLANES = 31
F32 = jnp.float32


def iota(shape, dim):
    return lax.broadcasted_iota(jnp.int32, shape, dim)


def parts_of(x):
    head = x.astype(jnp.bfloat16)
    rest = x - head.astype(F32)
    middle = rest.astype(jnp.bfloat16)
    return head, middle, (rest - middle.astype(F32)).astype(jnp.bfloat16)


def select_columns(x, chosen):
    rows = x.shape[0]
    whole = jnp.concatenate(parts_of(x), axis=0)
    out = jnp.dot(whole, chosen.astype(jnp.bfloat16), preferred_element_type=F32)
    return out[0:rows] + out[rows : 2 * rows] + out[2 * rows :]


def roll(x, shift, axis):
    shift = shift % x.shape[axis]
    return x if shift == 0 else pltpu.roll(x, shift, axis)


def parity(axis):
    return lax.rem(lax.axis_index(axis), 2) == 1


def restrict_kernel(
    fine_in, owner_in, flags_in, jac_in, coef_in, rhs, near, far,
    fine, owner, flags, jac, coef, sems,
):
    def tile_copy(source, target, sem, j):
        return pltpu.make_async_copy(source.at[:, 128 * j : 128 * (j + 1)], target.at[j], sem)

    owners = [tile_copy(owner_in, owner, sems.at[0, j], j) for j in range(4)]
    fines = [
        [tile_copy(fine_in.at[f], fine.at[f], sems.at[1 + f, j], j) for j in range(4)]
        for f in range(F)
    ]
    late = [
        pltpu.make_async_copy(flags_in, flags, sems.at[F + 1, 0]),
        pltpu.make_async_copy(coef_in, coef, sems.at[F + 1, 1]),
        pltpu.make_async_copy(jac_in, jac, sems.at[F + 1, 2]),
    ]
    for copy in owners + sum(fines, []) + late:
        copy.start()
    for copy in owners:
        copy.wait()

    def halves(load):
        return [
            jnp.concatenate([load(j, pl.ds(start, TX, 2)) for j in range(4)], axis=1)
            for start in (0, 1)
        ]

    shape = (TX, 2 * TY)
    row = iota(shape, 0)
    col = iota(shape, 1) >> 1
    codes = [
        ((o >> 8) - row + 1) * 3 + (o & (TY - 1)) - col + 1
        for o in halves(lambda j, rows: owner[j, rows, :])
    ]
    masks = [[code == k for code in codes] for k in range(9)]
    gathered = []
    for f in range(F):
        for copy in fines[f]:
            copy.wait()
        values = halves(lambda j, rows: fine[f, j, rows, :])
        total = None
        for dy in (-1, 0, 1):
            part = None
            for dx in (-1, 0, 1):
                mask = masks[(dx + 1) * 3 + dy + 1]
                moved = jnp.where(mask[0], values[0], 0.0) + jnp.where(mask[1], values[1], 0.0)
                moved = roll(moved, dx, 0)
                part = moved if part is None else part + moved
            part = roll(part, 2 * dy, 1)
            total = part if total is None else total + part
        gathered.append(total)
    pairs = ((iota((2 * TY, TY), 0) >> 1) == iota((2 * TY, TY), 1)).astype(F32)
    gathered.append(jnp.zeros((8, 2 * TY), F32))
    for copy in late:
        copy.wait()
    summed = select_columns(jnp.concatenate(gathered, axis=0), pairs)
    planes = [summed[TX * f : TX * (f + 1)] for f in range(F)]
    for f in range(F):
        rhs[f] = planes[f]
    planes.append((flags[...] + 1).astype(F32))

    odd = parity("gy")
    slot = iota((TX, 128), 1) >> 3
    for a in range(2):
        first = jnp.zeros((TX, 128), F32)
        last = jnp.zeros((TX, 128), F32)
        for t in range(16):
            p = 16 * a + t
            if p >= PLANES:
                continue
            if p < F * F:
                head, tail = jac[p // F, p % F, :, 0:128], jac[p // F, p % F, :, TY - 128 : TY]
            else:
                head, tail = planes[p - F * F][:, 0:128], planes[p - F * F][:, TY - 128 : TY]
            first = jnp.where(slot == t, roll(head, 8 * t, 1), first)
            last = jnp.where(slot == t, roll(tail, 8 * t - 120, 1), last)
        near[a] = jnp.where(odd, first, last)
        far[a] = jnp.where(odd, last, first)
    lane = iota((ROWS, 128), 1)
    first, last = near[1, 0:ROWS, :], far[1, 0:ROWS, :]
    for f in range(F):
        wide = jnp.concatenate([coef[f], coef[f]], axis=1)
        head, tail = roll(wide, 120 + f, 1), roll(wide, 120 + f - 63, 1)
        first = jnp.where(lane == 120 + f, jnp.where(odd, head, tail), first)
        last = jnp.where(lane == 120 + f, jnp.where(odd, tail, head), last)
    near[1, 0:ROWS, :] = first
    far[1, 0:ROWS, :] = last


RHS_AT, STATE_AT, CODE_AT, CORNER_AT, LINE_AT, ROWS_SENT = 50, 60, 65, 68, 74, 80


def rows_kernel(jac, rhs, flags, near, far):
    def write(out, first):
        start = 0 if first else TX - 2
        wide = 0 if first else TX - 3
        third = 2 if first else TX - 3
        for p in range(F * F):
            out[2 * p : 2 * p + 2] = jac[p // F, p % F, start : start + 2, :]
        kinds = flags[third : third + 1, :]
        interior, wall = kinds == 0, kinds == 2
        for f in range(F):
            at = RHS_AT + 2 * f
            out[at : at + 2] = rhs[f, start : start + 2, :]
            kept = interior if f in (1, 2) else interior | wall
            scaled = jnp.where(kept, 0.8 / jac[f, f, third : third + 1, :], 0.0)
            out[STATE_AT + f : STATE_AT + f + 1] = scaled * rhs[f, third : third + 1, :]
        out[CODE_AT : CODE_AT + 3] = (flags[wide : wide + 3, :] + 1).astype(F32)
        out[CORNER_AT:ROWS_SENT] = jnp.zeros((ROWS_SENT - CORNER_AT, TY), F32)

    odd = parity("gx")

    @pl.when(odd)
    def _():
        write(near, True)
        write(far, False)

    @pl.when(jnp.logical_not(odd))
    def _():
        write(near, False)
        write(far, True)


def corners_kernel(near_rows, far_rows, coef, near_y, far_y, near, far, low, high, turn, diag):
    odd = parity("gx")
    near[...] = near_rows[...]
    far[...] = far_rows[...]
    for side, strip in enumerate((far_y, near_y)):
        at = CORNER_AT + 3 * side
        for a in range(2):
            lanes = slice(128 * a, 128 * (a + 1))
            first, last = strip[a, 0:3, :], strip[a, TX - 3 : TX, :]
            near[at : at + 3, lanes] = jnp.where(odd, first, last)
            far[at : at + 3, lanes] = jnp.where(odd, last, first)

    lane = iota((ROWS, 128), 1)
    odd_y = parity("gy")
    right = jnp.where(odd_y, far_y[1, 0:ROWS, :], near_y[1, 0:ROWS, :])
    left = jnp.where(odd_y, near_y[1, 0:ROWS, :], far_y[1, 0:ROWS, :])
    diag[...] = jnp.full((8 * ROWS, 128), 4.0, F32)
    for f in range(F):
        wide = jnp.concatenate([coef[f], coef[f]], axis=1)
        wide = jnp.where(lane == 64, roll(right, 64 - 120 - f, 1), wide)
        wide = jnp.where(lane == 65, roll(left, 65 - 120 - f, 1), wide)
        wide = jnp.where((lane <= 65) & (wide > 0.0), wide, 4.0)
        for k in range(ROWS):
            diag[8 * k + f : 8 * k + f + 1, :] = wide[k : k + 1, :]
    lows, highs = [], []
    for k in range(ROWS):
        d = diag[8 * k : 8 * k + 8, :]
        inverse = 1.0 / (d - highs[-1] if k else d)
        lows.append(lows[-1] * inverse if k else inverse)
        highs.append(inverse)
        low[8 * k : 8 * k + 8] = lows[k]
        high[8 * k : 8 * k + 8] = highs[k]
    first_low = lows[-1]
    for k in range(ROWS - 2, -1, -1):
        first_low = lows[k] + highs[k] * first_low
    turn[...] = first_low
    lane = iota((8, 128), 1)
    ends = highs[-1]
    for q, part in enumerate((first_low, lows[-1], highs[-1])):
        ends = jnp.where(lane >> 1 == 33 + q, roll(part, 2 * (q + 1), 1), ends)
    near[LINE_AT : LINE_AT + F, 0:128] = jnp.where(lane < 64, first_low, roll(lows[-1], 64, 1))[0:F]
    near[LINE_AT : LINE_AT + F, 128:TY] = ends[0:F]


def unpack(near, far, p):
    odd = parity("gy")
    right = jnp.where(odd, far, near)
    left = jnp.where(odd, near, far)
    lane = iota(near.shape, 1)
    return jnp.where(
        lane < 8,
        roll(right, -8 * (p % 16), 1),
        jnp.where(lane >= 120, roll(left, 120 - 8 * (p % 16), 1), 0.0),
    )


def scale(code, jac, scaled):
    plain = (code == 1.0) | (code == 3.0)
    interior = code == 1.0
    for f in range(F):
        kept = interior if f in (1, 2) else plain
        scaled[f] = jnp.where(kept, 0.8 / jac[F * f + f], 0.0)


def own_kernel(
    jac_in, rhs_in, flags, near_y, far_y, jac, rhs, scaled
):
    near, far = [near_y[0], near_y[1]], [far_y[0], far_y[1]]
    for p in range(F * F):
        jac[p, :, 0:TY] = jac_in[p // F, p % F]
        jac[p, :, TY:EY] = unpack(near[p // 16], far[p // 16], p)
    for f in range(F):
        rhs[f, :, 0:TY] = rhs_in[f]
        rhs[f, :, TY:EY] = unpack(near[1], far[1], F * F + f)
    aside = unpack(near[1], far[1], F * F + F)
    code = jnp.concatenate([(flags[...] + 1).astype(F32), aside], axis=1)
    scale(code, jac, scaled)


def residual(f, state, rhs, jac):
    own = state[f]
    beside = roll(own, 1, 0) + roll(own, -1, 0) + roll(own, 1, 1) + roll(own, -1, 1)
    total = rhs(f) + beside
    for g in range(F):
        total = total - jac(F * f + g) * state[g]
    return total


def sweep(old, new, scaled, rhs, jac):
    for f in range(F):
        new[f] = old[f] + scaled(f) * residual(f, old, rhs, jac)


def planes_of(own, beyond):
    return lambda p: jnp.concatenate([own[p], beyond[p]], axis=0)


def columns(shape, fine_dim, coarse_dim):
    fine = iota(shape, fine_dim)
    coarse = iota(shape, coarse_dim)
    here = (coarse <= 64) & (fine >> 2 == coarse)
    return (here | ((coarse == 65) & (fine >= EY - 4))).astype(F32)


def before_kernel(
    jac_own, rhs_own, scaled_own, low, high, turn, far_x, near_x,
    state, jac, rhs, scaled, value, chip, near_state, far_state, sent, other, sides, beside, means, block, sems,
):
    odd = parity("gx")
    sides[0] = jnp.where(odd, near_x[...], far_x[...])
    sides[1] = jnp.where(odd, far_x[...], near_x[...])
    none = jnp.zeros((8, TY), F32)

    def put(out, at, rows):
        out[8 - rows : 8, 0:TY] = sides[0, at : at + rows]
        out[0:rows, 0:TY] = sides[1, at : at + rows]

    for side in range(2):
        at = CORNER_AT + 3 * side
        for a in range(2):
            lanes = slice(128 * a, 128 * (a + 1))
            beside[side, a] = jnp.zeros((8, 128), F32)
            beside[side, a, 5:8] = sides[0, at : at + 3, lanes]
            beside[side, a, 0:3] = sides[1, at : at + 3, lanes]
    far, near = [[beside[side, a] for a in range(2)] for side in range(2)]
    for p in range(F * F):
        jac[p, :, 0:TY] = none
        put(jac.at[p], 2 * p, 2)
        if p % (F + 1) == 0:
            jac[p, 5:6, 0:TY] = jnp.ones((1, TY), F32)
            jac[p, 2:3, 0:TY] = jnp.ones((1, TY), F32)
        jac[p, :, TY:EY] = unpack(near[p // 16], far[p // 16], p)
    for f in range(F):
        rhs[f, :, 0:TY] = none
        put(rhs.at[f], RHS_AT + 2 * f, 2)
        rhs[f, :, TY:EY] = unpack(near[1], far[1], F * F + f)
    code = scaled.at[F - 1]
    code[:, 0:TY] = none
    put(code, CODE_AT, 3)
    code[:, TY:EY] = unpack(near[1], far[1], F * F + F)
    scale(code[...], jac, scaled)

    jac_plane, rhs_plane = planes_of(jac_own, jac), planes_of(rhs_own, rhs)
    scaled_plane = planes_of(scaled_own, scaled)
    for f in range(F):
        state[f] = scaled_plane(f) * rhs_plane(f)
        state[f, TX + 5 : TX + 6, 0:TY] = sides[0, STATE_AT + f : STATE_AT + f + 1]
        state[f, TX + 2 : TX + 3, 0:TY] = sides[1, STATE_AT + f : STATE_AT + f + 1]
    sweep(state, other, scaled_plane, rhs_plane, jac_plane)
    sweep(other, state, scaled_plane, rhs_plane, jac_plane)
    means[...] = jnp.zeros((8 * ROWS, EY), F32)
    for f in range(F):
        left_over = residual(f, state, rhs_plane, jac_plane)[0:TX]
        left_over = left_over + roll(left_over, -1, 0)
        left_over = left_over + roll(left_over, -2, 0)
        for k in range(ROWS):
            means[8 * k + f : 8 * k + f + 1, :] = left_over[4 * k : 4 * k + 1]
    mean = select_columns(means[...] * 0.0625, columns((EY, 128), 0, 1))
    values = []
    for k in range(ROWS):
        rows = slice(8 * k, 8 * k + 8)
        here = mean[rows] + values[-1] if k else mean[rows]
        values.append(here * high[rows, :])
        value[rows] = values[k]
    first, last = values[-1], values[-1]
    for k in range(ROWS - 2, -1, -1):
        first = values[k] + high[8 * k : 8 * k + 8, :] * first
    lane = iota((8, 128), 1)

    packed = [near_x[ROWS_SENT - 8 :, 128 * a : 128 * (a + 1)] for a in range(2)]
    packed = [roll(part, ROWS_SENT - 8 - LINE_AT, 0) for part in packed]
    theirs = [packed[0], roll(packed[0], 64, 1), packed[1]]
    theirs = [jnp.where(lane < 64, theirs[q], roll(packed[1], -2 * (q + 1), 1)) for q in range(3)]
    own = [turn[...], low[8 * ROWS - 8 :, :], high[8 * ROWS - 8 :, :]]
    b0, c, c1 = [jnp.where(odd, theirs[q], own[q]) for q in range(3)]
    e0, g, g1 = [jnp.where(odd, own[q], theirs[q]) for q in range(3)]
    w = 1.0 / (1.0 - c1 * e0)
    cw, gw = c * w, g * w
    x0 = jnp.where(odd, cw * first, first + cw * e0 * last)
    x1 = jnp.where(odd, last + gw * c1 * first, gw * last)
    chip[0] = w
    chip[1] = jnp.where(odd, gw, cw)
    chip[2] = jnp.where(odd, first, last)
    chip[3] = jnp.where(odd, c1, e0)
    chip[4] = c
    chip[5] = g
    whole_b0, whole_c, whole_c1 = b0 + c * cw * e0, cw * g, g1 + g * gw * c1
    middle = roll(whole_c, 64, 1)
    pair = lane >> 1
    even_part = jnp.where(lane < 64, whole_b0, middle)
    for q, part in enumerate((x0, x1, whole_b0, whole_c, whole_c1)):
        even_part = jnp.where(pair == 48 + q, roll(part, 32 + 2 * q, 1), even_part)
    odd_part = jnp.where(lane < 64, whole_c1, middle)
    odd_part = jnp.where(pair == 32, x0, jnp.where(pair == 33, roll(x1, 2, 1), odd_part))
    main = jnp.where(lane < 64, x0, roll(x1, 64, 1))
    rest = jnp.where(odd, odd_part, even_part)
    each = block.shape[0]
    for f in range(F):
        both = jnp.concatenate([main[f : f + 1], rest[f : f + 1]], axis=0)
        for k in range(each):
            block[k, f] = both
    copies = [
        pltpu.make_async_copy(block, sent.at[k * each : (k + 1) * each], sems.at[k])
        for k in range(sent.shape[0] // each)
    ]
    for copy in copies:
        copy.start()
    for f in range(F):
        for j in range(EY // 128):
            lanes = slice(128 * j, 128 * (j + 1))
            first, last = state[f, 1:3, lanes], state[f, TX - 3 : TX - 1, lanes]
            near_state[f, j] = jnp.where(odd, first, last)
            far_state[f, j] = jnp.where(odd, last, first)
    for copy in copies:
        copy.wait()


def merge(one, two):
    a0, a1, b0, c, c1 = one
    d0, d1, e0, g, g1 = two
    w = 1.0 / (1.0 - c1 * e0)
    cw, gw = c * w, g * w
    return (
        a0 + cw * (d0 + e0 * a1),
        d1 + gw * (a1 + c1 * d0),
        b0 + c * cw * e0,
        cw * g,
        g1 + g * gw * c1,
    )


def between(one, two, below, above):
    a0, a1, b0, c, c1 = one
    d0, d1, e0, g, g1 = two
    outer = d0 + g * above
    last = (a1 + c * below + c1 * outer) / (1.0 - c1 * e0)
    return last, outer + e0 * last


def after_kernel(
    jac_own, rhs_own, scaled_own, low, high, jac_beyond, rhs_beyond, scaled_beyond, state_in, value, chip, far_state, near_state, got,
    correction_out, level_residual_out,
    state, other, ends, spread, tree, correction, level_residual, sems,
):
    count = got.shape[0]
    me = lax.axis_index("gx")
    lane = iota((F, 128), 1)

    odd = parity("gx")

    def stacked(k, part):
        return jnp.concatenate([got[k, f, part : part + 1, :] for f in range(F)], axis=0)

    def segment(k):
        main = stacked(2 * k, 0) + stacked(2 * k + 1, 0)
        even, other_core = stacked(2 * k, 1), stacked(2 * k + 1, 1)
        ends = roll(even, 64 - 96, 1)
        moving = ends + other_core
        middle = roll(jnp.where(lane < 96, even, other_core), 64, 1)
        inner = [main, roll(main, 64, 1), even, middle, other_core]
        outer = [moving, roll(moving, -2, 1)] + [roll(ends, -2 * q, 1) for q in (2, 3, 4)]
        return [jnp.where(lane < 64, inner[q], outer[q]) for q in range(5)]

    level, starts, total = [segment(k) for k in range(count // 2)], [], 0
    while True:
        starts.append(total)
        for parts in level:
            for q in range(5):
                tree[total, q, 0:F] = parts[q]
            total += 1
        if len(level) <= 2:
            break
        level = [merge(level[2 * k], level[2 * k + 1]) for k in range(len(level) // 2)]
    below = above = jnp.zeros((F, 128), F32)
    my_chip = me >> 1
    if count > 2:
        for size in range(len(starts) - 1, -1, -1):
            at = starts[size] + 2 * (my_chip >> (size + 1))
            one = [tree[at, q, 0:F] for q in range(5)]
            two = [tree[at + 1, q, 0:F] for q in range(5)]
            last, first = between(one, two, below, above)
            second = (my_chip >> size) & 1 == 1
            below, above = jnp.where(second, last, below), jnp.where(second, above, first)
    partner = me + 1 - 2 * (me & 1)
    main, rest = stacked(partner, 0), stacked(partner, 1)
    from_even = jnp.where(lane < 64, roll(main, 64, 1), roll(rest, 64 - 98, 1))
    from_odd = jnp.where(lane < 64, main, rest)
    w, share, own, turn, c, g = [chip[q, 0:F, :] for q in range(6)]
    theirs = jnp.where(odd, from_even, from_odd) / share
    lower, upper = c * below, g * above
    inside = jnp.where(odd, lower, upper) + theirs
    inside = w * (inside + turn * (own + jnp.where(odd, upper, lower)))
    below, above = jnp.where(odd, inside, below), jnp.where(odd, above, inside)

    used = lane <= 65
    ends[...] = jnp.zeros((64, 128), F32)
    ends[0:F] = jnp.where(used, below, 0.0)
    ends[8 * (ROWS + 1) : 8 * (ROWS + 1) + F] = jnp.where(used, above, 0.0)
    here = above
    for k in range(ROWS - 1, -1, -1):
        rows = slice(8 * k, 8 * k + F)
        here = value[rows] + low[rows] * below + high[rows] * here
        ends[8 * (k + 1) : 8 * (k + 1) + F] = jnp.where(used, here, 0.0)
    spread[...] = select_columns(ends[...], columns((128, EY), 1, 0))

    jac_plane, rhs_plane = planes_of(jac_own, jac_beyond), planes_of(rhs_own, rhs_beyond)
    scaled_plane = planes_of(scaled_own, scaled_beyond)
    upper = iota((8, EY), 0) < 4

    def repeated(row):
        return jnp.broadcast_to(spread[row : row + 1, :], (8, EY))

    for f in range(F):
        tiles = []
        for v in range(EX // 8):
            groups = (2 * v + 1, (2 * v + 2) % 8)
            one, two = [repeated(8 * group + f) for group in groups]
            tiles.append(jnp.where(upper, one, two))
        added = jnp.where(scaled_plane(f) != 0.0, jnp.concatenate(tiles, axis=0), 0.0)
        other[f] = state_in[f]
        for j in range(EY // 128):
            lanes = slice(128 * j, 128 * (j + 1))
            far, near = far_state[f, j], near_state[f, j]
            other[f, EX - 3 : EX - 1, lanes] = jnp.where(odd, near, far)
            other[f, TX + 1 : TX + 3, lanes] = jnp.where(odd, far, near)
        state[f] = other[f] + added
    sweep(state, other, scaled_plane, rhs_plane, jac_plane)
    sweep(other, state, scaled_plane, rhs_plane, jac_plane)
    copies = []
    for f in range(F):
        correction[f] = state[f, 0:TX, 0:TY]
        copies.append(
            pltpu.make_async_copy(correction.at[f], correction_out.at[f], sems.at[0, f])
        )
        copies[-1].start()
    for f in range(F):
        level_residual[f] = residual(f, state, rhs_plane, jac_plane)[0:TX, 0:TY]
        copies.append(
            pltpu.make_async_copy(level_residual.at[f], level_residual_out.at[f], sems.at[1, f])
        )
        copies[-1].start()
    for copy in copies:
        copy.wait()


def shape_of(*dims):
    return jax.ShapeDtypeStruct(dims, F32)


def call(kernel, outs, scratch, *args, space=pltpu.VMEM, out_space=None):
    return pl.pallas_call(
        kernel,
        out_shape=outs,
        in_specs=[pl.BlockSpec(memory_space=space)] * len(args),
        out_specs=[pl.BlockSpec(memory_space=o) for o in out_space or [pltpu.VMEM] * len(outs)],
        scratch_shapes=scratch,
        compiler_params=pltpu.CompilerParams(vmem_limit_bytes=32 * 1024 * 1024),
    )(*args)


def swap(value, axis, start):
    count = lax.axis_size(axis)
    firsts = range(start, count - 1, 2)
    return lax.ppermute(value, axis, [(i, i + 1) for i in firsts] + [(i + 1, i) for i in firsts])


def local(fine, owner, flags, jac, coef):
    strip = shape_of(2, TX, 128)
    rhs, near, far = call(
        restrict_kernel,
        [shape_of(F, TX, TY), strip, strip],
        [
            pltpu.VMEM((F, 4, 2 * TX, 128), F32),
            pltpu.VMEM((4, 2 * TX, 128), jnp.int32),
            pltpu.VMEM((TX, TY), jnp.int32),
            pltpu.VMEM((F, F, TX, TY), F32),
            pltpu.VMEM((F, ROWS, TY // 4), F32),
            pltpu.SemaphoreType.DMA((F + 2, 4)),
        ],
        *[pltpu.with_memory_space_constraint(x, pltpu.HBM) for x in (fine, owner, flags, jac, coef)],
        space=pltpu.HBM,
    )
    near_rows, far_rows = call(
        rows_kernel, [shape_of(ROWS_SENT, TY), shape_of(ROWS_SENT, TY)], [], jac, rhs, flags
    )
    far_y = swap(far, "gy", 1)
    near_y = swap(near, "gy", 0)
    rows, lines, line = shape_of(ROWS_SENT, TY), shape_of(8 * ROWS, 128), shape_of(8, 128)
    near_rows, far_rows, low, high, turn = call(
        corners_kernel,
        [rows, rows, lines, lines, line],
        [pltpu.VMEM((8 * ROWS, 128), F32)],
        near_rows, far_rows, coef, near_y, far_y,
    )
    far_x = swap(far_rows, "gx", 1)
    near_x = swap(near_rows, "gx", 0)
    count = lax.axis_size("gx")
    own = shape_of(F, TX, EY)
    jac_own, rhs_own, scaled_own = call(
        own_kernel, [shape_of(F * F, TX, EY), own, own], [], jac, rhs, flags, near_y, far_y
    )
    tile = pltpu.VMEM((F, EX, EY), F32)
    beyond = shape_of(F, 8, EY)
    ends = shape_of(F, EY // 128, 2, 128)
    state, jac_beyond, rhs_beyond, scaled_beyond, value, chip, near_state, far_state, sent = call(
        before_kernel,
        [
            shape_of(F, EX, EY), shape_of(F * F, 8, EY), beyond, beyond, lines, shape_of(6, 8, 128), ends, ends,
            shape_of(count, F, 2, 128),
        ],
        [
            tile,
            pltpu.VMEM((2, ROWS_SENT, TY), F32),
            pltpu.VMEM((2, 2, 8, 128), F32),
            pltpu.VMEM((8 * ROWS, EY), F32),
            pltpu.VMEM((min(count, 8), F, 2, 128), F32),
            pltpu.SemaphoreType.DMA((count,)),
        ],
        jac_own, rhs_own, scaled_own, low, high, turn, far_x, near_x,
        out_space=[pltpu.VMEM] * 8 + [pl.ANY],
    )
    got = lax.all_to_all(sent, "gx", 0, 0, tiled=True)
    far_state = swap(far_state, "gx", 1)
    near_state = swap(near_state, "gx", 0)
    return tuple(
        call(
            after_kernel,
            [shape_of(F, TX, TY), shape_of(F, TX, TY)],
            [
                tile,
                tile,
                pltpu.VMEM((64, 128), F32),
                pltpu.VMEM((64, EY), F32),
                pltpu.VMEM((count, 5, 8, 128), F32),
                pltpu.VMEM((F, TX, TY), F32),
                pltpu.VMEM((F, TX, TY), F32),
                pltpu.SemaphoreType.DMA((2, F)),
            ],
            jac_own, rhs_own, scaled_own, low, high, jac_beyond, rhs_beyond, scaled_beyond, state, value, chip,
            far_state, near_state, got,
            out_space=[pl.ANY] * 2,
        )
    )


def solution(mesh):
    in_specs = (
        P(None, "gx", "gy"),
        P("gx", "gy"),
        P("gx", "gy"),
        P(None, None, "gx", "gy"),
        P(None, "gx", "gy"),
    )
    out_specs = (P(None, "gx", "gy"), P(None, "gx", "gy"))
    return jax.shard_map(local, mesh=mesh, in_specs=in_specs, out_specs=out_specs, check_vma=False)
```

```python
import jax
import jax.numpy as jnp
from jax import lax
from jax.experimental import pallas as pl
from jax.experimental.pallas import tpu as pltpu
from jax.sharding import PartitionSpec as P

F = 5
TX = 24
TY = 256
EX = 32
EY = 384
ROWS = 6
PLANES = 31
F32 = jnp.float32


def iota(shape, dim):
    return lax.broadcasted_iota(jnp.int32, shape, dim)


def parts_of(x):
    head = x.astype(jnp.bfloat16)
    rest = x - head.astype(F32)
    middle = rest.astype(jnp.bfloat16)
    return head, middle, (rest - middle.astype(F32)).astype(jnp.bfloat16)


def select_columns(x, chosen):
    rows = x.shape[0]
    whole = jnp.concatenate(parts_of(x), axis=0)
    out = jnp.dot(whole, chosen.astype(jnp.bfloat16), preferred_element_type=F32)
    return out[0:rows] + out[rows : 2 * rows] + out[2 * rows :]


def roll(x, shift, axis):
    shift = shift % x.shape[axis]
    return x if shift == 0 else pltpu.roll(x, shift, axis)


def parity(axis):
    return lax.rem(lax.axis_index(axis), 2) == 1


def restrict_kernel(
    fine_in, owner_in, flags_in, jac_in, coef_in, rhs, near, far,
    fine, owner, flags, jac, coef, sems,
):
    def tile_copy(source, target, sem, j):
        return pltpu.make_async_copy(source.at[:, 128 * j : 128 * (j + 1)], target.at[j], sem)

    owners = [tile_copy(owner_in, owner, sems.at[0, j], j) for j in range(4)]
    fines = [
        [tile_copy(fine_in.at[f], fine.at[f], sems.at[1 + f, j], j) for j in range(4)]
        for f in range(F)
    ]
    late = [
        pltpu.make_async_copy(flags_in, flags, sems.at[F + 1, 0]),
        pltpu.make_async_copy(coef_in, coef, sems.at[F + 1, 1]),
        pltpu.make_async_copy(jac_in, jac, sems.at[F + 1, 2]),
    ]
    for copy in owners + sum(fines, []) + late:
        copy.start()
    for copy in owners:
        copy.wait()

    def halves(load):
        return [
            jnp.concatenate([load(j, pl.ds(start, TX, 2)) for j in range(4)], axis=1)
            for start in (0, 1)
        ]

    shape = (TX, 2 * TY)
    row = iota(shape, 0)
    col = iota(shape, 1) >> 1
    codes = [
        ((o >> 8) - row + 1) * 3 + (o & (TY - 1)) - col + 1
        for o in halves(lambda j, rows: owner[j, rows, :])
    ]
    masks = [[code == k for code in codes] for k in range(9)]
    gathered = []
    for f in range(F):
        for copy in fines[f]:
            copy.wait()
        values = halves(lambda j, rows: fine[f, j, rows, :])
        total = None
        for dy in (-1, 0, 1):
            part = None
            for dx in (-1, 0, 1):
                mask = masks[(dx + 1) * 3 + dy + 1]
                moved = jnp.where(mask[0], values[0], 0.0) + jnp.where(mask[1], values[1], 0.0)
                moved = roll(moved, dx, 0)
                part = moved if part is None else part + moved
            part = roll(part, 2 * dy, 1)
            total = part if total is None else total + part
        gathered.append(total)
    pairs = ((iota((2 * TY, TY), 0) >> 1) == iota((2 * TY, TY), 1)).astype(F32)
    gathered.append(jnp.zeros((8, 2 * TY), F32))
    for copy in late:
        copy.wait()
    summed = select_columns(jnp.concatenate(gathered, axis=0), pairs)
    planes = [summed[TX * f : TX * (f + 1)] for f in range(F)]
    for f in range(F):
        rhs[f] = planes[f]
    planes.append((flags[...] + 1).astype(F32))

    odd = parity("gy")
    slot = iota((TX, 128), 1) >> 3
    for a in range(2):
        first = jnp.zeros((TX, 128), F32)
        last = jnp.zeros((TX, 128), F32)
        for t in range(16):
            p = 16 * a + t
            if p >= PLANES:
                continue
            if p < F * F:
                head, tail = jac[p // F, p % F, :, 0:128], jac[p // F, p % F, :, TY - 128 : TY]
            else:
                head, tail = planes[p - F * F][:, 0:128], planes[p - F * F][:, TY - 128 : TY]
            first = jnp.where(slot == t, roll(head, 8 * t, 1), first)
            last = jnp.where(slot == t, roll(tail, 8 * t - 120, 1), last)
        near[a] = jnp.where(odd, first, last)
        far[a] = jnp.where(odd, last, first)
    lane = iota((ROWS, 128), 1)
    first, last = near[1, 0:ROWS, :], far[1, 0:ROWS, :]
    for f in range(F):
        wide = jnp.concatenate([coef[f], coef[f]], axis=1)
        head, tail = roll(wide, 120 + f, 1), roll(wide, 120 + f - 63, 1)
        first = jnp.where(lane == 120 + f, jnp.where(odd, head, tail), first)
        last = jnp.where(lane == 120 + f, jnp.where(odd, tail, head), last)
    near[1, 0:ROWS, :] = first
    far[1, 0:ROWS, :] = last


RHS_AT, STATE_AT, CODE_AT, CORNER_AT, LINE_AT, ROWS_SENT = 50, 60, 65, 68, 74, 80


def rows_kernel(jac, rhs, flags, near, far):
    def write(out, first):
        start = 0 if first else TX - 2
        wide = 0 if first else TX - 3
        third = 2 if first else TX - 3
        for p in range(F * F):
            out[2 * p : 2 * p + 2] = jac[p // F, p % F, start : start + 2, :]
        kinds = flags[third : third + 1, :]
        interior, wall = kinds == 0, kinds == 2
        for f in range(F):
            at = RHS_AT + 2 * f
            out[at : at + 2] = rhs[f, start : start + 2, :]
            kept = interior if f in (1, 2) else interior | wall
            scaled = jnp.where(kept, 0.8 / jac[f, f, third : third + 1, :], 0.0)
            out[STATE_AT + f : STATE_AT + f + 1] = scaled * rhs[f, third : third + 1, :]
        out[CODE_AT : CODE_AT + 3] = (flags[wide : wide + 3, :] + 1).astype(F32)
        out[CORNER_AT:ROWS_SENT] = jnp.zeros((ROWS_SENT - CORNER_AT, TY), F32)

    odd = parity("gx")

    @pl.when(odd)
    def _():
        write(near, True)
        write(far, False)

    @pl.when(jnp.logical_not(odd))
    def _():
        write(near, False)
        write(far, True)


def corners_kernel(near_rows, far_rows, coef, near_y, far_y, near, far, low, high, turn, diag):
    odd = parity("gx")
    near[...] = near_rows[...]
    far[...] = far_rows[...]
    for side, strip in enumerate((far_y, near_y)):
        at = CORNER_AT + 3 * side
        for a in range(2):
            lanes = slice(128 * a, 128 * (a + 1))
            first, last = strip[a, 0:3, :], strip[a, TX - 3 : TX, :]
            near[at : at + 3, lanes] = jnp.where(odd, first, last)
            far[at : at + 3, lanes] = jnp.where(odd, last, first)

    lane = iota((ROWS, 128), 1)
    odd_y = parity("gy")
    right = jnp.where(odd_y, far_y[1, 0:ROWS, :], near_y[1, 0:ROWS, :])
    left = jnp.where(odd_y, near_y[1, 0:ROWS, :], far_y[1, 0:ROWS, :])
    diag[...] = jnp.full((8 * ROWS, 128), 4.0, F32)
    for f in range(F):
        wide = jnp.concatenate([coef[f], coef[f]], axis=1)
        wide = jnp.where(lane == 64, roll(right, 64 - 120 - f, 1), wide)
        wide = jnp.where(lane == 65, roll(left, 65 - 120 - f, 1), wide)
        wide = jnp.where((lane <= 65) & (wide > 0.0), wide, 4.0)
        for k in range(ROWS):
            diag[8 * k + f : 8 * k + f + 1, :] = wide[k : k + 1, :]
    lows, highs = [], []
    for k in range(ROWS):
        d = diag[8 * k : 8 * k + 8, :]
        inverse = 1.0 / (d - highs[-1] if k else d)
        lows.append(lows[-1] * inverse if k else inverse)
        highs.append(inverse)
        low[8 * k : 8 * k + 8] = lows[k]
        high[8 * k : 8 * k + 8] = highs[k]
    first_low = lows[-1]
    for k in range(ROWS - 2, -1, -1):
        first_low = lows[k] + highs[k] * first_low
    turn[...] = first_low
    lane = iota((8, 128), 1)
    ends = highs[-1]
    for q, part in enumerate((first_low, lows[-1], highs[-1])):
        ends = jnp.where(lane >> 1 == 33 + q, roll(part, 2 * (q + 1), 1), ends)
    near[LINE_AT : LINE_AT + F, 0:128] = jnp.where(lane < 64, first_low, roll(lows[-1], 64, 1))[0:F]
    near[LINE_AT : LINE_AT + F, 128:TY] = ends[0:F]


def unpack(near, far, p):
    odd = parity("gy")
    right = jnp.where(odd, far, near)
    left = jnp.where(odd, near, far)
    lane = iota(near.shape, 1)
    return jnp.where(
        lane < 8,
        roll(right, -8 * (p % 16), 1),
        jnp.where(lane >= 120, roll(left, 120 - 8 * (p % 16), 1), 0.0),
    )


def scale(code, jac, scaled):
    plain = (code == 1.0) | (code == 3.0)
    interior = code == 1.0
    for f in range(F):
        kept = interior if f in (1, 2) else plain
        scaled[f] = jnp.where(kept, 0.8 / jac[F * f + f], 0.0)


def own_kernel(
    jac_in, rhs_in, flags, near_y, far_y, jac, rhs, scaled, first, second
):
    near, far = [near_y[0], near_y[1]], [far_y[0], far_y[1]]
    for p in range(F * F):
        jac[p, :, 0:TY] = jac_in[p // F, p % F]
        jac[p, :, TY:EY] = unpack(near[p // 16], far[p // 16], p)
    for f in range(F):
        rhs[f, :, 0:TY] = rhs_in[f]
        rhs[f, :, TY:EY] = unpack(near[1], far[1], F * F + f)
    aside = unpack(near[1], far[1], F * F + F)
    code = jnp.concatenate([(flags[...] + 1).astype(F32), aside], axis=1)
    scale(code, jac, scaled)

    for f in range(F):
        first[f] = scaled[f] * rhs[f]
    row = iota((TX, EY), 0)
    for f in range(F):
        own = first[f]
        above = jnp.where(row == 0, 0.0, roll(own, 1, 0))
        below = jnp.where(row == TX - 1, 0.0, roll(own, -1, 0))
        total = rhs[f] + above + below + roll(own, 1, 1) + roll(own, -1, 1)
        for g in range(F):
            total = total - jac[F * f + g] * first[g]
        second[f] = own + scaled[f] * total


def residual(f, state, rhs, jac):
    own = state[f]
    beside = roll(own, 1, 0) + roll(own, -1, 0) + roll(own, 1, 1) + roll(own, -1, 1)
    total = rhs(f) + beside
    for g in range(F):
        total = total - jac(F * f + g) * state[g]
    return total


def sweep(old, new, scaled, rhs, jac):
    for f in range(F):
        new[f] = old[f] + scaled(f) * residual(f, old, rhs, jac)


def planes_of(own, beyond):
    return lambda p: jnp.concatenate([own[p], beyond[p]], axis=0)


def columns(shape, fine_dim, coarse_dim):
    fine = iota(shape, fine_dim)
    coarse = iota(shape, coarse_dim)
    here = (coarse <= 64) & (fine >> 2 == coarse)
    return (here | ((coarse == 65) & (fine >= EY - 4))).astype(F32)


def before_kernel(
    jac_own, rhs_own, scaled_own, first_own, second_own, low, high, turn, far_x, near_x,
    state, jac, rhs, scaled, value, chip, near_state, far_state, sent, other, sides, beside, means, block, sems,
):
    odd = parity("gx")
    sides[0] = jnp.where(odd, near_x[...], far_x[...])
    sides[1] = jnp.where(odd, far_x[...], near_x[...])
    none = jnp.zeros((8, TY), F32)

    def put(out, at, rows):
        out[8 - rows : 8, 0:TY] = sides[0, at : at + rows]
        out[0:rows, 0:TY] = sides[1, at : at + rows]

    for side in range(2):
        at = CORNER_AT + 3 * side
        for a in range(2):
            lanes = slice(128 * a, 128 * (a + 1))
            beside[side, a] = jnp.zeros((8, 128), F32)
            beside[side, a, 5:8] = sides[0, at : at + 3, lanes]
            beside[side, a, 0:3] = sides[1, at : at + 3, lanes]
    far, near = [[beside[side, a] for a in range(2)] for side in range(2)]
    for p in range(F * F):
        jac[p, :, 0:TY] = none
        put(jac.at[p], 2 * p, 2)
        if p % (F + 1) == 0:
            jac[p, 5:6, 0:TY] = jnp.ones((1, TY), F32)
            jac[p, 2:3, 0:TY] = jnp.ones((1, TY), F32)
        jac[p, :, TY:EY] = unpack(near[p // 16], far[p // 16], p)
    for f in range(F):
        rhs[f, :, 0:TY] = none
        put(rhs.at[f], RHS_AT + 2 * f, 2)
        rhs[f, :, TY:EY] = unpack(near[1], far[1], F * F + f)
    code = scaled.at[F - 1]
    code[:, 0:TY] = none
    put(code, CODE_AT, 3)
    code[:, TY:EY] = unpack(near[1], far[1], F * F + F)
    scale(code[...], jac, scaled)

    jac_plane, rhs_plane = planes_of(jac_own, jac), planes_of(rhs_own, rhs)
    scaled_plane = planes_of(scaled_own, scaled)
    for f in range(F):
        state[f, TX:EX] = scaled[f] * rhs[f]
        state[f, TX + 5 : TX + 6, 0:TY] = sides[0, STATE_AT + f : STATE_AT + f + 1]
        state[f, TX + 2 : TX + 3, 0:TY] = sides[1, STATE_AT + f : STATE_AT + f + 1]
    row = iota((8, EY), 0)
    for f in range(F):
        beyond = state[f, TX:EX]
        next_up, next_down = roll(beyond, 1, 0), roll(beyond, -1, 0)
        above = jnp.where(row == 0, first_own[f, TX - 1 : TX, :], next_up)
        below = jnp.where(row == 7, first_own[f, 0:1, :], next_down)
        total = rhs[f] + above + below + roll(beyond, 1, 1) + roll(beyond, -1, 1)
        for g in range(F):
            total = total - jac[F * f + g] * state[g, TX:EX]
        other[f, TX:EX] = beyond + scaled[f] * total
        other[f, 0:8] = second_own[f, 0:8, :] + jnp.where(
            row == 0, scaled_own[f, 0:8, :] * next_up, 0.0
        )
        other[f, 8:16] = second_own[f, 8:16, :]
        other[f, 16:TX] = second_own[f, 16:TX, :] + jnp.where(
            row == 7, scaled_own[f, 16:TX, :] * next_down, 0.0
        )
    sweep(other, state, scaled_plane, rhs_plane, jac_plane)
    means[...] = jnp.zeros((8 * ROWS, EY), F32)
    for f in range(F):
        left_over = residual(f, state, rhs_plane, jac_plane)[0:TX]
        left_over = left_over + roll(left_over, -1, 0)
        left_over = left_over + roll(left_over, -2, 0)
        for k in range(ROWS):
            means[8 * k + f : 8 * k + f + 1, :] = left_over[4 * k : 4 * k + 1]
    mean = select_columns(means[...] * 0.0625, columns((EY, 128), 0, 1))
    values = []
    for k in range(ROWS):
        rows = slice(8 * k, 8 * k + 8)
        here = mean[rows] + values[-1] if k else mean[rows]
        values.append(here * high[rows, :])
        value[rows] = values[k]
    first, last = values[-1], values[-1]
    for k in range(ROWS - 2, -1, -1):
        first = values[k] + high[8 * k : 8 * k + 8, :] * first
    lane = iota((8, 128), 1)

    packed = [near_x[ROWS_SENT - 8 :, 128 * a : 128 * (a + 1)] for a in range(2)]
    packed = [roll(part, ROWS_SENT - 8 - LINE_AT, 0) for part in packed]
    theirs = [packed[0], roll(packed[0], 64, 1), packed[1]]
    theirs = [jnp.where(lane < 64, theirs[q], roll(packed[1], -2 * (q + 1), 1)) for q in range(3)]
    own = [turn[...], low[8 * ROWS - 8 :, :], high[8 * ROWS - 8 :, :]]
    b0, c, c1 = [jnp.where(odd, theirs[q], own[q]) for q in range(3)]
    e0, g, g1 = [jnp.where(odd, own[q], theirs[q]) for q in range(3)]
    w = 1.0 / (1.0 - c1 * e0)
    cw, gw = c * w, g * w
    x0 = jnp.where(odd, cw * first, first + cw * e0 * last)
    x1 = jnp.where(odd, last + gw * c1 * first, gw * last)
    chip[0] = w
    chip[1] = jnp.where(odd, gw, cw)
    chip[2] = jnp.where(odd, first, last)
    chip[3] = jnp.where(odd, c1, e0)
    chip[4] = c
    chip[5] = g
    whole_b0, whole_c, whole_c1 = b0 + c * cw * e0, cw * g, g1 + g * gw * c1
    middle = roll(whole_c, 64, 1)
    pair = lane >> 1
    even_part = jnp.where(lane < 64, whole_b0, middle)
    for q, part in enumerate((x0, x1, whole_b0, whole_c, whole_c1)):
        even_part = jnp.where(pair == 48 + q, roll(part, 32 + 2 * q, 1), even_part)
    odd_part = jnp.where(lane < 64, whole_c1, middle)
    odd_part = jnp.where(pair == 32, x0, jnp.where(pair == 33, roll(x1, 2, 1), odd_part))
    main = jnp.where(lane < 64, x0, roll(x1, 64, 1))
    rest = jnp.where(odd, odd_part, even_part)
    each = block.shape[0]
    for f in range(F):
        both = jnp.concatenate([main[f : f + 1], rest[f : f + 1]], axis=0)
        for k in range(each):
            block[k, f] = both
    copies = [
        pltpu.make_async_copy(block, sent.at[k * each : (k + 1) * each], sems.at[k])
        for k in range(sent.shape[0] // each)
    ]
    for copy in copies:
        copy.start()
    for f in range(F):
        for j in range(EY // 128):
            lanes = slice(128 * j, 128 * (j + 1))
            first, last = state[f, 1:3, lanes], state[f, TX - 3 : TX - 1, lanes]
            near_state[f, j] = jnp.where(odd, first, last)
            far_state[f, j] = jnp.where(odd, last, first)
    for copy in copies:
        copy.wait()


def merge(one, two):
    a0, a1, b0, c, c1 = one
    d0, d1, e0, g, g1 = two
    w = 1.0 / (1.0 - c1 * e0)
    cw, gw = c * w, g * w
    return (
        a0 + cw * (d0 + e0 * a1),
        d1 + gw * (a1 + c1 * d0),
        b0 + c * cw * e0,
        cw * g,
        g1 + g * gw * c1,
    )


def between(one, two, below, above):
    a0, a1, b0, c, c1 = one
    d0, d1, e0, g, g1 = two
    outer = d0 + g * above
    last = (a1 + c * below + c1 * outer) / (1.0 - c1 * e0)
    return last, outer + e0 * last


def after_kernel(
    jac_own, rhs_own, scaled_own, low, high, jac_beyond, rhs_beyond, scaled_beyond, state_in, value, chip, far_state, near_state, got,
    correction_out, level_residual_out,
    state, other, ends, spread, tree, correction, level_residual, sems,
):
    count = got.shape[0]
    me = lax.axis_index("gx")
    lane = iota((F, 128), 1)

    odd = parity("gx")

    def stacked(k, part):
        return jnp.concatenate([got[k, f, part : part + 1, :] for f in range(F)], axis=0)

    def segment(k):
        main = stacked(2 * k, 0) + stacked(2 * k + 1, 0)
        even, other_core = stacked(2 * k, 1), stacked(2 * k + 1, 1)
        ends = roll(even, 64 - 96, 1)
        moving = ends + other_core
        middle = roll(jnp.where(lane < 96, even, other_core), 64, 1)
        inner = [main, roll(main, 64, 1), even, middle, other_core]
        outer = [moving, roll(moving, -2, 1)] + [roll(ends, -2 * q, 1) for q in (2, 3, 4)]
        return [jnp.where(lane < 64, inner[q], outer[q]) for q in range(5)]

    level, starts, total = [segment(k) for k in range(count // 2)], [], 0
    while True:
        starts.append(total)
        for parts in level:
            for q in range(5):
                tree[total, q, 0:F] = parts[q]
            total += 1
        if len(level) <= 2:
            break
        level = [merge(level[2 * k], level[2 * k + 1]) for k in range(len(level) // 2)]
    below = above = jnp.zeros((F, 128), F32)
    my_chip = me >> 1
    if count > 2:
        for size in range(len(starts) - 1, -1, -1):
            at = starts[size] + 2 * (my_chip >> (size + 1))
            one = [tree[at, q, 0:F] for q in range(5)]
            two = [tree[at + 1, q, 0:F] for q in range(5)]
            last, first = between(one, two, below, above)
            second = (my_chip >> size) & 1 == 1
            below, above = jnp.where(second, last, below), jnp.where(second, above, first)
    partner = me + 1 - 2 * (me & 1)
    main, rest = stacked(partner, 0), stacked(partner, 1)
    from_even = jnp.where(lane < 64, roll(main, 64, 1), roll(rest, 64 - 98, 1))
    from_odd = jnp.where(lane < 64, main, rest)
    w, share, own, turn, c, g = [chip[q, 0:F, :] for q in range(6)]
    theirs = jnp.where(odd, from_even, from_odd) / share
    lower, upper = c * below, g * above
    inside = jnp.where(odd, lower, upper) + theirs
    inside = w * (inside + turn * (own + jnp.where(odd, upper, lower)))
    below, above = jnp.where(odd, inside, below), jnp.where(odd, above, inside)

    used = lane <= 65
    ends[...] = jnp.zeros((64, 128), F32)
    ends[0:F] = jnp.where(used, below, 0.0)
    ends[8 * (ROWS + 1) : 8 * (ROWS + 1) + F] = jnp.where(used, above, 0.0)
    here = above
    for k in range(ROWS - 1, -1, -1):
        rows = slice(8 * k, 8 * k + F)
        here = value[rows] + low[rows] * below + high[rows] * here
        ends[8 * (k + 1) : 8 * (k + 1) + F] = jnp.where(used, here, 0.0)
    spread[...] = select_columns(ends[...], columns((128, EY), 1, 0))

    jac_plane, rhs_plane = planes_of(jac_own, jac_beyond), planes_of(rhs_own, rhs_beyond)
    scaled_plane = planes_of(scaled_own, scaled_beyond)
    upper = iota((8, EY), 0) < 4

    def repeated(row):
        return jnp.broadcast_to(spread[row : row + 1, :], (8, EY))

    for f in range(F):
        tiles = []
        for v in range(EX // 8):
            groups = (2 * v + 1, (2 * v + 2) % 8)
            one, two = [repeated(8 * group + f) for group in groups]
            tiles.append(jnp.where(upper, one, two))
        added = jnp.where(scaled_plane(f) != 0.0, jnp.concatenate(tiles, axis=0), 0.0)
        other[f] = state_in[f]
        for j in range(EY // 128):
            lanes = slice(128 * j, 128 * (j + 1))
            far, near = far_state[f, j], near_state[f, j]
            other[f, EX - 3 : EX - 1, lanes] = jnp.where(odd, near, far)
            other[f, TX + 1 : TX + 3, lanes] = jnp.where(odd, far, near)
        state[f] = other[f] + added
    sweep(state, other, scaled_plane, rhs_plane, jac_plane)
    sweep(other, state, scaled_plane, rhs_plane, jac_plane)
    copies = []
    for f in range(F):
        correction[f] = state[f, 0:TX, 0:TY]
        copies.append(
            pltpu.make_async_copy(correction.at[f], correction_out.at[f], sems.at[0, f])
        )
        copies[-1].start()
    for f in range(F):
        level_residual[f] = residual(f, state, rhs_plane, jac_plane)[0:TX, 0:TY]
        copies.append(
            pltpu.make_async_copy(level_residual.at[f], level_residual_out.at[f], sems.at[1, f])
        )
        copies[-1].start()
    for copy in copies:
        copy.wait()


def shape_of(*dims):
    return jax.ShapeDtypeStruct(dims, F32)


def call(kernel, outs, scratch, *args, space=pltpu.VMEM, out_space=None):
    return pl.pallas_call(
        kernel,
        out_shape=outs,
        in_specs=[pl.BlockSpec(memory_space=space)] * len(args),
        out_specs=[pl.BlockSpec(memory_space=o) for o in out_space or [pltpu.VMEM] * len(outs)],
        scratch_shapes=scratch,
        compiler_params=pltpu.CompilerParams(vmem_limit_bytes=32 * 1024 * 1024),
    )(*args)


def swap(value, axis, start):
    count = lax.axis_size(axis)
    firsts = range(start, count - 1, 2)
    return lax.ppermute(value, axis, [(i, i + 1) for i in firsts] + [(i + 1, i) for i in firsts])


def local(fine, owner, flags, jac, coef):
    strip = shape_of(2, TX, 128)
    rhs, near, far = call(
        restrict_kernel,
        [shape_of(F, TX, TY), strip, strip],
        [
            pltpu.VMEM((F, 4, 2 * TX, 128), F32),
            pltpu.VMEM((4, 2 * TX, 128), jnp.int32),
            pltpu.VMEM((TX, TY), jnp.int32),
            pltpu.VMEM((F, F, TX, TY), F32),
            pltpu.VMEM((F, ROWS, TY // 4), F32),
            pltpu.SemaphoreType.DMA((F + 2, 4)),
        ],
        *[pltpu.with_memory_space_constraint(x, pltpu.HBM) for x in (fine, owner, flags, jac, coef)],
        space=pltpu.HBM,
    )
    near_rows, far_rows = call(
        rows_kernel, [shape_of(ROWS_SENT, TY), shape_of(ROWS_SENT, TY)], [], jac, rhs, flags
    )
    far_y = swap(far, "gy", 1)
    near_y = swap(near, "gy", 0)
    rows, lines, line = shape_of(ROWS_SENT, TY), shape_of(8 * ROWS, 128), shape_of(8, 128)
    near_rows, far_rows, low, high, turn = call(
        corners_kernel,
        [rows, rows, lines, lines, line],
        [pltpu.VMEM((8 * ROWS, 128), F32)],
        near_rows, far_rows, coef, near_y, far_y,
    )
    far_x = swap(far_rows, "gx", 1)
    near_x = swap(near_rows, "gx", 0)
    count = lax.axis_size("gx")
    own = shape_of(F, TX, EY)
    jac_own, rhs_own, scaled_own, first_own, second_own = call(
        own_kernel, [shape_of(F * F, TX, EY), own, own, own, own], [], jac, rhs, flags, near_y, far_y
    )
    tile = pltpu.VMEM((F, EX, EY), F32)
    beyond = shape_of(F, 8, EY)
    ends = shape_of(F, EY // 128, 2, 128)
    state, jac_beyond, rhs_beyond, scaled_beyond, value, chip, near_state, far_state, sent = call(
        before_kernel,
        [
            shape_of(F, EX, EY), shape_of(F * F, 8, EY), beyond, beyond, lines, shape_of(6, 8, 128), ends, ends,
            shape_of(count, F, 2, 128),
        ],
        [
            tile,
            pltpu.VMEM((2, ROWS_SENT, TY), F32),
            pltpu.VMEM((2, 2, 8, 128), F32),
            pltpu.VMEM((8 * ROWS, EY), F32),
            pltpu.VMEM((min(count, 8), F, 2, 128), F32),
            pltpu.SemaphoreType.DMA((count,)),
        ],
        jac_own, rhs_own, scaled_own, first_own, second_own, low, high, turn, far_x, near_x,
        out_space=[pltpu.VMEM] * 8 + [pl.ANY],
    )
    got = lax.all_to_all(sent, "gx", 0, 0, tiled=True)
    far_state = swap(far_state, "gx", 1)
    near_state = swap(near_state, "gx", 0)
    return tuple(
        call(
            after_kernel,
            [shape_of(F, TX, TY), shape_of(F, TX, TY)],
            [
                tile,
                tile,
                pltpu.VMEM((64, 128), F32),
                pltpu.VMEM((64, EY), F32),
                pltpu.VMEM((count, 5, 8, 128), F32),
                pltpu.VMEM((F, TX, TY), F32),
                pltpu.VMEM((F, TX, TY), F32),
                pltpu.SemaphoreType.DMA((2, F)),
            ],
            jac_own, rhs_own, scaled_own, low, high, jac_beyond, rhs_beyond, scaled_beyond, state, value, chip,
            far_state, near_state, got,
            out_space=[pl.ANY] * 2,
        )
    )


def solution(mesh):
    in_specs = (
        P(None, "gx", "gy"),
        P("gx", "gy"),
        P("gx", "gy"),
        P(None, None, "gx", "gy"),
        P(None, "gx", "gy"),
    )
    out_specs = (P(None, "gx", "gy"), P(None, "gx", "gy"))
    return jax.shard_map(local, mesh=mesh, in_specs=in_specs, out_specs=out_specs, check_vma=False)
```

```python
import jax
import jax.numpy as jnp
from jax import lax
from jax.experimental import pallas as pl
from jax.experimental.pallas import tpu as pltpu
from jax.sharding import PartitionSpec as P

F = 5
TX = 24
TY = 256
EX = 32
EY = 384
ROWS = 6
PLANES = 31
F32 = jnp.float32


def iota(shape, dim):
    return lax.broadcasted_iota(jnp.int32, shape, dim)


def parts_of(x):
    head = x.astype(jnp.bfloat16)
    rest = x - head.astype(F32)
    middle = rest.astype(jnp.bfloat16)
    return head, middle, (rest - middle.astype(F32)).astype(jnp.bfloat16)


def select_columns(x, chosen):
    rows = x.shape[0]
    whole = jnp.concatenate(parts_of(x), axis=0)
    out = jnp.dot(whole, chosen.astype(jnp.bfloat16), preferred_element_type=F32)
    return out[0:rows] + out[rows : 2 * rows] + out[2 * rows :]


def roll(x, shift, axis):
    shift = shift % x.shape[axis]
    return x if shift == 0 else pltpu.roll(x, shift, axis)


def parity(axis):
    return lax.rem(lax.axis_index(axis), 2) == 1


def restrict_kernel(
    fine_in, owner_in, flags_in, jac_in, coef_in, rhs, near, far,
    fine, owner, flags, jac, coef, sems,
):
    def tile_copy(source, target, sem, j):
        return pltpu.make_async_copy(source.at[:, 128 * j : 128 * (j + 1)], target.at[j], sem)

    owners = [tile_copy(owner_in, owner, sems.at[0, j], j) for j in range(4)]
    fines = [
        [tile_copy(fine_in.at[f], fine.at[f], sems.at[1 + f, j], j) for j in range(4)]
        for f in range(F)
    ]
    late = [
        pltpu.make_async_copy(flags_in, flags, sems.at[F + 1, 0]),
        pltpu.make_async_copy(coef_in, coef, sems.at[F + 1, 1]),
        pltpu.make_async_copy(jac_in, jac, sems.at[F + 1, 2]),
    ]
    for copy in owners + sum(fines, []) + late:
        copy.start()
    for copy in owners:
        copy.wait()

    def halves(load):
        return [
            jnp.concatenate([load(j, pl.ds(start, TX, 2)) for j in range(4)], axis=1)
            for start in (0, 1)
        ]

    shape = (TX, 2 * TY)
    row = iota(shape, 0)
    col = iota(shape, 1) >> 1
    codes = [
        ((o >> 8) - row + 1) * 3 + (o & (TY - 1)) - col + 1
        for o in halves(lambda j, rows: owner[j, rows, :])
    ]
    masks = [[code == k for code in codes] for k in range(9)]
    gathered = []
    for f in range(F):
        for copy in fines[f]:
            copy.wait()
        values = halves(lambda j, rows: fine[f, j, rows, :])
        total = None
        for dy in (-1, 0, 1):
            part = None
            for dx in (-1, 0, 1):
                mask = masks[(dx + 1) * 3 + dy + 1]
                moved = jnp.where(mask[0], values[0], 0.0) + jnp.where(mask[1], values[1], 0.0)
                moved = roll(moved, dx, 0)
                part = moved if part is None else part + moved
            part = roll(part, 2 * dy, 1)
            total = part if total is None else total + part
        gathered.append(total)
    pairs = ((iota((2 * TY, TY), 0) >> 1) == iota((2 * TY, TY), 1)).astype(F32)
    gathered.append(jnp.zeros((8, 2 * TY), F32))
    for copy in late:
        copy.wait()
    summed = select_columns(jnp.concatenate(gathered, axis=0), pairs)
    planes = [summed[TX * f : TX * (f + 1)] for f in range(F)]
    for f in range(F):
        rhs[f] = planes[f]
    planes.append((flags[...] + 1).astype(F32))

    odd = parity("gy")
    slot = iota((TX, 128), 1) >> 3
    for a in range(2):
        first = jnp.zeros((TX, 128), F32)
        last = jnp.zeros((TX, 128), F32)
        for t in range(16):
            p = 16 * a + t
            if p >= PLANES:
                continue
            if p < F * F:
                head, tail = jac[p // F, p % F, :, 0:128], jac[p // F, p % F, :, TY - 128 : TY]
            else:
                head, tail = planes[p - F * F][:, 0:128], planes[p - F * F][:, TY - 128 : TY]
            first = jnp.where(slot == t, roll(head, 8 * t, 1), first)
            last = jnp.where(slot == t, roll(tail, 8 * t - 120, 1), last)
        near[a] = jnp.where(odd, first, last)
        far[a] = jnp.where(odd, last, first)
    lane = iota((ROWS, 128), 1)
    first, last = near[1, 0:ROWS, :], far[1, 0:ROWS, :]
    for f in range(F):
        wide = jnp.concatenate([coef[f], coef[f]], axis=1)
        head, tail = roll(wide, 120 + f, 1), roll(wide, 120 + f - 63, 1)
        first = jnp.where(lane == 120 + f, jnp.where(odd, head, tail), first)
        last = jnp.where(lane == 120 + f, jnp.where(odd, tail, head), last)
    near[1, 0:ROWS, :] = first
    far[1, 0:ROWS, :] = last


RHS_AT, STATE_AT, CODE_AT, CORNER_AT, LINE_AT, ROWS_SENT = 50, 60, 65, 68, 74, 80


def rows_kernel(jac, rhs, flags, near, far):
    def write(out, first):
        start = 0 if first else TX - 2
        wide = 0 if first else TX - 3
        third = 2 if first else TX - 3
        for p in range(F * F):
            out[2 * p : 2 * p + 2] = jac[p // F, p % F, start : start + 2, :]
        kinds = flags[third : third + 1, :]
        interior, wall = kinds == 0, kinds == 2
        for f in range(F):
            at = RHS_AT + 2 * f
            out[at : at + 2] = rhs[f, start : start + 2, :]
            kept = interior if f in (1, 2) else interior | wall
            scaled = jnp.where(kept, 0.8 / jac[f, f, third : third + 1, :], 0.0)
            out[STATE_AT + f : STATE_AT + f + 1] = scaled * rhs[f, third : third + 1, :]
        out[CODE_AT : CODE_AT + 3] = (flags[wide : wide + 3, :] + 1).astype(F32)
        out[CORNER_AT:ROWS_SENT] = jnp.zeros((ROWS_SENT - CORNER_AT, TY), F32)

    odd = parity("gx")

    @pl.when(odd)
    def _():
        write(near, True)
        write(far, False)

    @pl.when(jnp.logical_not(odd))
    def _():
        write(near, False)
        write(far, True)


def put_corners(out, first_rows, near_y, far_y):
    for side, strip in enumerate((far_y, near_y)):
        at = CORNER_AT + 3 * side
        for a in range(2):
            lanes = slice(128 * a, 128 * (a + 1))
            first, last = strip[a, 0:3, :], strip[a, TX - 3 : TX, :]
            out[at : at + 3, lanes] = jnp.where(first_rows, first, last)


def far_kernel(far_rows, near_y, far_y, far):
    far[...] = far_rows[...]
    put_corners(far, jnp.logical_not(parity("gx")), near_y, far_y)


def near_kernel(near_rows, coef, near_y, far_y, near, low, high, turn, diag):
    near[...] = near_rows[...]
    put_corners(near, parity("gx"), near_y, far_y)

    lane = iota((ROWS, 128), 1)
    odd_y = parity("gy")
    right = jnp.where(odd_y, far_y[1, 0:ROWS, :], near_y[1, 0:ROWS, :])
    left = jnp.where(odd_y, near_y[1, 0:ROWS, :], far_y[1, 0:ROWS, :])
    diag[...] = jnp.full((8 * ROWS, 128), 4.0, F32)
    for f in range(F):
        wide = jnp.concatenate([coef[f], coef[f]], axis=1)
        wide = jnp.where(lane == 64, roll(right, 64 - 120 - f, 1), wide)
        wide = jnp.where(lane == 65, roll(left, 65 - 120 - f, 1), wide)
        wide = jnp.where((lane <= 65) & (wide > 0.0), wide, 4.0)
        for k in range(ROWS):
            diag[8 * k + f : 8 * k + f + 1, :] = wide[k : k + 1, :]
    lows, highs = [], []
    for k in range(ROWS):
        d = diag[8 * k : 8 * k + 8, :]
        inverse = 1.0 / (d - highs[-1] if k else d)
        lows.append(lows[-1] * inverse if k else inverse)
        highs.append(inverse)
        low[8 * k : 8 * k + 8] = lows[k]
        high[8 * k : 8 * k + 8] = highs[k]
    first_low = lows[-1]
    for k in range(ROWS - 2, -1, -1):
        first_low = lows[k] + highs[k] * first_low
    turn[...] = first_low
    lane = iota((8, 128), 1)
    ends = highs[-1]
    for q, part in enumerate((first_low, lows[-1], highs[-1])):
        ends = jnp.where(lane >> 1 == 33 + q, roll(part, 2 * (q + 1), 1), ends)
    near[LINE_AT : LINE_AT + F, 0:128] = jnp.where(lane < 64, first_low, roll(lows[-1], 64, 1))[0:F]
    near[LINE_AT : LINE_AT + F, 128:TY] = ends[0:F]


def unpack(near, far, p):
    odd = parity("gy")
    right = jnp.where(odd, far, near)
    left = jnp.where(odd, near, far)
    lane = iota(near.shape, 1)
    return jnp.where(
        lane < 8,
        roll(right, -8 * (p % 16), 1),
        jnp.where(lane >= 120, roll(left, 120 - 8 * (p % 16), 1), 0.0),
    )


def scale(code, jac, scaled):
    plain = (code == 1.0) | (code == 3.0)
    interior = code == 1.0
    for f in range(F):
        kept = interior if f in (1, 2) else plain
        scaled[f] = jnp.where(kept, 0.8 / jac[F * f + f], 0.0)


def own_kernel(
    jac_in, rhs_in, flags, near_y, far_y, jac, rhs, scaled, first, second
):
    near, far = [near_y[0], near_y[1]], [far_y[0], far_y[1]]
    for p in range(F * F):
        jac[p, :, 0:TY] = jac_in[p // F, p % F]
        jac[p, :, TY:EY] = unpack(near[p // 16], far[p // 16], p)
    for f in range(F):
        rhs[f, :, 0:TY] = rhs_in[f]
        rhs[f, :, TY:EY] = unpack(near[1], far[1], F * F + f)
    aside = unpack(near[1], far[1], F * F + F)
    code = jnp.concatenate([(flags[...] + 1).astype(F32), aside], axis=1)
    scale(code, jac, scaled)

    for f in range(F):
        first[f] = scaled[f] * rhs[f]
    row = iota((TX, EY), 0)
    for f in range(F):
        own = first[f]
        above = jnp.where(row == 0, 0.0, roll(own, 1, 0))
        below = jnp.where(row == TX - 1, 0.0, roll(own, -1, 0))
        total = rhs[f] + above + below + roll(own, 1, 1) + roll(own, -1, 1)
        for g in range(F):
            total = total - jac[F * f + g] * first[g]
        second[f] = own + scaled[f] * total


def residual(f, state, rhs, jac):
    own = state[f]
    beside = roll(own, 1, 0) + roll(own, -1, 0) + roll(own, 1, 1) + roll(own, -1, 1)
    total = rhs(f) + beside
    for g in range(F):
        total = total - jac(F * f + g) * state[g]
    return total


def sweep(old, new, scaled, rhs, jac):
    for f in range(F):
        new[f] = old[f] + scaled(f) * residual(f, old, rhs, jac)


def planes_of(own, beyond):
    return lambda p: jnp.concatenate([own[p], beyond[p]], axis=0)


def columns(shape, fine_dim, coarse_dim):
    fine = iota(shape, fine_dim)
    coarse = iota(shape, coarse_dim)
    here = (coarse <= 64) & (fine >> 2 == coarse)
    return (here | ((coarse == 65) & (fine >= EY - 4))).astype(F32)


def before_kernel(
    jac_own, rhs_own, scaled_own, first_own, second_own, low, high, turn, far_x, near_x,
    state, jac, rhs, scaled, value, chip, near_state, far_state, sent, other, sides, beside, means, block, sems,
):
    odd = parity("gx")
    sides[0] = jnp.where(odd, near_x[...], far_x[...])
    sides[1] = jnp.where(odd, far_x[...], near_x[...])
    none = jnp.zeros((8, TY), F32)

    def put(out, at, rows):
        out[8 - rows : 8, 0:TY] = sides[0, at : at + rows]
        out[0:rows, 0:TY] = sides[1, at : at + rows]

    for side in range(2):
        at = CORNER_AT + 3 * side
        for a in range(2):
            lanes = slice(128 * a, 128 * (a + 1))
            beside[side, a] = jnp.zeros((8, 128), F32)
            beside[side, a, 5:8] = sides[0, at : at + 3, lanes]
            beside[side, a, 0:3] = sides[1, at : at + 3, lanes]
    far, near = [[beside[side, a] for a in range(2)] for side in range(2)]
    for p in range(F * F):
        jac[p, :, 0:TY] = none
        put(jac.at[p], 2 * p, 2)
        if p % (F + 1) == 0:
            jac[p, 5:6, 0:TY] = jnp.ones((1, TY), F32)
            jac[p, 2:3, 0:TY] = jnp.ones((1, TY), F32)
        jac[p, :, TY:EY] = unpack(near[p // 16], far[p // 16], p)
    for f in range(F):
        rhs[f, :, 0:TY] = none
        put(rhs.at[f], RHS_AT + 2 * f, 2)
        rhs[f, :, TY:EY] = unpack(near[1], far[1], F * F + f)
    code = scaled.at[F - 1]
    code[:, 0:TY] = none
    put(code, CODE_AT, 3)
    code[:, TY:EY] = unpack(near[1], far[1], F * F + F)
    scale(code[...], jac, scaled)

    jac_plane, rhs_plane = planes_of(jac_own, jac), planes_of(rhs_own, rhs)
    scaled_plane = planes_of(scaled_own, scaled)
    for f in range(F):
        state[f, TX:EX] = scaled[f] * rhs[f]
        state[f, TX + 5 : TX + 6, 0:TY] = sides[0, STATE_AT + f : STATE_AT + f + 1]
        state[f, TX + 2 : TX + 3, 0:TY] = sides[1, STATE_AT + f : STATE_AT + f + 1]
    row = iota((8, EY), 0)
    for f in range(F):
        beyond = state[f, TX:EX]
        next_up, next_down = roll(beyond, 1, 0), roll(beyond, -1, 0)
        above = jnp.where(row == 0, first_own[f, TX - 1 : TX, :], next_up)
        below = jnp.where(row == 7, first_own[f, 0:1, :], next_down)
        total = rhs[f] + above + below + roll(beyond, 1, 1) + roll(beyond, -1, 1)
        for g in range(F):
            total = total - jac[F * f + g] * state[g, TX:EX]
        other[f, TX:EX] = beyond + scaled[f] * total
        other[f, 0:8] = second_own[f, 0:8, :] + jnp.where(
            row == 0, scaled_own[f, 0:8, :] * next_up, 0.0
        )
        other[f, 8:16] = second_own[f, 8:16, :]
        other[f, 16:TX] = second_own[f, 16:TX, :] + jnp.where(
            row == 7, scaled_own[f, 16:TX, :] * next_down, 0.0
        )
    sweep(other, state, scaled_plane, rhs_plane, jac_plane)
    means[...] = jnp.zeros((8 * ROWS, EY), F32)
    for f in range(F):
        left_over = residual(f, state, rhs_plane, jac_plane)[0:TX]
        left_over = left_over + roll(left_over, -1, 0)
        left_over = left_over + roll(left_over, -2, 0)
        for k in range(ROWS):
            means[8 * k + f : 8 * k + f + 1, :] = left_over[4 * k : 4 * k + 1]
    mean = select_columns(means[...] * 0.0625, columns((EY, 128), 0, 1))
    values = []
    for k in range(ROWS):
        rows = slice(8 * k, 8 * k + 8)
        here = mean[rows] + values[-1] if k else mean[rows]
        values.append(here * high[rows, :])
        value[rows] = values[k]
    first, last = values[-1], values[-1]
    for k in range(ROWS - 2, -1, -1):
        first = values[k] + high[8 * k : 8 * k + 8, :] * first
    lane = iota((8, 128), 1)

    packed = [near_x[ROWS_SENT - 8 :, 128 * a : 128 * (a + 1)] for a in range(2)]
    packed = [roll(part, ROWS_SENT - 8 - LINE_AT, 0) for part in packed]
    theirs = [packed[0], roll(packed[0], 64, 1), packed[1]]
    theirs = [jnp.where(lane < 64, theirs[q], roll(packed[1], -2 * (q + 1), 1)) for q in range(3)]
    own = [turn[...], low[8 * ROWS - 8 :, :], high[8 * ROWS - 8 :, :]]
    b0, c, c1 = [jnp.where(odd, theirs[q], own[q]) for q in range(3)]
    e0, g, g1 = [jnp.where(odd, own[q], theirs[q]) for q in range(3)]
    w = 1.0 / (1.0 - c1 * e0)
    cw, gw = c * w, g * w
    x0 = jnp.where(odd, cw * first, first + cw * e0 * last)
    x1 = jnp.where(odd, last + gw * c1 * first, gw * last)
    chip[0] = w
    chip[1] = jnp.where(odd, gw, cw)
    chip[2] = jnp.where(odd, first, last)
    chip[3] = jnp.where(odd, c1, e0)
    chip[4] = c
    chip[5] = g
    whole_b0, whole_c, whole_c1 = b0 + c * cw * e0, cw * g, g1 + g * gw * c1
    middle = roll(whole_c, 64, 1)
    pair = lane >> 1
    even_part = jnp.where(lane < 64, whole_b0, middle)
    for q, part in enumerate((x0, x1, whole_b0, whole_c, whole_c1)):
        even_part = jnp.where(pair == 48 + q, roll(part, 32 + 2 * q, 1), even_part)
    odd_part = jnp.where(lane < 64, whole_c1, middle)
    odd_part = jnp.where(pair == 32, x0, jnp.where(pair == 33, roll(x1, 2, 1), odd_part))
    main = jnp.where(lane < 64, x0, roll(x1, 64, 1))
    rest = jnp.where(odd, odd_part, even_part)
    each = block.shape[0]
    for f in range(F):
        both = jnp.concatenate([main[f : f + 1], rest[f : f + 1]], axis=0)
        for k in range(each):
            block[k, f] = both
    copies = [
        pltpu.make_async_copy(block, sent.at[k * each : (k + 1) * each], sems.at[k])
        for k in range(sent.shape[0] // each)
    ]
    for copy in copies:
        copy.start()
    for f in range(F):
        for j in range(EY // 128):
            lanes = slice(128 * j, 128 * (j + 1))
            first, last = state[f, 1:3, lanes], state[f, TX - 3 : TX - 1, lanes]
            near_state[f, j] = jnp.where(odd, first, last)
            far_state[f, j] = jnp.where(odd, last, first)
    for copy in copies:
        copy.wait()


def merge(one, two):
    a0, a1, b0, c, c1 = one
    d0, d1, e0, g, g1 = two
    w = 1.0 / (1.0 - c1 * e0)
    cw, gw = c * w, g * w
    return (
        a0 + cw * (d0 + e0 * a1),
        d1 + gw * (a1 + c1 * d0),
        b0 + c * cw * e0,
        cw * g,
        g1 + g * gw * c1,
    )


def between(one, two, below, above):
    a0, a1, b0, c, c1 = one
    d0, d1, e0, g, g1 = two
    outer = d0 + g * above
    last = (a1 + c * below + c1 * outer) / (1.0 - c1 * e0)
    return last, outer + e0 * last


def after_kernel(
    jac_own, rhs_own, scaled_own, low, high, jac_beyond, rhs_beyond, scaled_beyond, state_in, value, chip, far_state, near_state, got,
    correction_out, level_residual_out,
    state, other, ends, spread, tree, correction, level_residual, sems,
):
    count = got.shape[0]
    me = lax.axis_index("gx")
    lane = iota((F, 128), 1)

    odd = parity("gx")

    def stacked(k, part):
        return jnp.concatenate([got[k, f, part : part + 1, :] for f in range(F)], axis=0)

    def segment(k):
        main = stacked(2 * k, 0) + stacked(2 * k + 1, 0)
        even, other_core = stacked(2 * k, 1), stacked(2 * k + 1, 1)
        ends = roll(even, 64 - 96, 1)
        moving = ends + other_core
        middle = roll(jnp.where(lane < 96, even, other_core), 64, 1)
        inner = [main, roll(main, 64, 1), even, middle, other_core]
        outer = [moving, roll(moving, -2, 1)] + [roll(ends, -2 * q, 1) for q in (2, 3, 4)]
        return [jnp.where(lane < 64, inner[q], outer[q]) for q in range(5)]

    level, starts, total = [segment(k) for k in range(count // 2)], [], 0
    while True:
        starts.append(total)
        for parts in level:
            for q in range(5):
                tree[total, q, 0:F] = parts[q]
            total += 1
        if len(level) <= 2:
            break
        level = [merge(level[2 * k], level[2 * k + 1]) for k in range(len(level) // 2)]
    below = above = jnp.zeros((F, 128), F32)
    my_chip = me >> 1
    if count > 2:
        for size in range(len(starts) - 1, -1, -1):
            at = starts[size] + 2 * (my_chip >> (size + 1))
            one = [tree[at, q, 0:F] for q in range(5)]
            two = [tree[at + 1, q, 0:F] for q in range(5)]
            last, first = between(one, two, below, above)
            second = (my_chip >> size) & 1 == 1
            below, above = jnp.where(second, last, below), jnp.where(second, above, first)
    partner = me + 1 - 2 * (me & 1)
    main, rest = stacked(partner, 0), stacked(partner, 1)
    from_even = jnp.where(lane < 64, roll(main, 64, 1), roll(rest, 64 - 98, 1))
    from_odd = jnp.where(lane < 64, main, rest)
    w, share, own, turn, c, g = [chip[q, 0:F, :] for q in range(6)]
    theirs = jnp.where(odd, from_even, from_odd) / share
    lower, upper = c * below, g * above
    inside = jnp.where(odd, lower, upper) + theirs
    inside = w * (inside + turn * (own + jnp.where(odd, upper, lower)))
    below, above = jnp.where(odd, inside, below), jnp.where(odd, above, inside)

    used = lane <= 65
    ends[...] = jnp.zeros((64, 128), F32)
    ends[0:F] = jnp.where(used, below, 0.0)
    ends[8 * (ROWS + 1) : 8 * (ROWS + 1) + F] = jnp.where(used, above, 0.0)
    here = above
    for k in range(ROWS - 1, -1, -1):
        rows = slice(8 * k, 8 * k + F)
        here = value[rows] + low[rows] * below + high[rows] * here
        ends[8 * (k + 1) : 8 * (k + 1) + F] = jnp.where(used, here, 0.0)
    spread[...] = select_columns(ends[...], columns((128, EY), 1, 0))

    jac_plane, rhs_plane = planes_of(jac_own, jac_beyond), planes_of(rhs_own, rhs_beyond)
    scaled_plane = planes_of(scaled_own, scaled_beyond)
    upper = iota((8, EY), 0) < 4

    def repeated(row):
        return jnp.broadcast_to(spread[row : row + 1, :], (8, EY))

    for f in range(F):
        tiles = []
        for v in range(EX // 8):
            groups = (2 * v + 1, (2 * v + 2) % 8)
            one, two = [repeated(8 * group + f) for group in groups]
            tiles.append(jnp.where(upper, one, two))
        added = jnp.where(scaled_plane(f) != 0.0, jnp.concatenate(tiles, axis=0), 0.0)
        other[f] = state_in[f]
        for j in range(EY // 128):
            lanes = slice(128 * j, 128 * (j + 1))
            far, near = far_state[f, j], near_state[f, j]
            other[f, EX - 3 : EX - 1, lanes] = jnp.where(odd, near, far)
            other[f, TX + 1 : TX + 3, lanes] = jnp.where(odd, far, near)
        state[f] = other[f] + added
    sweep(state, other, scaled_plane, rhs_plane, jac_plane)
    sweep(other, state, scaled_plane, rhs_plane, jac_plane)
    copies = []
    for f in range(F):
        correction[f] = state[f, 0:TX, 0:TY]
        copies.append(
            pltpu.make_async_copy(correction.at[f], correction_out.at[f], sems.at[0, f])
        )
        copies[-1].start()
    for f in range(F):
        level_residual[f] = residual(f, state, rhs_plane, jac_plane)[0:TX, 0:TY]
        copies.append(
            pltpu.make_async_copy(level_residual.at[f], level_residual_out.at[f], sems.at[1, f])
        )
        copies[-1].start()
    for copy in copies:
        copy.wait()


def shape_of(*dims):
    return jax.ShapeDtypeStruct(dims, F32)


def call(kernel, outs, scratch, *args, space=pltpu.VMEM, out_space=None):
    return pl.pallas_call(
        kernel,
        out_shape=outs,
        in_specs=[pl.BlockSpec(memory_space=space)] * len(args),
        out_specs=[pl.BlockSpec(memory_space=o) for o in out_space or [pltpu.VMEM] * len(outs)],
        scratch_shapes=scratch,
        compiler_params=pltpu.CompilerParams(vmem_limit_bytes=32 * 1024 * 1024),
    )(*args)


def swap(value, axis, start):
    count = lax.axis_size(axis)
    firsts = range(start, count - 1, 2)
    return lax.ppermute(value, axis, [(i, i + 1) for i in firsts] + [(i + 1, i) for i in firsts])


def local(fine, owner, flags, jac, coef):
    strip = shape_of(2, TX, 128)
    rhs, near, far = call(
        restrict_kernel,
        [shape_of(F, TX, TY), strip, strip],
        [
            pltpu.VMEM((F, 4, 2 * TX, 128), F32),
            pltpu.VMEM((4, 2 * TX, 128), jnp.int32),
            pltpu.VMEM((TX, TY), jnp.int32),
            pltpu.VMEM((F, F, TX, TY), F32),
            pltpu.VMEM((F, ROWS, TY // 4), F32),
            pltpu.SemaphoreType.DMA((F + 2, 4)),
        ],
        *[pltpu.with_memory_space_constraint(x, pltpu.HBM) for x in (fine, owner, flags, jac, coef)],
        space=pltpu.HBM,
    )
    near_rows, far_rows = call(
        rows_kernel, [shape_of(ROWS_SENT, TY), shape_of(ROWS_SENT, TY)], [], jac, rhs, flags
    )
    far_y = swap(far, "gy", 1)
    near_y = swap(near, "gy", 0)
    rows, lines, line = shape_of(ROWS_SENT, TY), shape_of(8 * ROWS, 128), shape_of(8, 128)
    (far_rows,) = call(far_kernel, [rows], [], far_rows, near_y, far_y)
    far_x = swap(far_rows, "gx", 1)
    near_rows, low, high, turn = call(
        near_kernel,
        [rows, lines, lines, line],
        [pltpu.VMEM((8 * ROWS, 128), F32)],
        near_rows, coef, near_y, far_y,
    )
    near_x = swap(near_rows, "gx", 0)
    count = lax.axis_size("gx")
    own = shape_of(F, TX, EY)
    jac_own, rhs_own, scaled_own, first_own, second_own = call(
        own_kernel, [shape_of(F * F, TX, EY), own, own, own, own], [], jac, rhs, flags, near_y, far_y
    )
    tile = pltpu.VMEM((F, EX, EY), F32)
    beyond = shape_of(F, 8, EY)
    ends = shape_of(F, EY // 128, 2, 128)
    state, jac_beyond, rhs_beyond, scaled_beyond, value, chip, near_state, far_state, sent = call(
        before_kernel,
        [
            shape_of(F, EX, EY), shape_of(F * F, 8, EY), beyond, beyond, lines, shape_of(6, 8, 128), ends, ends,
            shape_of(count, F, 2, 128),
        ],
        [
            tile,
            pltpu.VMEM((2, ROWS_SENT, TY), F32),
            pltpu.VMEM((2, 2, 8, 128), F32),
            pltpu.VMEM((8 * ROWS, EY), F32),
            pltpu.VMEM((min(count, 8), F, 2, 128), F32),
            pltpu.SemaphoreType.DMA((count,)),
        ],
        jac_own, rhs_own, scaled_own, first_own, second_own, low, high, turn, far_x, near_x,
        out_space=[pltpu.VMEM] * 8 + [pl.ANY],
    )
    got = lax.all_to_all(sent, "gx", 0, 0, tiled=True)
    far_state = swap(far_state, "gx", 1)
    near_state = swap(near_state, "gx", 0)
    return tuple(
        call(
            after_kernel,
            [shape_of(F, TX, TY), shape_of(F, TX, TY)],
            [
                tile,
                tile,
                pltpu.VMEM((64, 128), F32),
                pltpu.VMEM((64, EY), F32),
                pltpu.VMEM((count, 5, 8, 128), F32),
                pltpu.VMEM((F, TX, TY), F32),
                pltpu.VMEM((F, TX, TY), F32),
                pltpu.SemaphoreType.DMA((2, F)),
            ],
            jac_own, rhs_own, scaled_own, low, high, jac_beyond, rhs_beyond, scaled_beyond, state, value, chip,
            far_state, near_state, got,
            out_space=[pl.ANY] * 2,
        )
    )


def solution(mesh):
    in_specs = (
        P(None, "gx", "gy"),
        P("gx", "gy"),
        P("gx", "gy"),
        P(None, None, "gx", "gy"),
        P(None, "gx", "gy"),
    )
    out_specs = (P(None, "gx", "gy"), P(None, "gx", "gy"))
    return jax.shard_map(local, mesh=mesh, in_specs=in_specs, out_specs=out_specs, check_vma=False)
```
